32 devices in a mesh: dp: 8 (over y, x, core), mp: 4 (over z).
Axes of the slice: x: 2, y: 2, z: 4, core: 2. Of those that a mesh axis runs over, the one named last changes fastest.
Arguments:
- tokens: bfloat16 [4096, 768], P('dp'), may hold values from -6 to 6
- encoder: bfloat16 [16, 1500, 768], P('dp', 'mp'), may hold values from -6 to 6
- lengths: int32 [8, 2], P('dp'), may hold values from 1 to 448, 512 in all within a row
- norm_gains: float32 [3, 768], replicated, may hold values from 0.5 to 1.5
- norm_biases: float32 [3, 768], replicated, may hold values from -1 to 1
- self_in: bfloat16 [3, 768, 768], P(None, None, 'mp'), may hold values from -0.21875 to 0.21875
- cross_in: bfloat16 [3, 768, 768], P(None, None, 'mp'), may hold values from -0.21875 to 0.21875
- in_biases: float32 [4, 768], P(None, 'mp'), may hold values from -1 to 1
- self_out: bfloat16 [768, 768], P('mp'), may hold values from -0.875 to 0.875
- cross_out: bfloat16 [768, 768], P('mp'), may hold values from -6 to 6
- out_biases: float32 [3, 768], replicated, may hold values from -1 to 1
- fc_up: bfloat16 [768, 3072], P(None, 'mp'), may hold values from -0.21875 to 0.21875
- up_bias: float32 [3072], P('mp'), may hold values from -1 to 1
- fc_down: bfloat16 [3072, 768], P('mp'), may hold values from -0.4375 to 0.4375
- cotangent: bfloat16 [4096, 768], P('dp'), may hold values from -6 to 6
Outputs:
- layer_out: bfloat16 [4096, 768], P('dp')
- token_grad: bfloat16 [4096, 768], P('dp')
- encoder_grad: bfloat16 [16, 1500, 768], P('dp', 'mp')
- norm_gains_grad: float32 [3, 768], replicated
- norm_biases_grad: float32 [3, 768], replicated
- self_in_grad: float32 [3, 768, 768], P(None, 'dp', 'mp')
- cross_in_grad: float32 [3, 768, 768], P(None, 'dp', 'mp')
- in_biases_grad: float32 [4, 768], P(None, 'mp')
- self_out_grad: float32 [768, 768], P('mp', 'dp')
- cross_out_grad: float32 [768, 768], P('mp', 'dp')
- out_biases_grad: float32 [3, 768], replicated
- fc_up_grad: float32 [768, 3072], P('dp', 'mp')
- up_bias_grad: float32 [3072], P('mp')
- fc_down_grad: float32 [3072, 768], P('mp', 'dp')
The draws below stay inside these ranges and needn't reach their ends.
Inputs may be any that keep to these rules, and one draw needn't show every extreme that they name: `lengths`: each row sums to 512.
All inputs are finite; a program needn't handle non-finite values.
Results may differ from the reference program's by a relative error of at most 0.024.
Values may be sent and summed in bfloat16 or wider, within the bound.
A program may use at most 128 MiB of HBM per device.

```python
import math
import jax
import jax.numpy as jnp
import numpy as np
from jax import lax

D = 768
HEADS = 12
HEAD_DIM = 64
FF = 3072
ENC = 1500
TOK_DEV = 512
CLIPS_DEV = 2
MOST = 448
TOKENS = 4096
CLIPS = 16
N_DP = 8


def level_of(own_key, dims, cuts, smallest, high):
    level, own = 1.0, jax.random.fold_in(own_key, 6)
    for dim, shards_of in cuts:
        draws = jnp.exp(jax.random.uniform(jax.random.fold_in(own, dim), (shards_of,), jnp.float32, smallest / len(cuts), high / len(cuts)))
        level = level * jnp.repeat(draws, dims[dim] // shards_of).reshape([-1 if axis == dim else 1 for axis in range(len(dims))])
    return level


def profile(count, total, most, slope):
    weights = [(1 << 20) // math.isqrt(rank ** slope) + 1 for rank in range(2, count + 1)]
    surplus, counts = total - most - (count - 1), [1] * (count - 1)
    while surplus > 0:
        candidates = [i for i in range(count - 1) if counts[i] < most]
        whole, budget = sum([weights[i] for i in candidates]), surplus
        for i in candidates:
            extra = min(most - counts[i], max(1, budget * weights[i] // whole), surplus)
            counts[i] = counts[i] + extra
            surplus = surplus - extra
    return np.array([most] + counts)


def ragged_sizes(rng, number_of, total, reach, lean):
    if number_of == 2:
        one = jax.random.randint(rng, (), max(1, total - reach), min(reach, total - 1) + 1)
        return jnp.stack([one, total - one])
    sizes = jnp.asarray(profile(number_of, total, reach, lean), jnp.int32)
    pairs = (number_of - 1) // 2
    donor, taker = sizes[1:1 + 2 * pairs:2], sizes[2:2 + 2 * pairs:2]
    room = jnp.minimum(donor - 1, reach - taker)
    moved = jax.random.randint(jax.random.fold_in(rng, 1), (pairs,), 0, 1 << 20) % (room + 1)
    sizes = sizes.at[1:1 + 2 * pairs:2].set(donor - moved).at[2:2 + 2 * pairs:2].set(taker + moved)
    return sizes[jax.random.permutation(jax.random.fold_in(rng, 2), number_of)]


def noise(stream_key, dims, width, most, pieces=(), held_as=jnp.bfloat16):
    array = width * jax.random.normal(stream_key, dims, jnp.float32)
    if pieces:
        array = array * level_of(stream_key, dims, pieces, -0.22, 0.18)
    return jnp.clip(array, -most, most).astype(held_as)


def setup_inputs(seed: int = 0) -> dict:
    key_of = jax.random.split(jax.random.key(seed), 16)
    tokens = noise(key_of[0], (TOKENS, D), 1.0, 6.0, ((0, 8),))
    encoder = noise(key_of[1], (CLIPS, ENC, D), 1.0, 6.0, ((0, 8), (1, 4)))
    lengths = jax.vmap(lambda own: ragged_sizes(own, CLIPS_DEV, TOK_DEV, MOST, 2))(jax.random.split(key_of[2], N_DP)).reshape((N_DP, CLIPS_DEV)).astype(jnp.int32)
    norm_gains = jnp.clip(1.0 + 0.1 * jax.random.normal(key_of[3], (3, D), jnp.float32), 0.5, 1.5)
    norm_biases = noise(key_of[4], (3, D), 0.2, 1.0, (), jnp.float32)
    self_in = noise(key_of[5], (3, D, D), D ** -0.5, 0.21875, ((2, 4),))
    cross_in = noise(key_of[6], (3, D, D), D ** -0.5, 0.21875, ((2, 4),))
    in_biases = noise(key_of[7], (4, D), 0.2, 1.0, ((1, 4),), jnp.float32)
    self_out = noise(key_of[8], (D, D), (max(1, D // 16)) ** -0.5, 0.875, ((0, 4),))
    cross_out = noise(key_of[9], (D, D), (max(1, D // 512)) ** -0.5, 6.0, ((0, 4),))
    out_biases = noise(key_of[10], (3, D), 0.2, 1.0, (), jnp.float32)
    fc_up = noise(key_of[11], (D, FF), D ** -0.5, 0.21875, ((1, 4),))
    up_bias = noise(key_of[12], (FF,), 0.2, 1.0, ((0, 4),), jnp.float32)
    fc_down = noise(key_of[13], (FF, D), (max(1, FF // 16)) ** -0.5, 0.4375, ((0, 4),))
    cotangent = noise(key_of[14], (TOKENS, D), 1.0, 6.0, ((0, 8),))
    return dict(tokens=tokens, encoder=encoder, lengths=lengths, norm_gains=norm_gains, norm_biases=norm_biases, self_in=self_in, cross_in=cross_in, in_biases=in_biases, self_out=self_out, cross_out=cross_out, out_biases=out_biases, fc_up=fc_up, up_bias=up_bias, fc_down=fc_down, cotangent=cotangent)


highest = lax.Precision.HIGHEST
epsilon = 1e-05
factor = 0.125
masked_value = -1e+30

@jax.custom_vjp
def low(v):
    return lax.optimization_barrier(v.astype(jnp.bfloat16)).astype(jnp.float32)

@jax.custom_vjp
def low_back(v):
    return v

def low_keep(v):
    return (low(v), None)

def low_pass(kept, grad):
    return (grad,)

def back_keep(v):
    return (v, None)

def back_low(kept, grad):
    return (low(grad),)
low.defvjp(low_keep, low_pass)
low_back.defvjp(back_keep, back_low)

def layer_norm(values, norm_gain, offset):
    average = lax.optimization_barrier(jnp.mean(values, axis=-1, keepdims=True))
    centred = values - average
    variance = lax.optimization_barrier(jnp.mean(centred * centred, axis=-1, keepdims=True))
    return centred * lax.rsqrt(variance + epsilon) * norm_gain + offset

def matmul(left_side, right_side):
    return jnp.dot(left_side, right_side, precision=highest)

def split_heads(matrix):
    return matrix.reshape(matrix.shape[0], HEADS, HEAD_DIM).transpose(1, 0, 2)

def merge_heads(stacked):
    return stacked.transpose(1, 0, 2).reshape(stacked.shape[1], -1)

def attend(queries, key_rows, value_rows, allowed):

    def one_head(inputs):
        head_query, head_key, head_value = inputs
        scores = low_back(factor * jnp.dot(head_query, head_key.T, precision=highest))
        scores = jnp.where(allowed, scores, masked_value)
        row_max = lax.optimization_barrier(jnp.max(scores, axis=-1, keepdims=True))
        exponent = jnp.exp(scores - row_max)
        probabilities = exponent / lax.optimization_barrier(jnp.sum(exponent, axis=-1, keepdims=True))
        return jnp.dot(low(probabilities), head_value, precision=highest)
    stacked = lax.map(jax.checkpoint(one_head), (split_heads(queries), split_heads(key_rows), split_heads(value_rows)))
    return merge_heads(stacked)

def build_masks(group_lengths):
    positions = jnp.arange(TOK_DEV, dtype=jnp.int32)
    clip_ends = jnp.cumsum(group_lengths.astype(jnp.int32))
    token_clip = lax.optimization_barrier(jnp.sum((positions[:, None] >= clip_ends[None, :]).astype(jnp.int32), axis=1))
    self_allowed = (token_clip[:, None] == token_clip[None, :]) & (positions[None, :] <= positions[:, None])
    frame_clip = jnp.arange(CLIPS_DEV * ENC, dtype=jnp.int32) // ENC
    cross_allowed = token_clip[:, None] == frame_clip[None, :]
    return (self_allowed, cross_allowed)

def layer_forward(inputs, frames, params, self_allowed, cross_allowed):
    norm_gains, norm_biases, self_in, cross_in, in_biases, self_out, cross_out, out_biases, fc_up, up_bias, fc_down = params
    normed = low(layer_norm(inputs, norm_gains[0], norm_biases[0]))
    queries = low(low_back(matmul(normed, self_in[0])) + in_biases[0])
    key_rows = low(low_back(matmul(normed, self_in[1])))
    value_rows = low(low_back(matmul(normed, self_in[2])) + in_biases[1])
    attended = low_back(low(attend(queries, key_rows, value_rows, self_allowed)))
    middle = inputs + low_back(matmul(attended, self_out)) + out_biases[0]
    normed = low(layer_norm(middle, norm_gains[1], norm_biases[1]))
    queries = low(low_back(matmul(normed, cross_in[0])) + in_biases[2])
    key_rows = low(low_back(matmul(frames, cross_in[1])))
    value_rows = low(low_back(matmul(frames, cross_in[2])) + in_biases[3])
    attended = low_back(low(attend(queries, key_rows, value_rows, cross_allowed)))
    after_cross = middle + low_back(matmul(attended, cross_out)) + out_biases[1]
    normed = low(layer_norm(after_cross, norm_gains[2], norm_biases[2]))
    upward = low_back(matmul(normed, fc_up)) + up_bias
    active = low(jax.nn.gelu(upward, approximate=False))
    return after_cross + low_back(matmul(active, fc_down)) + out_biases[2]

def reference(tokens, encoder, lengths, norm_gains, norm_biases, self_in, cross_in, in_biases, self_out, cross_out, out_biases, fc_up, up_bias, fc_down, cotangent):
    weights = tuple((member.astype(jnp.float32) for member in (norm_gains, norm_biases, self_in, cross_in, in_biases, self_out, cross_out, out_biases, fc_up, up_bias, fc_down)))
    token_groups = tokens.astype(jnp.float32).reshape(N_DP, TOK_DEV, -1)
    frame_groups = encoder.astype(jnp.float32).reshape(N_DP, CLIPS_DEV * ENC, -1)
    tangent_groups = cotangent.astype(jnp.float32).reshape(N_DP, TOK_DEV, -1)

    def one_group(totals, inputs):
        group_tokens, group_frames, group_lengths, group_tangent = inputs
        self_allowed, cross_allowed = build_masks(group_lengths)

        def forward(token_rows, frame_rows, *params):
            return layer_forward(token_rows, frame_rows, params, self_allowed, cross_allowed)
        output, pullback = jax.vjp(forward, group_tokens, group_frames, *weights)
        gradients = pullback(group_tangent)
        totals = tuple((running + gradient for running, gradient in zip(totals, gradients[2:])))
        return (totals, (output.astype(jnp.bfloat16), gradients[0].astype(jnp.bfloat16), gradients[1].astype(jnp.bfloat16)))
    start_totals = tuple((jnp.zeros(member.shape, jnp.float32) for member in weights))
    totals, outcome = lax.scan(one_group, start_totals, (token_groups, frame_groups, lengths.astype(jnp.int32), tangent_groups))
    layer_out = outcome[0].reshape(N_DP * TOK_DEV, -1)
    token_grad = outcome[1].reshape(N_DP * TOK_DEV, -1)
    encoder_grad = outcome[2].reshape(N_DP * CLIPS_DEV, ENC, -1)
    return (layer_out, token_grad, encoder_grad, totals[0], totals[1], totals[2], totals[3], totals[4], totals[5], totals[6], totals[7], totals[8], totals[9], totals[10])
```

```python
import functools

import jax
import jax.numpy as jnp
from jax import lax
from jax.experimental import pallas as pl
from jax.experimental.pallas import tpu as pltpu
from jax.sharding import PartitionSpec as P

HEAD_DIM = 64
epsilon = 1e-05
factor = 0.125
masked_value = -1e30
f32 = jnp.float32
bf16 = jnp.bfloat16
MESH = pl.DeviceIdType.MESH
VMEM = pl.BlockSpec(memory_space=pltpu.VMEM)
ANY = pl.BlockSpec(memory_space=pl.ANY)
PLANE = 8


def flip(index, bit):
    return index + bit - 2 * bit * lax.rem(index // bit, 2)


def remote(src, dst, send, recv, device):
    return pltpu.make_async_remote_copy(
        src_ref=src, dst_ref=dst, send_sem=send, recv_sem=recv, device_id=device, device_id_type=MESH
    )


def greet(devices):
    barrier = pltpu.get_barrier_semaphore()
    for device in devices:
        pl.semaphore_signal(barrier, inc=1, device_id=device, device_id_type=MESH)


def pair_sum(left, right):
    return (left.astype(f32) + right.astype(f32)).astype(bf16)


def gather_kernel(pack, attended, weights, parts, own, zsend, wsend, wrecv, osend, orecv, local):
    d, m = lax.axis_index("dp"), lax.axis_index("mp")
    mine = lax.rem(d, PLANE)
    base = d - mine
    up, down = m < 3, m > 0
    barrier = pltpu.get_barrier_semaphore()
    greet([(base + flip(mine, 1), m), (base + flip(mine, 2), m), (base + flip(mine, 4), m)])
    greet([(base + flip(flip(mine, 2), 4), m)])

    @pl.when(up)
    def _():
        greet([(d, m + 1)])

    @pl.when(down)
    def _():
        greet([(d, m - 1)])

    both = jnp.logical_and(up, down)

    @pl.when(both)
    def _():
        pl.semaphore_wait(barrier, 6)

    @pl.when(jnp.logical_not(both))
    def _():
        pl.semaphore_wait(barrier, 5)

    def weight_hop(k, step):
        o = m - step * k
        src = pack.at[mine] if k == 0 else weights.at[o, mine]
        return remote(src, weights.at[o, mine], zsend.at[k, (step + 1) // 2], wrecv.at[o, mine], (d, m + step))

    def part_hop(k, step):
        o = m - step * k
        src = attended if k == 0 else parts.at[o]
        return remote(src, parts.at[o], osend.at[k, (step + 1) // 2], orecv.at[o], (d, m + step))

    def weight_came(o, s):
        remote(weights.at[o, s], weights.at[o, s], wsend.at[0, 0], wrecv.at[o, s], (d, m)).wait_recv()

    def spread(o, k):
        to = base + (flip(mine, k) if k != 6 else flip(flip(mine, 2), 4))
        return remote(weights.at[o, mine], weights.at[o, mine], wsend.at[o, k], wrecv.at[o, mine], (to, m))

    def pass_on(o, k):
        s = flip(mine, k) if k != 6 else flip(flip(mine, 2), 4)
        to = base + flip(mine, 1)
        return remote(weights.at[o, s], weights.at[o, s], wsend.at[o, k + 1], wrecv.at[o, s], (to, m))

    whole = pltpu.make_async_copy(pack, weights.at[m], local.at[0])
    whole.start()
    own_part = pltpu.make_async_copy(attended, parts.at[m], local.at[1])
    own_part.start()
    steps = ((1, up), (-1, down))
    for hop in (weight_hop, part_hop):
        for step, can in steps:

            @pl.when(can)
            def _(hop=hop, step=step):
                hop(0, step).start()

    def origin(k, step):
        o = m - step * k
        return o, (o >= 0) if step > 0 else (o <= 3)

    for k in (1, 2, 3):
        for step, can in steps:
            o, have = origin(k, step)

            @pl.when(have)
            def _(o=o, k=k, step=step, can=can):
                weight_came(o, mine)
                if k < 3:

                    @pl.when(can)
                    def _():
                        weight_hop(k, step).start()

                for way in (6, 2, 4, 1):
                    spread(o, way).start()

    for k in (1, 2, 3):
        for step, can in steps:
            o, have = origin(k, step)

            @pl.when(have)
            def _(o=o, k=k, step=step, can=can):
                remote(parts.at[o], parts.at[o], osend.at[0, 0], orecv.at[o], (d, m)).wait_recv()
                if k < 3:

                    @pl.when(can)
                    def _():
                        part_hop(k, step).start()

    for k in (1, 2, 3):
        for step, can in steps:
            o, have = origin(k, step)

            @pl.when(have)
            def _(o=o):
                for way in (2, 4, 6):
                    s = flip(mine, way) if way != 6 else flip(flip(mine, 2), 4)
                    weight_came(o, s)
                    pass_on(o, way).start()

    for j in (1, 2, 3):
        o = lax.rem(m + j, 4)
        for way in (0, 2, 4, 6):
            s = flip(mine, way) if way in (2, 4) else (mine if way == 0 else flip(flip(mine, 2), 4))
            weight_came(o, flip(s, 1))
    for k in (0, 1, 2):
        for step, can in steps:
            o, have = origin(k, step)

            @pl.when(jnp.logical_and(have, can))
            def _(k=k, step=step):
                weight_hop(k, step).wait_send()
                part_hop(k, step).wait_send()

    for j in (1, 2, 3):
        o = lax.rem(m + j, 4)
        for way in (1, 2, 4, 6):
            spread(o, way).wait_send()
        for way in (2, 4, 6):
            pass_on(o, way).wait_send()
    whole.wait()
    own_part.wait()
    own[...] = jnp.zeros_like(own)


def gather(pack, attended):
    rows, cols = pack.shape[1:]
    dma = pltpu.SemaphoreType.DMA
    weights, parts, _ = pl.pallas_call(
        gather_kernel,
        out_shape=(
            jax.ShapeDtypeStruct((4,) + pack.shape, bf16),
            jax.ShapeDtypeStruct((4,) + attended.shape, bf16),
            jax.ShapeDtypeStruct((8, 128), f32),
        ),
        in_specs=[ANY, ANY],
        out_specs=[ANY, ANY, VMEM],
        scratch_shapes=[
            dma((3, 2)), dma((4, 8)), dma((4, 8)), dma((3, 2)), dma((4,)), dma((2,)),
        ],
        compiler_params=pltpu.CompilerParams(collective_id=1, has_side_effects=True),
        name="gather",
    )(pack, attended)
    return weights, parts


def total_kernel(count, lag, x_ref, o_ref, from_edge, half, other, whole, sa, ra, sb, rb, sr, rr):
    d, m = lax.axis_index("dp"), lax.axis_index("mp")
    edge = jnp.logical_or(m == 0, m == 3)
    inner = jnp.logical_not(edge)
    near, peer = flip(m, 1), 3 - m
    barrier = pltpu.get_barrier_semaphore()
    greet([(d, near)])

    @pl.when(inner)
    def _():
        greet([(d, peer)])
        pl.semaphore_wait(barrier, 2)

    @pl.when(edge)
    def _():
        pl.semaphore_wait(barrier, 1)

    rows = x_ref.shape[0] // count

    def block(c):
        return pl.ds(c * rows, rows)

    def inward(c):
        return remote(x_ref.at[block(c)], from_edge.at[c], sa.at[c], ra.at[c], (d, near))

    def across(c):
        return remote(half.at[c], other.at[c], sb.at[c], rb.at[c], (d, peer))

    def outward(c):
        return remote(whole.at[c], whole.at[c], sr.at[c], rr.at[c], (d, near))

    @pl.when(edge)
    def _():
        for c in range(count):
            inward(c).start()
        for c in range(count):
            outward(c).wait_recv()
            o_ref[block(c)] = whole[c]
        for c in range(count):
            inward(c).wait_send()

    @pl.when(inner)
    def _():
        for i in range(count + lag):
            if i < count:
                inward(i).wait_recv()
                half[i] = pair_sum(x_ref[block(i)], from_edge[i])
                across(i).start()
            c = i - lag
            if c >= 0:
                across(c).wait_recv()
                value = pair_sum(half[c], other[c])
                whole[c] = value
                outward(c).start()
                o_ref[block(c)] = value
        for c in range(count):
            across(c).wait_send()
            outward(c).wait_send()


def total(x, count=16, lag=3):
    rows, cols = x.shape
    buffer = pltpu.VMEM((count, rows // count, cols), bf16)
    dma = pltpu.SemaphoreType.DMA((count,))
    return pl.pallas_call(
        functools.partial(total_kernel, count, lag),
        out_shape=jax.ShapeDtypeStruct(x.shape, bf16),
        in_specs=[VMEM],
        out_specs=VMEM,
        scratch_shapes=[buffer] * 4 + [dma] * 6,
        compiler_params=pltpu.CompilerParams(collective_id=2, has_side_effects=True),
        name="total",
    )(x)


def share_kernel(x_ref, o_ref, slots, send, recv):
    d, m = lax.axis_index("dp"), lax.axis_index("mp")
    greet([(d, lax.rem(m + k, 4)) for k in (1, 2, 3)])
    pl.semaphore_wait(pltpu.get_barrier_semaphore(), 3)
    for k in (1, 2, 3):
        remote(x_ref, slots.at[m], send.at[k], recv.at[m], (d, lax.rem(m + k, 4))).start()
    slots[m] = x_ref[...]
    for k in (1, 2, 3):
        o = lax.rem(m + k, 4)
        remote(x_ref, slots.at[o], send.at[k], recv.at[o], (d, o)).wait_recv()
    o_ref[...] = slots[...]
    for k in (1, 2, 3):
        remote(x_ref, slots.at[m], send.at[k], recv.at[m], (d, lax.rem(m + k, 4))).wait_send()


def share(x, number):
    return pl.pallas_call(
        share_kernel,
        out_shape=jax.ShapeDtypeStruct((4,) + x.shape, x.dtype),
        in_specs=[VMEM],
        out_specs=VMEM,
        scratch_shapes=[
            pltpu.VMEM((4,) + x.shape, x.dtype), pltpu.SemaphoreType.DMA((4,)), pltpu.SemaphoreType.DMA((4,)),
        ],
        compiler_params=pltpu.CompilerParams(collective_id=number, has_side_effects=True),
        name="share",
    )(x)


def scatter_kernel(n, x_ref, o_ref, z_ref, came, half, slots, mine, blocks, s1, r1, s2, r2, s3, r3):
    d, m = lax.axis_index("dp"), lax.axis_index("mp")
    core, chip = lax.rem(d, 2), d // 2
    chips = n // 2
    sibling = flip(d, 1)
    greet([(sibling, m)])
    for k in range(1, chips):
        greet([(2 * lax.rem(chip + k, chips) + core, m)])
    for k in (1, 2, 3):
        greet([(d, lax.rem(m + k, 4))])
    pl.semaphore_wait(pltpu.get_barrier_semaphore(), chips + 3)

    def to_sibling(k):
        c = lax.rem(chip + k, chips)
        return remote(x_ref.at[2 * c + 1 - core], came.at[c], s1.at[c], r1.at[c], (sibling, m))

    def to_chip(k):
        c = lax.rem(chip + k, chips)
        return remote(half.at[c], slots.at[chip], s2.at[c], r2.at[chip], (2 * c + core, m))

    def from_chip(k):
        c = lax.rem(chip + k, chips)
        return remote(half.at[c], slots.at[c], s2.at[c], r2.at[c], (2 * c + core, m))

    order = list(range(1, chips)) + [0]
    for k in order:
        to_sibling(k).start()
    for k in order:
        c = lax.rem(chip + k, chips)
        to_sibling(k).wait_recv()
        half[c] = pair_sum(x_ref[2 * c + core], came[c])
        if k:
            to_chip(k).start()
    mine[...] = half[chip].astype(f32)
    for k in range(1, chips):
        from_chip(k).wait_recv()
        mine[...] += slots[lax.rem(chip + k, chips)].astype(f32)
    cols = o_ref.shape[1]
    width = z_ref.shape[2]
    o_ref[...] = mine[:, :cols]
    for j in range(4):
        for t in range(2):
            at = cols + t * 4 * width + j * width
            blocks[j, t] = mine[:, at : at + width].astype(bf16)

    def to_plane(k):
        t = lax.rem(m + k, 4)
        return remote(blocks.at[t], blocks.at[4 + m], s3.at[k], r3.at[m], (d, t))

    for k in (1, 2, 3):
        to_plane(k).start()
    total = blocks[m].astype(f32)
    for k in (1, 2, 3):
        o = lax.rem(m + k, 4)
        remote(blocks.at[o], blocks.at[4 + o], s3.at[k], r3.at[o], (d, o)).wait_recv()
        total = total + blocks[4 + o].astype(f32)
    z_ref[...] = total
    for k in order:
        to_sibling(k).wait_send()
    for k in range(1, chips):
        to_chip(k).wait_send()
    for k in (1, 2, 3):
        to_plane(k).wait_send()


def scatter(x, width):
    n, rows, cols = x.shape
    kept = cols - 8 * width
    chips = n // 2
    dma = pltpu.SemaphoreType.DMA
    buffer = pltpu.VMEM((chips, rows, cols), bf16)
    return pl.pallas_call(
        functools.partial(scatter_kernel, n),
        out_shape=(jax.ShapeDtypeStruct((rows, kept), f32), jax.ShapeDtypeStruct((2, rows, width), f32)),
        in_specs=[VMEM],
        out_specs=[VMEM, VMEM],
        scratch_shapes=[
            buffer, buffer, buffer, pltpu.VMEM((rows, cols), f32), pltpu.VMEM((8, 2, rows, width), bf16),
            dma((chips,)), dma((chips,)), dma((chips,)), dma((chips,)), dma((4,)), dma((4,)),
        ],
        compiler_params=pltpu.CompilerParams(
            collective_id=4, has_side_effects=True, vmem_limit_bytes=56 * 2**20
        ),
        name="scatter",
    )(x)


def vectors_kernel(steps, x_ref, y_ref, ox_ref, oy_ref, xs, ys, xr, yr, s1, r1, s2, r2):
    d, m = lax.axis_index("dp"), lax.axis_index("mp")
    partners = [(flip(d, 1 << i), m) for i in range(steps)] + [(d, flip(m, 1)), (d, flip(m, 2))]
    greet(partners)
    pl.semaphore_wait(pltpu.get_barrier_semaphore(), steps + 2)
    xs[0] = x_ref[...]
    ys[0] = y_ref[...]
    for i in range(steps + 2):
        copies = [remote(ys.at[i], yr.at[i], s2.at[i], r2.at[i], partners[i])]
        if i < steps:
            copies.append(remote(xs.at[i], xr.at[i], s1.at[i], r1.at[i], partners[i]))
        for copy in copies:
            copy.start()
        for copy in copies:
            copy.wait()
        ys[i + 1] = ys[i] + yr[i]
        if i < steps:
            xs[i + 1] = xs[i] + xr[i]
    ox_ref[...] = xs[steps]
    oy_ref[...] = ys[steps + 2]


def vectors(x, y, n):
    steps = n.bit_length() - 1
    dma = pltpu.SemaphoreType.DMA
    return pl.pallas_call(
        functools.partial(vectors_kernel, steps),
        out_shape=(jax.ShapeDtypeStruct(x.shape, f32), jax.ShapeDtypeStruct(y.shape, f32)),
        in_specs=[VMEM, VMEM],
        out_specs=[VMEM, VMEM],
        scratch_shapes=[
            pltpu.VMEM((steps + 1,) + x.shape, f32), pltpu.VMEM((steps + 3,) + y.shape, f32),
            pltpu.VMEM((steps,) + x.shape, f32), pltpu.VMEM((steps + 2,) + y.shape, f32),
            dma((steps,)), dma((steps,)), dma((steps + 2,)), dma((steps + 2,)),
        ],
        compiler_params=pltpu.CompilerParams(collective_id=5, has_side_effects=True),
        name="vectors",
    )(x, y)


def layer_norm(values, norm_gain, offset):
    average = jnp.mean(values, axis=-1, keepdims=True)
    centred = values - average
    variance = jnp.mean(centred * centred, axis=-1, keepdims=True)
    return centred * lax.rsqrt(variance + epsilon) * norm_gain + offset


def exact_gelu(values):
    return jax.nn.gelu(values, approximate=False)


def product(left_side, right_side):
    return jnp.dot(left_side, right_side, preferred_element_type=f32)


def left_product(left_side, right_side):
    return lax.dot_general(left_side, right_side, (((0,), (0,)), ((), ())), preferred_element_type=f32)


def right_product(left_side, right_side):
    return lax.dot_general(left_side, right_side, (((1,), (1,)), ((), ())), preferred_element_type=f32)


def split_heads(matrix):
    return matrix.reshape(matrix.shape[0], -1, HEAD_DIM).transpose(1, 0, 2)


def merge_heads(stacked):
    return stacked.transpose(1, 0, 2).reshape(stacked.shape[1], -1)


def einsum(spec, a, b):
    return jnp.einsum(spec, a, b, preferred_element_type=f32)


def scores_of(q, k, allowed):
    return jnp.where(allowed, factor * einsum("htd,hsd->hts", q, k), masked_value)


def attention_forward(queries, key_rows, value_rows, allowed):
    q, k, v = split_heads(queries), split_heads(key_rows), split_heads(value_rows)
    scores = scores_of(q, k, allowed)
    row_max = jnp.max(scores, axis=-1, keepdims=True)
    exponent = jnp.exp(scores - row_max)
    row_total = jnp.sum(exponent, axis=-1, keepdims=True)
    probabilities = (exponent / row_total).astype(bf16)
    return einsum("hts,hsd->htd", probabilities, v), (row_max + jnp.log(row_total))[..., 0]


def attention_backward(queries, key_rows, value_rows, allowed, log_totals, upstream, inner=None):
    q, k, v, up = split_heads(queries), split_heads(key_rows), split_heads(value_rows), split_heads(upstream)
    p = jnp.exp(scores_of(q, k, allowed) - log_totals[..., None])
    value_grad = einsum("hts,htd->hsd", p.astype(bf16), up)
    prob_grad = einsum("htd,hsd->hts", up, v)
    if inner is None:
        inner = jnp.sum(p * prob_grad, axis=-1)
    score_grad = (p * (prob_grad - inner[..., None])).astype(bf16)
    return (
        merge_heads(factor * einsum("hts,hsd->htd", score_grad, k)),
        merge_heads(factor * einsum("hts,htd->hsd", score_grad, q)),
        merge_heads(value_grad),
    )


def by_owner(grad, n):
    return grad.astype(bf16).reshape(n, grad.shape[0] // n, grad.shape[1])


def shards(
    n, tokens, encoder, lengths, norm_gains, norm_biases, self_in, cross_in, in_biases, self_out, cross_out,
    out_biases, fc_up, up_bias, fc_down, cotangent,
):
    row_count, width = tokens.shape
    clip_count, frame_count = encoder.shape[:2]
    own = self_in.shape[2]
    mp = lax.axis_index("mp")
    positions = jnp.arange(row_count, dtype=jnp.int32)
    clip_ends = jnp.cumsum(lengths[0])
    token_clip = jnp.sum((positions[:, None] >= clip_ends[None, :]).astype(jnp.int32), axis=1)
    self_allowed = (token_clip[:, None] == token_clip[None, :]) & (positions[None, :] <= positions[:, None])
    frames = encoder.reshape(clip_count * frame_count, -1)
    frame_clip = jnp.arange(clip_count * frame_count, dtype=jnp.int32) // frame_count
    cross_allowed = token_clip[:, None] == frame_clip[None, :]

    inputs = tokens.astype(f32)
    normed_self, pull_first = jax.vjp(layer_norm, inputs, norm_gains[0], norm_biases[0])
    normed_self = normed_self.astype(bf16)
    self_queries = (product(normed_self, self_in[0]) + in_biases[0]).astype(bf16)
    self_keys = product(normed_self, self_in[1]).astype(bf16)
    self_values = (product(normed_self, self_in[2]) + in_biases[1]).astype(bf16)
    attended, self_totals = attention_forward(self_queries, self_keys, self_values, self_allowed)
    self_attended = merge_heads(attended).astype(bf16)

    pack = jnp.concatenate(
        [self_out, cross_in[0].T, cross_in[1].T, cross_in[2].T, cross_out, jnp.zeros((64, width), bf16)]
    ).reshape(PLANE, -1, width)
    halves = row_count // 2
    sent = jnp.concatenate([self_attended[:halves], self_attended[halves:]], axis=1)
    weights, parts = gather(pack, sent)
    weights = weights.reshape(4, -1, width)[:, : 5 * own].reshape(4, 5, own, width)
    weights = weights.transpose(1, 0, 2, 3).reshape(5, 4 * own, width)
    whole_self_out, query_in, key_in, value_in, whole_cross_out = weights
    parts = parts.reshape(4, halves, 2, own).transpose(2, 1, 0, 3).reshape(row_count, 4 * own)

    middle = inputs + product(parts, whole_self_out) + out_biases[0]
    normed_cross, pull_second = jax.vjp(layer_norm, middle, norm_gains[1], norm_biases[1])
    normed_cross = normed_cross.astype(bf16)
    biases = share(in_biases[2:].reshape(2, own), 3).transpose(1, 0, 2).reshape(2, 4 * own)
    cross_queries = (right_product(normed_cross, query_in) + biases[0]).astype(bf16)
    cross_keys = right_product(frames, key_in).astype(bf16)
    cross_values = (right_product(frames, value_in) + biases[1]).astype(bf16)
    local_out, local_totals = attention_forward(cross_queries, cross_keys, cross_values, cross_allowed)
    all_totals = share(jnp.pad(local_totals, ((0, 4), (0, 0))), 6)[:, :12]
    top = jnp.max(all_totals, axis=0)
    cross_totals = top + jnp.log(jnp.sum(jnp.exp(all_totals - top), axis=0))
    local_out = local_out * jnp.exp(local_totals - cross_totals)[..., None]
    cross_attended = total(merge_heads(local_out).astype(bf16))
    after_cross = middle + product(cross_attended, whole_cross_out) + out_biases[1]

    normed_mlp, pull_third = jax.vjp(layer_norm, after_cross, norm_gains[2], norm_biases[2])
    normed_mlp = normed_mlp.astype(bf16)
    upward = product(normed_mlp, fc_up) + up_bias
    active, pull_gelu = jax.vjp(exact_gelu, upward)
    active = active.astype(bf16)
    down = total(product(active, fc_down).astype(bf16))
    layer_out = (after_cross + down.astype(f32) + out_biases[2]).astype(bf16)

    grad_low = cotangent
    grad_out = cotangent.astype(f32)
    down_bias_grad = jnp.sum(grad_out, axis=0)
    fc_down_grad = left_product(grad_low, active)
    (upward_grad,) = pull_gelu(right_product(grad_low, fc_down))
    up_bias_grad = jnp.sum(upward_grad, axis=0)
    upward_low = upward_grad.astype(bf16)
    fc_up_grad = left_product(normed_mlp, upward_low)
    mlp_normed_grad = total(right_product(upward_low, fc_up).astype(bf16)).astype(f32)
    cross_side_grad, third_gain_grad, third_bias_grad = pull_third(mlp_normed_grad)
    cross_side_grad = cross_side_grad + grad_out
    cross_bias_grad = jnp.sum(cross_side_grad, axis=0)
    cross_side_low = cross_side_grad.astype(bf16)
    own_cols = lambda a: lax.dynamic_slice_in_dim(a, mp * own, own, axis=1)
    cross_out_grad = left_product(cross_side_low, own_cols(cross_attended))
    cross_upstream = right_product(cross_side_low, whole_cross_out).astype(bf16)
    inner = jnp.sum(split_heads(cross_upstream).astype(f32) * split_heads(cross_attended).astype(f32), axis=-1)
    query_grad, key_grad, value_grad = attention_backward(
        cross_queries, cross_keys, cross_values, cross_allowed, cross_totals, cross_upstream, inner
    )
    cross_query_low = total(query_grad.astype(bf16))
    cross_value_bias = jnp.sum(value_grad, axis=0)
    cross_query_bias = jnp.sum(own_cols(cross_query_low).astype(f32), axis=0)
    key_low, value_low = key_grad.astype(bf16), value_grad.astype(bf16)
    query_weight_grad = left_product(normed_cross, own_cols(cross_query_low))
    key_weight_grad = left_product(frames, key_low)
    value_weight_grad = left_product(frames, value_low)
    encoder_grad = (product(key_low, key_in) + product(value_low, value_in)).astype(bf16)
    encoder_grad = encoder_grad.reshape(clip_count, frame_count, -1)
    cross_normed_grad = product(cross_query_low, query_in)
    middle_grad, second_gain_grad, second_bias_grad = pull_second(cross_normed_grad)
    middle_grad = middle_grad + cross_side_grad
    self_bias_grad = jnp.sum(middle_grad, axis=0)
    middle_low = middle_grad.astype(bf16)
    self_out_grad = left_product(middle_low, self_attended)
    self_upstream = right_product(middle_low, self_out).astype(bf16)
    query_grad, key_grad, value_grad = attention_backward(
        self_queries, self_keys, self_values, self_allowed, self_totals, self_upstream
    )
    self_query_bias = jnp.sum(query_grad, axis=0)
    self_value_bias = jnp.sum(value_grad, axis=0)
    lows = [query_grad.astype(bf16), key_grad.astype(bf16), value_grad.astype(bf16)]
    self_in_grad = [left_product(normed_self, low) for low in lows]
    self_term = sum(right_product(low, self_in[i]) for i, low in enumerate(lows))
    self_normed_grad = total(self_term.astype(bf16)).astype(f32)
    input_grad, first_gain_grad, first_bias_grad = pull_first(self_normed_grad)
    token_grad = (input_grad + middle_grad).astype(bf16)

    grads = self_in_grad + [
        query_weight_grad, fc_up_grad, fc_down_grad, self_out_grad, cross_out_grad, key_weight_grad,
        value_weight_grad,
    ]
    kept, shared = scatter(jnp.concatenate([by_owner(g, n) for g in grads], axis=2), own)
    hidden = fc_up.shape[1]
    pieces = jnp.split(
        kept, [own, 2 * own, 3 * own, 4 * own, 4 * own + hidden, 4 * own + 2 * hidden, 5 * own + 2 * hidden], axis=1
    )
    self_in_grad = jnp.stack(pieces[:3])
    cross_in_grad = jnp.stack([pieces[3], shared[0], shared[1]])
    fc_up_grad, fc_down_grad, self_out_grad, cross_out_grad = (
        pieces[4], pieces[5].T, pieces[6].T, pieces[7].T,
    )
    pad = lambda v: jnp.pad(v, (0, width - v.shape[0]))
    rows = [
        first_gain_grad, second_gain_grad, third_gain_grad, first_bias_grad, second_bias_grad, third_bias_grad,
        self_bias_grad, cross_bias_grad, down_bias_grad, pad(self_query_bias), pad(self_value_bias),
        pad(cross_query_bias),
    ]
    rows = rows + list(up_bias_grad.reshape(-1, width))
    rows = rows + [jnp.zeros((width,), f32)] * (-len(rows) % 8)
    extra = jnp.pad(cross_value_bias[None], ((0, 7), (0, 0)))
    sums, extra = vectors(jnp.stack(rows), extra, n)
    in_biases_grad = jnp.stack(
        [sums[9, :own], sums[10, :own], sums[11, :own], lax.dynamic_slice_in_dim(extra[0], mp * own, own)]
    )
    return (
        layer_out, token_grad, encoder_grad, sums[0:3], sums[3:6], self_in_grad, cross_in_grad, in_biases_grad,
        self_out_grad, cross_out_grad, sums[6:9], fc_up_grad, sums[12 : 12 + hidden // width].reshape(hidden),
        fc_down_grad,
    )


def solution(mesh):
    in_specs = (
        P("dp", None), P("dp", "mp", None), P("dp", None), P(), P(), P(None, None, "mp"), P(None, None, "mp"),
        P(None, "mp"), P("mp", None), P("mp", None), P(), P(None, "mp"), P("mp"), P("mp", None), P("dp", None),
    )
    out_specs = (
        P("dp", None), P("dp", None), P("dp", "mp", None), P(), P(), P(None, "dp", "mp"), P(None, "dp", "mp"),
        P(None, "mp"), P("mp", "dp"), P("mp", "dp"), P(), P("dp", "mp"), P("mp"), P("mp", "dp"),
    )
    body = functools.partial(shards, mesh.shape["dp"])
    return jax.shard_map(body, mesh=mesh, in_specs=in_specs, out_specs=out_specs, check_vma=False)
```

```python
import functools
import types

import jax
import jax.numpy as jnp
from jax import lax
from jax.experimental import pallas as pl
from jax.experimental.pallas import tpu as pltpu
from jax.sharding import PartitionSpec as P

HEAD = 64
PAIR = 2 * HEAD
PLANE = 8
UNIT = 64
FRAMES = 384
epsilon = 1e-05
factor = 0.125
masked_value = -1e30
f32 = jnp.float32
bf16 = jnp.bfloat16
MESH = pl.DeviceIdType.MESH
VMEM = pl.BlockSpec(memory_space=pltpu.VMEM)
SMEM = pl.BlockSpec(memory_space=pltpu.SMEM)
ANY = pl.BlockSpec(memory_space=pl.ANY)


def nn(a, b):
    return jnp.dot(a, b, preferred_element_type=f32)


def nt(a, b):
    return lax.dot_general(a, b, (((1,), (1,)), ((), ())), preferred_element_type=f32)


def tn(a, b):
    return lax.dot_general(a, b, (((0,), (0,)), ((), ())), preferred_element_type=f32)


def flip(index, bit):
    return index + bit - 2 * bit * lax.rem(index // bit, 2)


def remote(src, dst, send, recv, device):
    return pltpu.make_async_remote_copy(
        src_ref=src, dst_ref=dst, send_sem=send, recv_sem=recv, device_id=device, device_id_type=MESH
    )


def greet(devices):
    barrier = pltpu.get_barrier_semaphore()
    for device in devices:
        pl.semaphore_signal(barrier, inc=1, device_id=device, device_id_type=MESH)


def await_greetings(count):
    pl.semaphore_wait(pltpu.get_barrier_semaphore(), count)


def pair_sum(left, right):
    return (left.astype(f32) + right.astype(f32)).astype(bf16)


class Place:
    def __init__(self):
        self.d, self.m = d, m = lax.axis_index("dp"), lax.axis_index("mp")
        self.mine = lax.rem(d, PLANE)
        self.base = d - self.mine
        self.half = m // 2
        self.rank = m + self.half * (3 - 2 * m)
        self.edge, self.inner = self.rank == 0, self.rank == 1
        self.near = flip(m, 1)
        self.peer = 3 - m

    def origin(self, j):
        index = 1 - self.rank if j == 0 else j + 1
        return index + self.half * (3 - 2 * index)

    def line(self, m):
        return (self.d, m)

    def plane(self, s):
        return (self.base + s, self.m)

    def way(self, k):
        s = self.mine
        for bit in (1, 2, 4):
            if k & bit:
                s = flip(s, bit)
        return s


class Gather:
    def __init__(self, at, big, zsend, wsend, wrecv):
        self.at, self.big, self.zsend, self.wsend, self.wrecv = at, big, zsend, wsend, wrecv

    def rows(self, o, s, i):
        unit = 2 * s + i
        matrix, piece = unit // 3, lax.rem(unit, 3)
        return self.big.at[matrix, pl.ds(pl.multiple_of(o * 192 + piece * UNIT, UNIT), UNIT)]

    def copy(self, o, s, i, send, device):
        block = self.rows(o, s, i)
        return remote(block, block, send, self.wrecv.at[o, 2 * s + i], device)

    def came(self, o, s, i):
        self.copy(o, s, i, self.zsend.at[0, 0, 0], self.at.line(self.at.m)).wait_recv()

    def own(self, i, to_peer):
        at = self.at
        return self.copy(at.m, at.mine, i, self.zsend.at[0, to_peer, i], at.line(at.peer if to_peer else at.near))

    def forward(self, j, i):
        at = self.at
        to = at.peer if j == 0 else at.near
        return self.copy(at.origin(j), at.mine, i, self.zsend.at[1 + j, 0, i], at.line(to))

    def spread(self, j, i, k):
        at = self.at
        return self.copy(at.origin(j), at.mine, i, self.wsend.at[j, k, i], at.plane(at.way(k)))

    def corner(self, j, k):
        at = self.at
        i = 0 if k == 2 else 1
        return self.copy(at.origin(j), at.way(k), i, self.wsend.at[j, 0, i], at.plane(at.way(6 - k)))

    def sibling(self, j, k, i):
        at = self.at
        return self.copy(at.origin(j), at.way(k), i, self.wsend.at[j, k + 1, i], at.plane(at.way(1)))

    def start(self):
        at = self.at
        for i in (0, 1):
            self.own(i, 0).start()

        @pl.when(at.inner)
        def _():
            for i in (0, 1):
                self.own(i, 1).start()

    def from_line(self, j):
        at = self.at
        for i in (0, 1):
            self.came(at.origin(j), at.mine, i)

        @pl.when(at.inner)
        def _():
            for i in (0, 1):
                self.forward(j, i).start()

        for k in (2, 4, 1):
            for i in (0, 1):
                self.spread(j, i, k).start()

    def from_sides(self, j):
        o = self.at.origin(j)
        for k in (2, 4):
            for i in (0, 1):
                self.came(o, self.at.way(k), i)
                if i == (0 if k == 2 else 1):
                    self.corner(j, k).start()
                self.sibling(j, k, i).start()

    def from_corner(self, j):
        o = self.at.origin(j)
        for i in (0, 1):
            self.came(o, self.at.way(6), i)
            self.sibling(j, 6, i).start()

    def from_sibling(self, j):
        o = self.at.origin(j)
        for k in (1, 3, 5, 7):
            for i in (0, 1):
                self.came(o, self.at.way(k), i)

    def finish(self):
        at = self.at
        for i in (0, 1):
            self.own(i, 0).wait_send()

        @pl.when(at.inner)
        def _():
            for i in (0, 1):
                self.own(i, 1).wait_send()
                for j in range(3):
                    self.forward(j, i).wait_send()

        for j in range(3):
            for i in (0, 1):
                for k in (2, 4, 1):
                    self.spread(j, i, k).wait_send()
                for k in (2, 4, 6):
                    self.sibling(j, k, i).wait_send()
            for k in (2, 4):
                self.corner(j, k).wait_send()

    @staticmethod
    def semaphores():
        dma = pltpu.SemaphoreType.DMA
        return [dma((4, 2, 2)), dma((3, 8, 2)), dma((4, 2 * PLANE))]


class Parts:
    def __init__(self, at, slots, send, recv):
        self.at, self.slots, self.send, self.recv = at, slots, send, recv

    def copy(self, o, send, to):
        return remote(self.slots.at[o], self.slots.at[o], send, self.recv.at[o], self.at.line(to))

    def own(self, to_peer):
        at = self.at
        return self.copy(at.m, self.send.at[to_peer], at.peer if to_peer else at.near)

    def forward(self, j):
        at = self.at
        return self.copy(at.origin(j), self.send.at[2 + j], at.peer if j == 0 else at.near)

    def start(self):
        self.own(0).start()

        @pl.when(self.at.inner)
        def _():
            self.own(1).start()

    def step(self, j):
        self.copy(self.at.origin(j), self.send.at[0], self.at.m).wait_recv()

        @pl.when(self.at.inner)
        def _():
            self.forward(j).start()

    def finish(self):
        self.own(0).wait_send()

        @pl.when(self.at.inner)
        def _():
            self.own(1).wait_send()
            for j in range(3):
                self.forward(j).wait_send()

    @staticmethod
    def semaphores():
        dma = pltpu.SemaphoreType.DMA
        return [dma((5,)), dma((4,))]


class Direct:
    def __init__(self, at, slots, send, recv):
        self.at, self.slots, self.send, self.recv = at, slots, send, recv

    def copy(self, o, k):
        to = lax.rem(self.at.m + k, 4)
        return remote(self.slots.at[o], self.slots.at[o], self.send.at[k], self.recv.at[o], self.at.line(to))

    def start(self):
        for k in (1, 2, 3):
            self.copy(self.at.m, k).start()

    def finish(self):
        for k in (1, 2, 3):
            self.copy(lax.rem(self.at.m + k, 4), k).wait_recv()
        for k in (1, 2, 3):
            self.copy(self.at.m, k).wait_send()

    @staticmethod
    def semaphores():
        dma = pltpu.SemaphoreType.DMA
        return [dma((4,)), dma((4,))]


class Everyone:
    def __init__(self, at, size, stride, slots, send, recv):
        self.at, self.size, self.stride, self.slots, self.send, self.recv = at, size, stride, slots, send, recv
        self.place = lax.rem(at.d // stride, size)

    def copy(self, o, k):
        to = self.at.d + (lax.rem(self.place + k, self.size) - self.place) * self.stride
        return remote(
            self.slots.at[o], self.slots.at[o], self.send.at[k], self.recv.at[o], (to, self.at.m)
        )

    def start(self):
        for k in range(1, self.size):
            self.copy(self.place, k).start()

    def finish(self):
        for k in range(1, self.size):
            self.copy(lax.rem(self.place + k, self.size), k).wait_recv()
        for k in range(1, self.size):
            self.copy(self.place, k).wait_send()
        total = self.slots[0]
        for o in range(1, self.size):
            total = total + self.slots[o]
        return total

    @staticmethod
    def semaphores(size):
        dma = pltpu.SemaphoreType.DMA
        return [dma((size,)), dma((size,))]


class Scatter:
    def __init__(self, at, n, x, came, slots, s1, r1, s2, r2):
        self.at, self.x, self.came, self.slots = at, x, came, slots
        self.s1, self.r1, self.s2, self.r2 = s1, r1, s2, r2
        self.core, self.chip, self.chips = lax.rem(at.d, 2), at.d // 2, n // 2
        self.order = list(range(1, self.chips)) + [0]

    def to_sibling(self, k):
        c = lax.rem(self.chip + k, self.chips)
        other = 1 - self.core
        return remote(
            self.x.at[2 * c + other], self.came.at[c], self.s1.at[c], self.r1.at[c],
            (2 * self.chip + other, self.at.m),
        )

    def between(self, k, slot):
        c = lax.rem(self.chip + k, self.chips)
        return remote(
            self.x.at[2 * c + self.core], self.slots.at[slot], self.s2.at[c], self.r2.at[slot],
            (2 * c + self.core, self.at.m),
        )

    def start(self):
        for k in self.order:
            self.to_sibling(k).start()

    def fold(self):
        for k in self.order:
            c = lax.rem(self.chip + k, self.chips)
            self.to_sibling(k).wait_recv()
            block = 2 * c + self.core
            self.x[block] = pair_sum(self.x[block], self.came[c])
            if k:
                self.between(k, self.chip).start()

    def finish(self):
        total = self.x[2 * self.chip + self.core].astype(f32)
        for k in range(1, self.chips):
            c = lax.rem(self.chip + k, self.chips)
            self.between(k, c).wait_recv()
            total = total + self.slots[c].astype(f32)
        for k in self.order:
            self.to_sibling(k).wait_send()
        for k in range(1, self.chips):
            self.between(k, self.chip).wait_send()
        return total

    @staticmethod
    def buffers(n, rows, cols):
        half = pltpu.VMEM((n // 2, rows, cols), bf16)
        dma = pltpu.SemaphoreType.DMA((n // 2,))
        return [half, half, dma, dma, dma, dma]


class Total:
    def __init__(self, at, blocks, x, ends, other, out, sa, ra, sb, rb, sr, rr, rooms=None):
        self.at, self.blocks, self.rooms = at, blocks, rooms or blocks
        self.x, self.ends, self.other, self.out = x, ends, other, out
        self.sa, self.ra, self.sb, self.rb, self.sr, self.rr = sa, ra, sb, rb, sr, rr
        self.count = len(blocks)

    def inward(self, c):
        b = self.blocks[c]
        return remote(self.x.at[b], self.ends.at[self.rooms[c]], self.sa.at[c], self.ra.at[c], self.at.line(self.at.near))

    def across(self, c):
        b = self.blocks[c]
        return remote(self.x.at[b], self.other.at[self.rooms[c]], self.sb.at[c], self.rb.at[c], self.at.line(self.at.peer))

    def outward(self, c):
        b = self.blocks[c]
        return remote(self.out.at[b], self.out.at[b], self.sr.at[c], self.rr.at[c], self.at.line(self.at.near))

    def send(self, c):
        @pl.when(self.at.edge)
        def _():
            self.inward(c).start()

    def fold(self, c):
        @pl.when(self.at.inner)
        def _():
            b = self.blocks[c]
            self.inward(c).wait_recv()
            self.x[b] = pair_sum(self.x[b], self.ends[self.rooms[c]])
            self.across(c).start()

    def close(self, c):
        @pl.when(self.at.inner)
        def _():
            b = self.blocks[c]
            self.across(c).wait_recv()
            self.out[b] = pair_sum(self.x[b], self.other[self.rooms[c]])
            self.outward(c).start()

    def take(self, c):
        @pl.when(self.at.edge)
        def _():
            self.outward(c).wait_recv()

    def run(self, lag=3):
        for c in range(self.count):
            self.send(c)
        for i in range(self.count + lag):
            if i < self.count:
                self.fold(i)
            if i >= lag:
                self.close(i - lag)
        for c in range(self.count):
            self.take(c)

    def finish(self):
        @pl.when(self.at.edge)
        def _():
            for c in range(self.count):
                self.inward(c).wait_send()

        @pl.when(self.at.inner)
        def _():
            for c in range(self.count):
                self.across(c).wait_send()
                self.outward(c).wait_send()

    @staticmethod
    def semaphores(count):
        return [pltpu.SemaphoreType.DMA((count,))] * 6


def normal(values):
    average = jnp.mean(values, axis=-1, keepdims=True)
    centred = values - average
    variance = jnp.mean(centred * centred, axis=-1, keepdims=True)
    scale = lax.rsqrt(variance + epsilon)
    return centred * scale, scale


def row_blocks(count, size, body):
    def step(i, carry):
        body(pl.ds(pl.multiple_of(i * size, size), size))
        return carry

    lax.fori_loop(0, count // size, step, 0)


def iota(shape, axis):
    return lax.broadcasted_iota(jnp.int32, shape, axis)


def pair_tiles(tile):
    turned = pltpu.roll(tile, HEAD, axis=1)
    low = iota(tile.shape, 1) < HEAD
    return jnp.where(low, tile, turned), jnp.where(low, turned, tile)


def back_normal(values, upstream, gain):
    xhat, scale = normal(values)
    scaled = upstream * gain
    first = jnp.mean(scaled, axis=-1, keepdims=True)
    second = jnp.mean(scaled * xhat, axis=-1, keepdims=True)
    return scale * (scaled - first - xhat * second), upstream * xhat


def by_eights(values):
    return jnp.sum(values.reshape(-1, 8, values.shape[1]), axis=0)


def own_columns(at, source, target):
    width = target.shape[1]
    for j in range(4):

        @pl.when(at.m == j)
        def _(j=j):
            target[...] = source[:, j * width : (j + 1) * width]


def self_mask(rows, keys, start, clip_start):
    row = iota((rows, keys), 0) + start
    col = iota((rows, keys), 1)
    return jnp.logical_and(col <= row, (row >= clip_start) == (col >= clip_start))


def self_forward(r, clip_start):
    rows = r.tokens.shape[0]

    def normed(block):
        xhat, _ = normal(r.tokens[block].astype(f32))
        r.n1[block] = (xhat * r.norm_gains[0:1] + r.norm_biases[0:1]).astype(bf16)

    row_blocks(rows, 64, normed)
    r.q1[...] = (nt(r.n1[...], r.self_in[0]) + r.in_biases[0:1]).astype(bf16)
    r.k1[...] = nt(r.n1[...], r.self_in[1]).astype(bf16)
    r.v1[...] = (nt(r.n1[...], r.self_in[2]) + r.in_biases[1:2]).astype(bf16)
    half = rows // 2
    for part in range(2):
        block, keys = pl.ds(part * half, half), (part + 1) * half
        allowed = self_mask(half, keys, part * half, clip_start)
        for h in range(r.q1.shape[1] // HEAD):
            cols = pl.ds(h * HEAD, HEAD)
            scores = nt(r.q1[block, cols] * bf16(factor), r.k1[0:keys, cols])
            scores = jnp.where(allowed, scores, masked_value)
            top = jnp.max(scores, axis=1, keepdims=True)
            power = jnp.exp(scores - top)
            total = jnp.sum(power, axis=1, keepdims=True)
            chance = (power * (1 / total)).astype(bf16)
            r.o1[block, cols] = nn(chance, r.v1[0:keys, cols]).astype(bf16)
            r.lse1[block, pl.ds(h, 1)] = top + jnp.log(total)


def self_backward(r, clip_start):
    rows = r.tokens.shape[0]
    half = rows // 2
    r.dk_sum[...] = jnp.zeros_like(r.dk_sum)
    r.dv_sum[...] = jnp.zeros_like(r.dv_sum)
    bias = []
    for part in range(2):
        block, keys = pl.ds(part * half, half), (part + 1) * half
        allowed = self_mask(half, keys, part * half, clip_start)
        for h in range(r.q1.shape[1] // HEAD):
            cols = pl.ds(h * HEAD, HEAD)
            query, upstream = r.q1[block, cols] * bf16(factor), r.do1[block, cols]
            scores = jnp.where(allowed, nt(query, r.k1[0:keys, cols]), masked_value)
            chance = jnp.exp(scores - r.lse1[block, pl.ds(h, 1)])
            slope = nt(upstream, r.v1[0:keys, cols])
            inner = jnp.sum(chance * slope, axis=1, keepdims=True)
            change = (chance * (slope - inner)).astype(bf16)
            query_grad = nn(change, r.k1[0:keys, cols]) * factor
            r.dq1[block, cols] = query_grad.astype(bf16)
            bias.append(jnp.sum(query_grad, axis=0, keepdims=True))
            r.dk_sum[cols, 0:keys] += tn(query, change)
            r.dv_sum[cols, 0:keys] += tn(upstream, chance.astype(bf16))
    r.dk1[...] = r.dk_sum[...].T.astype(bf16)
    r.dv1[...] = r.dv_sum[...].T.astype(bf16)
    heads = len(bias) // 2
    for h in range(heads):
        r.in_bias_sums[0:1, h * HEAD : (h + 1) * HEAD] = bias[h] + bias[heads + h]


def keys_and_values(r, matrix, bias, pairs):
    both = [nt(r.frames[clip], r.big[matrix]) for clip in range(2)]
    if bias is not None:
        both = [value + r.bias[bias : bias + 1] for value in both]
    for t in range(both[0].shape[1] // PAIR):
        first, second = (value[:, t * PAIR : (t + 1) * PAIR] for value in both)
        low = iota(first.shape, 1) < HEAD
        turned_first, turned_second = pltpu.roll(first, HEAD, axis=1), pltpu.roll(second, HEAD, axis=1)
        pairs[:, 2 * t * PAIR : (2 * t + 1) * PAIR] = jnp.where(low, first, turned_second).astype(bf16)
        pairs[:, (2 * t + 1) * PAIR : (2 * t + 2) * PAIR] = jnp.where(low, turned_first, second).astype(bf16)


def to_pairs(value, pairs, block, clip_start, scale):
    rows = value.shape[0]
    keep = (iota((rows, PAIR), 1) < HEAD) == (iota((rows, PAIR), 0) + block.start < clip_start)
    for t in range(value.shape[1] // PAIR):
        for e, tile in enumerate(pair_tiles(value[:, t * PAIR : (t + 1) * PAIR])):
            at = (2 * t + e) * PAIR
            pairs[block, at : at + PAIR] = (jnp.where(keep, tile, 0.0) * scale).astype(bf16)


def from_pair(even, odd, first):
    low = iota(even.shape, 1) < HEAD
    even = jnp.where(first, even, pltpu.roll(even, HEAD, axis=1))
    odd = jnp.where(first, pltpu.roll(odd, HEAD, axis=1), odd)
    return jnp.where(low, even, odd)


GROUP = 2 * PAIR
GROUP_HEADS = 4


def cross_forward(r, g, clip_start, frame_count):
    rows = r.q_pair.shape[0]
    lane = iota((rows, PAIR), 1)
    first = iota((rows, PAIR), 0) < clip_start
    valid = iota((rows, FRAMES), 1) < frame_count
    r.stats[g] = jnp.zeros_like(r.stats[g])

    def body(j, carry):
        halves = []
        for e in (0, 1):
            cols = pl.ds(pl.multiple_of(2 * GROUP * g + 2 * PAIR * j + PAIR * e, PAIR), PAIR)
            scores = jnp.where(valid, nt(r.q_pair[:, cols], r.k_pair[:, cols]), masked_value)
            top = jnp.max(scores, axis=1, keepdims=True)
            power = jnp.exp(scores - top)
            total = jnp.sum(power, axis=1, keepdims=True)
            halves.append(nn(power.astype(bf16), r.v_pair[:, cols]) * (1 / total))
            r.stats[g] = jnp.where(lane == 2 * j + e, top + jnp.log(total), r.stats[g])
        r.g3[:, pl.ds(pl.multiple_of(GROUP * g + PAIR * j, PAIR), PAIR)] = from_pair(*halves, first)
        return carry

    lax.fori_loop(0, 2, body, 0)


def merge_stats(r, g, exchange, at):
    exchange.finish()
    every = [r.stat_slots[g, o] for o in range(4)]
    top = functools.reduce(jnp.maximum, every)
    total = top + jnp.log(sum(jnp.exp(value - top) for value in every))
    weight = jnp.exp(r.stat_slots[g, at.m] - total)
    spare = jnp.zeros((PAIR - 16, total.shape[1]), f32)
    r.stats[g] = jnp.concatenate([total, weight, spare], axis=0).T
    low = iota((total.shape[1], PAIR), 1) < HEAD
    for j in range(2):
        even, odd = (r.stats[g, :, 8 + 2 * j + e : 9 + 2 * j + e] for e in (0, 1))
        cols = pl.ds(g * GROUP + j * PAIR, PAIR)
        r.part_a[:, cols] = (r.g3[:, cols] * jnp.where(low, even, odd)).astype(bf16)


def cross_backward(r, g, clip_start, frame_count):
    rows = r.q_pair.shape[0]
    lane = iota((rows, PAIR), 1)
    first = iota((rows, PAIR), 0) < clip_start
    valid = iota((rows, FRAMES), 1) < frame_count

    def column(index):
        return jnp.sum(jnp.where(lane == index, r.stats[g], 0.0), axis=1, keepdims=True)

    def body(j, carry):
        halves = []
        for e in (0, 1):
            cols = pl.ds(pl.multiple_of(2 * GROUP * g + 2 * PAIR * j + PAIR * e, PAIR), PAIR)
            query, key, upstream = r.q_pair[:, cols], r.k_pair[:, cols], r.do_pair[:, cols]
            scores = jnp.where(valid, nt(query, key), masked_value)
            chance = jnp.exp(scores - column(2 * j + e))
            slope = nt(upstream, r.v_pair[:, cols])
            change = (chance * (slope - column(16 + 2 * j + e))).astype(bf16)
            value_grad = tn(upstream, chance.astype(bf16)).astype(bf16)
            key_grad = tn(query, change).astype(bf16)
            halves.append(nn(change, key) * factor)
            head = pl.ds(pl.multiple_of(GROUP * g + PAIR * j + HEAD * e, HEAD), HEAD)
            for clip in range(2):
                r.dv_t[clip, head] = value_grad[clip * HEAD : (clip + 1) * HEAD]
                r.dk_t[clip, head] = key_grad[clip * HEAD : (clip + 1) * HEAD]
        cols = pl.ds(pl.multiple_of(GROUP * g + PAIR * j, PAIR), PAIR)
        r.part_a[:, cols] = from_pair(*halves, first).astype(bf16)
        return carry

    lax.fori_loop(0, 2, body, 0)


def put_blocks(x, column, first_row, value):
    per = x.shape[1]
    for i in range(value.shape[0] // per):
        x[first_row // per + i, :, column : column + value.shape[1]] = value[i * per : (i + 1) * per].astype(bf16)


def weight_grad(x, column, left, right):
    part = left.shape[1] // 2
    return [
        functools.partial(
            lambda i: put_blocks(x, column, i * part, tn(left[:, i * part : (i + 1) * part], right[...])), i
        )
        for i in range(2)
    ]


def interleave(steps, jobs):
    done = 0
    for i, step in enumerate(steps):
        step()
        while done < len(jobs) and done * len(steps) < (i + 1) * len(jobs):
            jobs[done]()
            done += 1
    for job in jobs[done:]:
        job()


def layer_kernel(names, n, *refs):
    r = types.SimpleNamespace(**dict(zip(names, refs)))
    at = Place()
    own = r.self_out.shape[0]
    rows, width = r.tokens.shape
    frame_count = r.encoder.shape[1]
    clip_start = r.lengths[0, 0]
    half = rows // 2
    groups = width // GROUP
    spare = pl.ds(0, rows)
    r.n3, r.low, r.dn1 = r.big.at[5, spare], r.big.at[0, spare], r.dn3
    r.a, r.dul = r.layer_out, r.token_grad
    greet([(lax.rem(at.d + k, n), at.m) for k in range(1, n)] + [at.line(lax.rem(at.m + k, 4)) for k in (1, 2, 3)])

    block = pl.ds(pl.multiple_of(at.m * own, UNIT), own)
    loads = [
        pltpu.make_async_copy(source, target, r.load.at[i])
        for i, (source, target) in enumerate(
            (
                (r.self_out, r.big.at[0, block]), (r.cross_in.at[0], r.big.at[1, block]),
                (r.cross_in.at[1], r.big.at[2, block]), (r.cross_in.at[2], r.big.at[3, block]),
                (r.cross_out, r.big.at[4, block]), (r.fc_up_in, r.fc_up), (r.fc_down_in, r.fc_down),
                (r.cotangent_in, r.cotangent),
            )
        )
    ]
    for load in loads:
        load.start()
    for load in loads[:5]:
        load.wait()
    r.bias_slots[at.m, 0:2, 0:own] = r.in_biases[2:4]
    await_greetings(n + 2)

    gather = Gather(at, r.big, r.g_0, r.g_1, r.g_2)
    gather.start()
    biases = Direct(at, r.bias_slots, r.b_0, r.b_1)
    biases.start()
    self_forward(r, clip_start)
    r.parts[at.m, :, 0:own] = r.o1[0:half]
    r.parts[at.m, :, own : 2 * own] = r.o1[half:rows]
    parts = Parts(at, r.parts, r.p_0, r.p_1)
    gather.from_line(0)
    parts.start()
    for clip in range(2):
        r.frames[clip] = jnp.zeros_like(r.frames[clip])
        r.frames[clip, 0:frame_count] = r.encoder[clip]
    gather.from_line(1)
    gather.from_line(2)
    gather.from_sides(0)
    parts.step(0)
    gather.from_sides(1)
    parts.step(1)
    gather.from_sides(2)
    for j in range(3):
        gather.from_corner(j)
    biases.finish()
    for o in range(4):
        r.bias[:, o * own : (o + 1) * own] = r.bias_slots[o, :, 0:own]
    for j in range(3):
        gather.from_sibling(j)
    keys_and_values(r, 2, None, r.k_pair)
    keys_and_values(r, 3, 1, r.v_pair)
    parts.step(2)

    for o in range(4):
        cols = pl.ds(o * own, own)
        r.part_b[0:half, cols] = r.parts[o, :, 0:own]
        r.part_b[half:rows, cols] = r.parts[o, :, own : 2 * own]
    r.x2[...] = r.tokens[...].astype(f32) + nn(r.part_b[...], r.big[0]) + r.out_biases[0:1]

    def second_norm(block):
        xhat, _ = normal(r.x2[block])
        r.n2[block] = (xhat * r.norm_gains[1:2] + r.norm_biases[1:2]).astype(bf16)

    row_blocks(rows, 64, second_norm)
    queries = (nt(r.n2[...], r.big[1]) + r.bias[0:1]).astype(bf16).astype(f32)
    to_pairs(queries, r.q_pair, pl.ds(0, rows), clip_start, factor)

    tiles = [
        (pl.ds(i * half, half), pl.ds(t * PAIR, PAIR)) for t in range(width // PAIR) for i in range(2)
    ]
    strips = [pl.ds(c * 32, 32) for c in range(rows // 32)]
    per = len(tiles) // groups
    o2_sum = Total(at, tiles, r.part_a, r.ends, r.other_a, r.o2, *(getattr(r, f"t_{i}") for i in range(6)))
    exchange = [Direct(at, r.stat_slots.at[g], r.s_0.at[g], r.s_1.at[g]) for g in range(groups)]

    def merged(g):
        merge_stats(r, g, exchange[g], at)
        for c in range(per * g, per * (g + 1)):
            o2_sum.send(c)

    def add_cross(g):
        for c in range(per * g, per * (g + 1)):
            o2_sum.take(c)
        cols = pl.ds(g * GROUP, GROUP)
        term = nn(r.o2[:, cols], r.big[4, cols])
        r.x3[...] = (r.x2[...] + r.out_biases[1:2] if g == 0 else r.x3[...]) + term

    for g in range(groups):
        cross_forward(r, g, clip_start, frame_count)
        r.stat_slots[g, at.m] = r.stats[g].T[0:8]
        exchange[g].start()
        if g:
            merged(g - 1)
        if g > 1:
            for c in range(per * (g - 2), per * (g - 1)):
                o2_sum.fold(c)
    merged(groups - 1)
    for g in range(groups):
        if g >= groups - 2:
            for c in range(per * g, per * (g + 1)):
                o2_sum.fold(c)
        if g:
            for c in range(per * (g - 1), per * g):
                o2_sum.close(c)
            add_cross(g - 1)
    for c in range(per * (groups - 1), per * groups):
        o2_sum.close(c)
    add_cross(groups - 1)
    gather.finish()
    parts.finish()
    o2_sum.finish()

    for load in loads[5:]:
        load.wait()
    dn3_sum = Total(at, strips, r.part_a, r.ends, r.other_b, r.dn3, *(getattr(r, f"u_{i}") for i in range(6)))
    down_sum = Total(
        at, strips, r.part_b, r.ends_b, r.other_c, r.down, *(getattr(r, f"v_{i}") for i in range(6)),
        rooms=strips[: len(strips) // 2] * 2,
    )

    for part in range(2):
        rows_of = pl.ds(part * half, half)

        def third_norm(block, part=part):
            block = pl.ds(pl.multiple_of(part * half + block.start, 64), 64)
            xhat, _ = normal(r.x3[block])
            r.n3[block] = (xhat * r.norm_gains[2:3] + r.norm_biases[2:3]).astype(bf16)

        row_blocks(half, 64, third_norm)
        upward = nn(r.n3[rows_of], r.fc_up[...]) + r.up_bias[...]
        normal_share = 0.5 * (1.0 + lax.erf(upward * (0.5**0.5)))
        density = jnp.exp(-0.5 * upward * upward) * 0.3989422804014327
        r.a[rows_of] = (upward * normal_share).astype(bf16)
        slope = nt(r.cotangent[rows_of], r.fc_down[...])
        change = slope * (normal_share + upward * density)
        r.up_sum[part] = by_eights(change)
        r.dul[rows_of] = change.astype(bf16)
        r.part_a[rows_of] = nt(r.dul[rows_of], r.fc_up[...]).astype(bf16)
        for c in range(part * len(strips) // 2, (part + 1) * len(strips) // 2):
            dn3_sum.send(c)

    scatter_1 = Scatter(at, n, r.grads_1, r.came_1, r.slots_1, *(getattr(r, f"x_{i}") for i in range(4)))
    scatter_2 = Scatter(at, n, r.grads_1, r.came_2, r.slots_2, *(getattr(r, f"y_{i}") for i in range(4)))
    scatter_3 = Scatter(at, n, r.grads_3, r.came_3, r.slots_3, *(getattr(r, f"w_{i}") for i in range(4)))

    def down_part(part):
        rows_of = pl.ds(part * half, half)
        r.part_b[rows_of] = nn(r.a[rows_of], r.fc_down[...]).astype(bf16)
        if part == 0:
            for c in range(len(strips) // 2):
                down_sum.send(c)

    for k in range(3):
        r.bias_sums[k] = jnp.zeros_like(r.bias_sums[k])
        r.gain_sums[k] = jnp.zeros_like(r.gain_sums[k])
        r.out_sums[k] = jnp.zeros_like(r.out_sums[k])

    def back_third(block):
        upstream = r.dn3[block].astype(f32)
        grad = r.cotangent[block].astype(f32)
        change, gain = back_normal(r.x3[block], upstream, r.norm_gains[2:3])
        total = grad + change
        r.g3[block] = total
        r.low[block] = total.astype(bf16)
        r.gain_sums[2] += by_eights(gain)
        r.bias_sums[2] += by_eights(upstream)
        r.out_sums[1] += by_eights(total)
        r.out_sums[2] += by_eights(grad)

    lag = 3

    def sum_steps(total, taken):
        def step(i):
            if i < total.count:
                total.fold(i)
            c = i - lag
            if c >= 0:
                total.close(c)
                if c % 2:
                    total.take(c - 1)
                    total.take(c)
                    taken(pl.ds((c - 1) * 32, 64))

        return [functools.partial(step, i) for i in range(total.count + lag)]

    jobs = [functools.partial(down_part, 0)]
    jobs += weight_grad(r.grads_1, 0, r.n3, r.dul)
    jobs += weight_grad(r.grads_1, width, r.cotangent, r.a)
    jobs += [scatter_1.start, functools.partial(down_part, 1), scatter_1.fold]
    interleave(sum_steps(dn3_sum, back_third), jobs)
    dn3_sum.finish()

    upstream = nt(r.low[...], r.big[4]).astype(bf16).astype(f32)
    to_pairs(upstream, r.do_pair, pl.ds(0, rows), clip_start, 1.0)
    r.do2_sum[...] = by_eights(upstream)
    lane = iota((rows, PAIR), 1)
    for t in range(width // PAIR):
        cols = slice(t * PAIR, (t + 1) * PAIR)
        terms = upstream[:, cols] * r.o2[:, cols].astype(f32)
        g, j = t // 2, t % 2
        even = jnp.sum(jnp.where(lane < HEAD, terms, 0.0), axis=1, keepdims=True)
        odd = jnp.sum(jnp.where(lane < HEAD, 0.0, terms), axis=1, keepdims=True)
        r.stats[g] = jnp.where(lane == 16 + 2 * j, even, jnp.where(lane == 17 + 2 * j, odd, r.stats[g]))

    dq_sum = Total(at, tiles, r.part_a, r.ends, r.other_a, r.dq2, *(getattr(r, f"q_{i}") for i in range(6)))

    def add_query(g):
        for c in range(per * g, per * (g + 1)):
            dq_sum.take(c)
        cols = pl.ds(g * GROUP, GROUP)
        term = nn(r.dq2[:, cols], r.big[1, cols])
        r.dn2[...] = term if g == 0 else r.dn2[...] + term

    down_half = len(strips) // 2
    for g in range(groups):
        cross_backward(r, g, clip_start, frame_count)
        for c in range(per * g, per * (g + 1)):
            dq_sum.send(c)
        if g:
            for c in range(per * (g - 1), per * g):
                dq_sum.fold(c)
        else:
            for c in range(down_half):
                down_sum.fold(c)
            for c in range(down_half):
                down_sum.close(c)
    for c in range(down_half):
        down_sum.take(c)
    for c in range(down_half, 2 * down_half):
        down_sum.send(c)

    def result_1():
        total = scatter_1.finish()
        r.fc_up_grad[...] = total[:, 0:width]
        r.fc_down_grad[...] = total[:, width:]

    def frame_grads(clip):
        value = tn(r.dk_t[clip], r.big[2]) + tn(r.dv_t[clip], r.big[3])
        r.encoder_grad[clip] = value[0:frame_count].astype(bf16)

    def cross_weight(source, column):
        value = sum(nn(source[clip], r.frames[clip]) for clip in range(2))
        value = value.astype(bf16).T
        put_blocks(r.grads_1, column, 0, value)

    def cross_out_grad():
        own_columns(at, r.o2, r.own_part)
        for job in weight_grad(r.grads_3, 5 * own, r.low, r.own_part):
            job()

    jobs = [
        result_1,
        functools.partial(cross_weight, r.dk_t, 0),
        functools.partial(cross_weight, r.dv_t, width),
        scatter_2.start,
        cross_out_grad,
        functools.partial(frame_grads, 0),
        scatter_2.fold,
        functools.partial(frame_grads, 1),
    ]
    steps = [functools.partial(dq_sum.fold, c) for c in range(per * (groups - 1), per * groups)]
    for g in range(groups):
        steps += [functools.partial(dq_sum.close, c) for c in range(per * g, per * (g + 1))]
        steps += [functools.partial(add_query, g)]
    interleave(steps, jobs)
    dq_sum.finish()

    def back_second(block):
        upstream = r.dn2[block]
        change, gain = back_normal(r.x2[block], upstream, r.norm_gains[1:2])
        total = r.g3[block] + change
        r.x2[block] = total
        r.low[block] = total.astype(bf16)
        r.gain_sums[1] += by_eights(gain)
        r.bias_sums[1] += by_eights(upstream)
        r.out_sums[0] += by_eights(total)

    row_blocks(rows, 64, back_second)
    upstream = nt(r.low[...], r.self_out[...])
    r.do1[...] = upstream.astype(bf16)
    self_backward(r, clip_start)
    for c in range(down_half, 2 * down_half):
        down_sum.fold(c)
    dn1_sum = Total(at, strips, r.part_b, r.ends, r.other_b, r.dn1, *(getattr(r, f"z_{i}") for i in range(6)))
    for c in range(down_half, 2 * down_half):
        down_sum.close(c)
    down_sum.finish()
    for part in range(2):
        rows_of = pl.ds(part * half, half)
        value = nn(r.dq1[rows_of], r.self_in[0]) + nn(r.dk1[rows_of], r.self_in[1])
        r.part_b[rows_of] = (value + nn(r.dv1[rows_of], r.self_in[2])).astype(bf16)
        for c in range(part * down_half, (part + 1) * down_half):
            dn1_sum.send(c)

    def back_first(block):
        upstream = r.dn1[block].astype(f32)
        change, gain = back_normal(r.tokens[block].astype(f32), upstream, r.norm_gains[0:1])
        r.token_grad[block] = (change + r.x2[block]).astype(bf16)
        r.gain_sums[0] += by_eights(gain)
        r.bias_sums[0] += by_eights(upstream)

    def query_weight():
        own_columns(at, r.dq2, r.own_part)
        for job in weight_grad(r.grads_3, 3 * own, r.n2, r.own_part):
            job()
        total = jnp.sum(r.own_part[...].astype(f32), axis=0, keepdims=True)
        r.in_bias_sums[2:3, 0:own] = total

    def squeeze(values):
        return jnp.sum(values, axis=0, keepdims=True)

    early = [Everyone(at, PLANE, 1, r.early_slots, r.e_0, r.e_1)]
    late = [Everyone(at, PLANE, 1, r.late_slots, r.l_0, r.l_1)]
    if n > PLANE:
        early.append(Everyone(at, n // PLANE, PLANE, r.early_slots_2, r.m_0, r.m_1))
        late.append(Everyone(at, n // PLANE, PLANE, r.late_slots_2, r.n_0, r.n_1))

    def finish_all(stages):
        total = stages[0].finish()
        for stage in stages[1:]:
            stage.slots[stage.place] = total
            stage.start()
            total = stage.finish()
        return total


    def early_vectors():
        r.in_bias_sums[1:2, 0:own] = squeeze(r.do1[...].astype(f32))
        total = squeeze(r.do2_sum[...])
        for j in range(4):

            @pl.when(at.m == j)
            def _(j=j):
                r.in_bias_sums[3:4, 0:own] = total[:, j * own : (j + 1) * own]

        lines = [squeeze(r.gain_sums[k]) for k in (1, 2)] + [squeeze(r.bias_sums[k]) for k in (1, 2)]
        lines += [squeeze(r.out_sums[k]) for k in range(3)] + [squeeze(r.up_sum[0] + r.up_sum[1])]
        place = early[0].place
        r.early_slots[place, 0:8] = jnp.concatenate(lines, axis=0)
        r.early_slots[place, 8:16] = jnp.zeros((8, width), f32)
        for k in range(4):
            r.early_slots[place, 8:9, k * own : (k + 1) * own] = r.in_bias_sums[k : k + 1, 0:own]
        early[0].start()

    def early_results():
        total = finish_all(early)
        r.norm_gains_grad[1:3] = total[0:2]
        r.norm_biases_grad[1:3] = total[2:4]
        r.out_biases_grad[...] = total[4:7]
        r.up_bias_grad[...] = total[7:8]
        for k in range(4):
            r.in_biases_grad[k : k + 1] = total[8:9, k * own : (k + 1) * own]

    plane = Direct(at, r.plane_slots, r.d_0, r.d_1)

    def result_2():
        total = scatter_2.finish()
        for j in range(4):
            for t in range(2):
                cols = slice(t * width + j * own, t * width + (j + 1) * own)
                r.plane_out[j, t] = total[:, cols].astype(bf16)

        for k in (1, 2, 3):
            to = lax.rem(at.m + k, 4)
            remote(r.plane_out.at[to], r.plane_slots.at[at.m], r.d_0.at[k], r.d_1.at[at.m], at.line(to)).start()

    def result_2_end():
        total = r.plane_out[at.m].astype(f32)
        for k in (1, 2, 3):
            o = lax.rem(at.m + k, 4)
            remote(r.plane_out.at[o], r.plane_slots.at[o], r.d_0.at[k], r.d_1.at[o], at.line(o)).wait_recv()
            total = total + r.plane_slots[o].astype(f32)
        r.cross_in_grad[1:3] = total
        for k in (1, 2, 3):
            to = lax.rem(at.m + k, 4)
            remote(r.plane_out.at[to], r.plane_slots.at[at.m], r.d_0.at[k], r.d_1.at[at.m], at.line(to)).wait_send()

    def layer_result():
        def write(block):
            total = r.x3[block] + r.down[block].astype(f32) + r.out_biases[2:3]
            r.layer_out[block] = total.astype(bf16)

        for c in range(down_half, down_sum.count):
            down_sum.take(c)
        row_blocks(rows, 64, write)

    def result_3():
        total = scatter_3.finish()
        for i in range(3):
            r.self_in_grad[i] = total[:, i * own : (i + 1) * own]
        r.cross_in_grad[0] = total[:, 3 * own : 4 * own]
        r.self_out_grad[...] = total[:, 4 * own : 5 * own].T
        r.cross_out_grad[...] = total[:, 5 * own : 6 * own].T

    jobs = [query_weight]
    jobs += weight_grad(r.grads_3, 0, r.n1, r.dq1) + weight_grad(r.grads_3, own, r.n1, r.dk1)
    jobs += weight_grad(r.grads_3, 2 * own, r.n1, r.dv1) + weight_grad(r.grads_3, 4 * own, r.low, r.o1)
    jobs += [scatter_3.start, early_vectors, result_2, scatter_3.fold, layer_result, early_results, result_2_end]
    interleave(sum_steps(dn1_sum, back_first), jobs)
    dn1_sum.finish()
    place = late[0].place
    r.late_slots[place] = jnp.zeros_like(r.late_slots[place])
    r.late_slots[place, 0:1] = squeeze(r.gain_sums[0])
    r.late_slots[place, 1:2] = squeeze(r.bias_sums[0])
    late[0].start()
    result_3()
    total = finish_all(late)
    r.norm_gains_grad[0:1] = total[0:1]
    r.norm_biases_grad[0:1] = total[1:2]


def layer(n, inputs):
    tokens, self_in = inputs["tokens"], inputs["self_in"]
    rows, width = tokens.shape
    own = self_in.shape[1]
    hidden = inputs["fc_up_in"].shape[1]
    groups = width // GROUP
    per = width // n
    S = jax.ShapeDtypeStruct
    outs = dict(
        layer_out=S((rows, width), bf16), token_grad=S((rows, width), bf16),
        encoder_grad=S(inputs["encoder"].shape, bf16), norm_gains_grad=S((3, width), f32),
        norm_biases_grad=S((3, width), f32), self_in_grad=S((3, per, own), f32), cross_in_grad=S((3, per, own), f32),
        in_biases_grad=S((4, own), f32), self_out_grad=S((own, per), f32), cross_out_grad=S((own, per), f32),
        out_biases_grad=S((3, width), f32), fc_up_grad=S((per, hidden), f32), up_bias_grad=S((1, hidden), f32),
        fc_down_grad=S((per, hidden), f32),
    )
    dma = pltpu.SemaphoreType.DMA
    low, full = pltpu.VMEM((rows, width), bf16), pltpu.VMEM((rows, width), f32)
    thin = pltpu.VMEM((rows, own), bf16)
    wide = pltpu.VMEM((rows, 2 * width), bf16)
    frame_pair = pltpu.VMEM((FRAMES, 2 * width), bf16)
    scratch = dict(
        fc_up=pltpu.VMEM((width, hidden), bf16), fc_down=pltpu.VMEM((hidden, width), bf16), cotangent=low,
        load=dma((8,)), big=pltpu.VMEM((6, width, width), bf16), bias=pltpu.VMEM((8, width), f32),
        bias_slots=pltpu.VMEM((4, 8, 256), f32), parts=pltpu.VMEM((4, rows // 2, 2 * own), bf16),
        frames=pltpu.VMEM((2, FRAMES, width), bf16), n1=low, n2=low, o2=low,
        dq2=low, dn3=low, down=low, part_a=low, part_b=low, ends=low, ends_b=pltpu.VMEM((rows // 2, width), bf16), other_a=low, other_b=low,
        other_c=pltpu.VMEM((rows // 2, width), bf16), x2=full, x3=full, g3=full, dn2=full, q1=thin, k1=thin, v1=thin, o1=thin, do1=thin, dq1=thin,
        dk1=thin, dv1=thin, own_part=thin, lse1=pltpu.VMEM((rows, 8), f32), q_pair=wide, do_pair=wide,
        k_pair=frame_pair, v_pair=frame_pair, stats=pltpu.VMEM((groups, rows, PAIR), f32),
        stat_slots=pltpu.VMEM((groups, 4, 8, rows), f32), dk_t=pltpu.VMEM((2, width, FRAMES), bf16),
        dv_t=pltpu.VMEM((2, width, FRAMES), bf16), dk_sum=pltpu.VMEM((own, rows), f32),
        dv_sum=pltpu.VMEM((own, rows), f32), gain_sums=pltpu.VMEM((3, 8, width), f32),
        bias_sums=pltpu.VMEM((3, 8, width), f32), out_sums=pltpu.VMEM((3, 8, width), f32),
        up_sum=pltpu.VMEM((2, 8, hidden), f32), do2_sum=pltpu.VMEM((8, width), f32),
        in_bias_sums=pltpu.VMEM((8, 256), f32), early_slots=pltpu.VMEM((PLANE, 16, width), f32),
        late_slots=pltpu.VMEM((PLANE, 8, width), f32), plane_out=pltpu.VMEM((4, 2, per, own), bf16),
        plane_slots=pltpu.VMEM((4, 2, per, own), bf16), grads_1=pltpu.VMEM((n, per, 2 * width), bf16),
        grads_3=pltpu.VMEM((n, per, 6 * own), bf16),
    )
    group_dma = [dma((groups, 4)), dma((groups, 4))]
    for letter, group in (
        ("g", Gather.semaphores()), ("b", Direct.semaphores()), ("p", Parts.semaphores()), ("s", group_dma),
        ("t", Total.semaphores(2 * width // PAIR)), ("u", Total.semaphores(rows // 32)),
        ("v", Total.semaphores(rows // 32)), ("q", Total.semaphores(2 * width // PAIR)),
        ("z", Total.semaphores(rows // 32)), ("e", Everyone.semaphores(PLANE)), ("l", Everyone.semaphores(PLANE)),
        ("d", Direct.semaphores()),
    ):
        for i, one in enumerate(group):
            scratch[f"{letter}_{i}"] = one
    if n > PLANE:
        scratch["early_slots_2"] = pltpu.VMEM((n // PLANE, 16, width), f32)
        scratch["late_slots_2"] = pltpu.VMEM((n // PLANE, 8, width), f32)
        for letter in ("m", "n"):
            for i, one in enumerate(Everyone.semaphores(n // PLANE)):
                scratch[f"{letter}_{i}"] = one
    for k, letter, cols in ((1, "x", 2 * width), (2, "y", 2 * width), (3, "w", 6 * own)):
        came, slots, *semaphores = Scatter.buffers(n, per, cols)
        scratch[f"came_{k}"], scratch[f"slots_{k}"] = came, slots
        for i, one in enumerate(semaphores):
            scratch[f"{letter}_{i}"] = one
    names = list(inputs) + list(outs) + list(scratch)
    late = ("fc_up_in", "fc_down_in", "cotangent_in", "cross_in", "cross_out")
    result = pl.pallas_call(
        functools.partial(layer_kernel, names, n),
        out_shape=list(outs.values()),
        in_specs=[SMEM if name == "lengths" else ANY if name in late else VMEM for name in inputs],
        out_specs=[VMEM] * len(outs),
        scratch_shapes=list(scratch.values()),
        compiler_params=pltpu.CompilerParams(
            collective_id=1, has_side_effects=True, vmem_limit_bytes=63 * 2**20
        ),
        name="layer",
    )(*inputs.values())
    return dict(zip(outs, result))


def shards(
    n, tokens, encoder, lengths, norm_gains, norm_biases, self_in, cross_in, in_biases, self_out, cross_out,
    out_biases, fc_up, up_bias, fc_down, cotangent,
):
    outs = layer(
        n,
        dict(
            tokens=tokens, encoder=encoder, lengths=lengths, norm_gains=norm_gains, norm_biases=norm_biases,
            self_in=self_in.transpose(0, 2, 1),
            cross_in=cross_in.transpose(0, 2, 1), in_biases=in_biases, self_out=self_out, cross_out=cross_out,
            out_biases=out_biases, up_bias=up_bias.reshape(1, -1), fc_up_in=fc_up, fc_down_in=fc_down,
            cotangent_in=cotangent,
        ),
    )
    outs["fc_down_grad"] = outs["fc_down_grad"].T
    outs["up_bias_grad"] = outs["up_bias_grad"].reshape(-1)
    return tuple(outs.values())


def solution(mesh):
    in_specs = (
        P("dp", None), P("dp", "mp", None), P("dp", None), P(), P(), P(None, None, "mp"), P(None, None, "mp"),
        P(None, "mp"), P("mp", None), P("mp", None), P(), P(None, "mp"), P("mp"), P("mp", None), P("dp", None),
    )
    out_specs = (
        P("dp", None), P("dp", None), P("dp", "mp", None), P(), P(), P(None, "dp", "mp"), P(None, "dp", "mp"),
        P(None, "mp"), P("mp", "dp"), P("mp", "dp"), P(), P("dp", "mp"), P("mp"), P("mp", "dp"),
    )
    body = functools.partial(shards, mesh.shape["dp"])
    return jax.shard_map(body, mesh=mesh, in_specs=in_specs, out_specs=out_specs, check_vma=False)
```

```python
import functools
import types

import jax
import jax.numpy as jnp
from jax import lax
from jax.experimental import pallas as pl
from jax.experimental.pallas import tpu as pltpu
from jax.sharding import PartitionSpec as P

HEAD = 64
PAIR = 2 * HEAD
PLANE = 8
SLICE = 128
UNIT = 64
FRAMES = 384
epsilon = 1e-05
factor = 0.125
masked_value = -1e30
f32 = jnp.float32
bf16 = jnp.bfloat16
MESH = pl.DeviceIdType.MESH
VMEM = pl.BlockSpec(memory_space=pltpu.VMEM)
SMEM = pl.BlockSpec(memory_space=pltpu.SMEM)
ANY = pl.BlockSpec(memory_space=pl.ANY)


def nn(a, b):
    return jnp.dot(a, b, preferred_element_type=f32)


def nt(a, b):
    return lax.dot_general(a, b, (((1,), (1,)), ((), ())), preferred_element_type=f32)


def tn(a, b):
    return lax.dot_general(a, b, (((0,), (0,)), ((), ())), preferred_element_type=f32)


def flip(index, bit):
    return index + bit - 2 * bit * lax.rem(index // bit, 2)


def remote(src, dst, send, recv, device):
    return pltpu.make_async_remote_copy(
        src_ref=src, dst_ref=dst, send_sem=send, recv_sem=recv, device_id=device, device_id_type=MESH
    )


def greet(devices):
    barrier = pltpu.get_barrier_semaphore()
    for device in devices:
        pl.semaphore_signal(barrier, inc=1, device_id=device, device_id_type=MESH)


def await_greetings(count):
    pl.semaphore_wait(pltpu.get_barrier_semaphore(), count)


def pair_sum(left, right):
    return (left.astype(f32) + right.astype(f32)).astype(bf16)


class Place:
    def __init__(self):
        self.d, self.m = d, m = lax.axis_index("dp"), lax.axis_index("mp")
        self.mine = lax.rem(d, PLANE)
        self.base = d - self.mine
        self.half = m // 2
        self.rank = m + self.half * (3 - 2 * m)
        self.edge, self.inner = self.rank == 0, self.rank == 1
        self.near = flip(m, 1)
        self.peer = 3 - m

    def origin(self, j):
        index = 1 - self.rank if j == 0 else j + 1
        return index + self.half * (3 - 2 * index)

    def line(self, m):
        return (self.d, m)

    def plane(self, s):
        return (self.base + s, self.m)

    def way(self, k):
        s = self.mine
        for bit in (1, 2, 4):
            if k & bit:
                s = flip(s, bit)
        return s


class Gather:
    def __init__(self, at, packed, line_send, side_send, corner_send, core_send, recv, core_recv):
        self.at, self.packed = at, packed
        self.line_send, self.side_send, self.corner_send = line_send, side_send, corner_send
        self.core_send, self.recv, self.core_recv = core_send, recv, core_recv
        self.core, self.chip = lax.rem(at.mine, 2), at.mine // 2

    def copy(self, o, chip, i, send, device):
        start = (self.core * 4 + chip) * SLICE + i * UNIT
        block = self.packed.at[o, pl.ds(pl.multiple_of(start, UNIT), UNIT)]
        return remote(block, block, send, self.recv.at[o, chip, i], device)

    def came(self, o, chip, i):
        self.copy(o, chip, i, self.line_send, self.at.line(self.at.m)).wait_recv()

    def start(self):
        at = self.at
        for i in (0, 1):
            self.copy(at.m, self.chip, i, self.line_send, at.line(at.near)).start()

            @pl.when(at.inner)
            def _(i=i):
                self.copy(at.m, self.chip, i, self.line_send, at.line(at.peer)).start()

    def from_line(self, j):
        at = self.at
        o = at.origin(j)
        for i in (0, 1):
            self.came(o, self.chip, i)

            @pl.when(at.inner)
            def _(i=i):
                to = at.peer if j == 0 else at.near
                self.copy(o, self.chip, i, self.line_send, at.line(to)).start()

            for k in (2, 4):
                self.copy(o, self.chip, i, self.side_send, at.plane(at.way(k))).start()

    def from_sides(self, j):
        at = self.at
        o = at.origin(j)
        for k, i in ((2, 0), (4, 1)):
            chip = flip(self.chip, k // 2)
            self.came(o, chip, i)
            self.copy(o, chip, i, self.corner_send, at.plane(at.way(6 - k))).start()

    def core_copy(self, j, mine):
        core = self.core if mine else 1 - self.core
        block = self.packed.at[self.at.origin(j), pl.ds(pl.multiple_of(core * 4 * SLICE, SLICE), 4 * SLICE)]
        return remote(block, block, self.core_send.at[j], self.core_recv.at[j], self.at.plane(self.at.way(1)))

    def from_corner(self, j):
        o = self.at.origin(j)
        for k, i in ((2, 1), (4, 0)):
            self.came(o, flip(self.chip, k // 2), i)
        for i in (0, 1):
            self.came(o, flip(flip(self.chip, 1), 2), i)
        self.core_copy(j, True).start()

    def from_core(self, j):
        self.core_copy(j, False).wait_recv()

    def sent(self, rows, send):
        block = self.packed.at[0, pl.ds(0, rows)]
        remote(block, block, send, self.core_recv.at[0], self.at.line(self.at.near)).wait_send()

    def finish(self):
        at = self.at

        @pl.when(at.edge)
        def _():
            self.sent(SLICE, self.line_send)

        @pl.when(at.inner)
        def _():
            self.sent(5 * SLICE, self.line_send)

        self.sent(6 * SLICE, self.side_send)
        self.sent(3 * SLICE, self.corner_send)
        for j in range(3):
            self.core_copy(j, True).wait_send()

    @staticmethod
    def semaphores():
        dma = pltpu.SemaphoreType.DMA
        return [dma, dma, dma, dma((3,)), dma((4, 4, 2)), dma((3,))]


class Parts:
    def __init__(self, at, slots, send, recv):
        self.at, self.slots, self.send, self.recv = at, slots, send, recv

    def copy(self, o, send, to):
        return remote(self.slots.at[o], self.slots.at[o], send, self.recv.at[o], self.at.line(to))

    def own(self, to_peer):
        at = self.at
        return self.copy(at.m, self.send.at[to_peer], at.peer if to_peer else at.near)

    def forward(self, j):
        at = self.at
        return self.copy(at.origin(j), self.send.at[2 + j], at.peer if j == 0 else at.near)

    def start(self):
        self.own(0).start()

        @pl.when(self.at.inner)
        def _():
            self.own(1).start()

    def step(self, j):
        self.copy(self.at.origin(j), self.send.at[0], self.at.m).wait_recv()

        @pl.when(self.at.inner)
        def _():
            self.forward(j).start()

    def finish(self):
        self.own(0).wait_send()

        @pl.when(self.at.inner)
        def _():
            self.own(1).wait_send()
            for j in range(3):
                self.forward(j).wait_send()

    @staticmethod
    def semaphores():
        dma = pltpu.SemaphoreType.DMA
        return [dma((5,)), dma((4,))]


class Direct:
    def __init__(self, at, slots, send, recv):
        self.at, self.slots, self.send, self.recv = at, slots, send, recv

    def copy(self, o, k):
        to = lax.rem(self.at.m + k, 4)
        return remote(self.slots.at[o], self.slots.at[o], self.send.at[k], self.recv.at[o], self.at.line(to))

    def start(self):
        for k in (1, 2, 3):
            self.copy(self.at.m, k).start()

    def finish(self):
        for k in (1, 2, 3):
            self.copy(lax.rem(self.at.m + k, 4), k).wait_recv()
        for k in (1, 2, 3):
            self.copy(self.at.m, k).wait_send()

    @staticmethod
    def semaphores():
        dma = pltpu.SemaphoreType.DMA
        return [dma((4,)), dma((4,))]


class Everyone:
    def __init__(self, at, size, stride, slots, send, recv):
        self.at, self.size, self.stride, self.slots, self.send, self.recv = at, size, stride, slots, send, recv
        self.place = lax.rem(at.d // stride, size)

    def copy(self, o, k):
        to = self.at.d + (lax.rem(self.place + k, self.size) - self.place) * self.stride
        return remote(
            self.slots.at[o], self.slots.at[o], self.send.at[k], self.recv.at[o], (to, self.at.m)
        )

    def start(self):
        for k in range(1, self.size):
            self.copy(self.place, k).start()

    def finish(self):
        for k in range(1, self.size):
            self.copy(lax.rem(self.place + k, self.size), k).wait_recv()
        for k in range(1, self.size):
            self.copy(self.place, k).wait_send()
        total = self.slots[0]
        for o in range(1, self.size):
            total = total + self.slots[o]
        return total

    @staticmethod
    def semaphores(size):
        dma = pltpu.SemaphoreType.DMA
        return [dma((size,)), dma((size,))]


class Scatter:
    def __init__(self, at, n, x, came, slots, s1, r1, s2, r2):
        self.at, self.x, self.came, self.slots = at, x, came, slots
        self.s1, self.r1, self.s2, self.r2 = s1, r1, s2, r2
        self.core, self.chip, self.chips = lax.rem(at.d, 2), at.d // 2, n // 2
        self.order = list(range(1, self.chips)) + [0]

    def to_sibling(self, k):
        c = lax.rem(self.chip + k, self.chips)
        other = 1 - self.core
        return remote(
            self.x.at[2 * c + other], self.came.at[c], self.s1.at[c], self.r1.at[c],
            (2 * self.chip + other, self.at.m),
        )

    def between(self, k, slot):
        c = lax.rem(self.chip + k, self.chips)
        return remote(
            self.x.at[2 * c + self.core], self.slots.at[slot], self.s2.at[c], self.r2.at[slot],
            (2 * c + self.core, self.at.m),
        )

    def start(self):
        for k in self.order:
            self.to_sibling(k).start()

    def fold(self):
        for k in self.order:
            c = lax.rem(self.chip + k, self.chips)
            self.to_sibling(k).wait_recv()
            block = 2 * c + self.core
            self.x[block] = pair_sum(self.x[block], self.came[c])
            if k:
                self.between(k, self.chip).start()

    def finish(self):
        total = self.x[2 * self.chip + self.core].astype(f32)
        for k in range(1, self.chips):
            c = lax.rem(self.chip + k, self.chips)
            self.between(k, c).wait_recv()
            total = total + self.slots[c].astype(f32)
        for k in self.order:
            self.to_sibling(k).wait_send()
        for k in range(1, self.chips):
            self.between(k, self.chip).wait_send()
        return total

    @staticmethod
    def buffers(n, rows, cols):
        half = pltpu.VMEM((n // 2, rows, cols), bf16)
        dma = pltpu.SemaphoreType.DMA((n // 2,))
        return [half, half, dma, dma, dma, dma]


class Total:
    def __init__(self, at, whole, blocks, x, ends, other, out, sa, ra, sb, rb, sr, rr, rooms=None):
        self.at, self.whole, self.blocks, self.rooms = at, whole, blocks, rooms or blocks
        self.x, self.ends, self.other, self.out = x, ends, other, out
        self.sa, self.ra, self.sb, self.rb, self.sr, self.rr = sa, ra, sb, rb, sr, rr
        self.count = len(blocks)
        self.size = whole.size * x.shape[1] * 2 / self.count

    def inward(self, c):
        room = self.ends.at[self.rooms[c]]
        return remote(self.x.at[self.blocks[c]], room, self.sa, self.ra.at[c], self.at.line(self.at.near))

    def across(self, c):
        room = self.other.at[self.rooms[c]]
        return remote(self.x.at[self.blocks[c]], room, self.sb, self.rb.at[c], self.at.line(self.at.peer))

    def outward(self, c):
        block = self.out.at[self.blocks[c]]
        return remote(block, block, self.sr, self.rr.at[c], self.at.line(self.at.near))

    def send(self, c):
        @pl.when(self.at.edge)
        def _():
            self.inward(c).start()

    def fold(self, c):
        @pl.when(self.at.inner)
        def _():
            b = self.blocks[c]
            self.inward(c).wait_recv()
            self.x[b] = pair_sum(self.x[b], self.ends[self.rooms[c]])
            self.across(c).start()

    def close(self, c):
        @pl.when(self.at.inner)
        def _():
            b = self.blocks[c]
            self.across(c).wait_recv()
            self.out[b] = pair_sum(self.x[b], self.other[self.rooms[c]])
            self.outward(c).start()

    def take(self, c):
        @pl.when(self.at.edge)
        def _():
            self.outward(c).wait_recv()

    def sent(self, source, send):
        block = source.at[self.whole]
        remote(block, block, send, self.ra.at[0], self.at.line(self.at.near)).wait_send()

    def finish(self):
        @pl.when(self.at.edge)
        def _():
            self.sent(self.x, self.sa)

        @pl.when(self.at.inner)
        def _():
            self.sent(self.x, self.sb)
            self.sent(self.out, self.sr)

    @staticmethod
    def semaphores(count):
        dma = pltpu.SemaphoreType.DMA
        return [dma((2,)), dma((2, count))] * 3


class SoftTotal:
    def __init__(self, at, r, h, block, blocks, sums, letter, groups):
        self.at, self.r, self.h, self.block, self.sums = at, r, h, block, sums
        self.semaphores = [getattr(r, f"{letter}_{i}").at[h] for i in range(6)]
        self.blocks, self.groups = blocks, groups
        self.count = len(blocks)
        self.each = self.count // groups
        self.size = sums.size

    def small(self, kind, source, target, g, to):
        send, recv = self.semaphores[2 * kind], self.semaphores[2 * kind + 1]
        return remote(source.at[self.h, g], target.at[self.h, g], send, recv.at[g], self.at.line(to))

    def small_sent(self, kind, source):
        whole = source.at[self.h]
        send, recv = self.semaphores[2 * kind], self.semaphores[2 * kind + 1]
        remote(whole, whole, send, recv.at[0], self.at.line(self.at.near)).wait_send()

    def inward(self, g):
        return self.small(0, self.r.lse_own, self.r.lse_end, g, self.at.near)

    def across(self, g):
        return self.small(1, self.r.lse_mid, self.r.lse_far, g, self.at.peer)

    def outward(self, g):
        return self.small(2, self.r.lse_all, self.r.lse_all, g, self.at.near)

    def spread(self, tables, rows, tile):
        low = iota((rows.size, PAIR), 1) < HEAD
        return jnp.where(low, tables[:, 2 * tile : 2 * tile + 1], tables[:, 2 * tile + 1 : 2 * tile + 2])

    def columns(self, *tables):
        spare = jnp.zeros((PAIR - 8 * len(tables), self.block.size), f32)
        return jnp.concatenate([*tables, spare], axis=0).T

    def merge(self, left, right):
        top = jnp.maximum(left, right)
        total = top + jnp.log(jnp.exp(left - top) + jnp.exp(right - top))
        return total, jnp.exp(left - total), jnp.exp(right - total)

    def send(self, c):
        g = c // self.each

        @pl.when(self.at.edge)
        def _():
            if c % self.each == 0:
                self.inward(g).start()
            rows, cols = self.blocks[c]
            self.r.part_a[rows, cols] = self.r.g3[rows, cols].astype(bf16)

        self.sums.send(c)

    def fold(self, c):
        r, sums, g = self.r, self.sums, c // self.each

        @pl.when(self.at.inner)
        def _():
            if c % self.each == 0:
                self.inward(g).wait_recv()
                total, own, end = self.merge(r.lse_own[self.h, g], r.lse_end[self.h, g])
                r.lse_mid[self.h, g] = total
                self.across(g).start()
                r.stats[g, self.block] = self.columns(own, end)
            sums.inward(c).wait_recv()
            rows, cols = self.blocks[c]
            table = r.stats[g, rows]
            for t in range(2):
                tile = pl.ds(cols.start + t * PAIR, PAIR)
                value = r.g3[rows, tile] * self.spread(table, rows, t)
                value = value + r.ends[rows, tile].astype(f32) * self.spread(table[:, 8:], rows, t)
                r.part_a[rows, tile] = value.astype(bf16)
            sums.across(c).start()

    def close(self, c):
        r, sums, g, at = self.r, self.sums, c // self.each, self.at

        @pl.when(at.inner)
        def _():
            lower = at.half == 0
            if c % self.each == 0:
                self.across(g).wait_recv()
                mid, far = r.lse_mid[self.h, g], r.lse_far[self.h, g]
                total, left, right = self.merge(jnp.where(lower, mid, far), jnp.where(lower, far, mid))
                r.lse_all[self.h, g] = total
                self.outward(g).start()
                r.stats[g, self.block] = self.columns(total, left, right)
            sums.across(c).wait_recv()
            rows, cols = self.blocks[c]
            table = r.stats[g, rows]
            for t in range(2):
                tile = pl.ds(cols.start + t * PAIR, PAIR)
                mid, far = r.part_a[rows, tile].astype(f32), r.other_a[rows, tile].astype(f32)
                left, right = jnp.where(lower, mid, far), jnp.where(lower, far, mid)
                value = left * self.spread(table[:, 8:], rows, t) + right * self.spread(table[:, 16:], rows, t)
                r.o2[rows, tile] = value.astype(bf16)
            sums.outward(c).start()

    def take(self, c):
        g = c // self.each
        self.sums.take(c)
        if c % self.each == 0:

            @pl.when(self.at.edge)
            def _():
                self.outward(g).wait_recv()
                self.r.stats[g, self.block] = self.columns(self.r.lse_all[self.h, g])

    def finish(self):
        self.sums.finish()

        @pl.when(self.at.edge)
        def _():
            self.small_sent(0, self.r.lse_own)

        @pl.when(self.at.inner)
        def _():
            self.small_sent(1, self.r.lse_mid)
            self.small_sent(2, self.r.lse_all)


def normal(values):
    average = jnp.mean(values, axis=-1, keepdims=True)
    centred = values - average
    variance = jnp.mean(centred * centred, axis=-1, keepdims=True)
    scale = lax.rsqrt(variance + epsilon)
    return centred * scale, scale


def row_blocks(count, size, body):
    def step(i, carry):
        body(pl.ds(pl.multiple_of(i * size, size), size))
        return carry

    lax.fori_loop(0, count // size, step, 0)


def iota(shape, axis):
    return lax.broadcasted_iota(jnp.int32, shape, axis)


def pair_tiles(tile):
    turned = pltpu.roll(tile, HEAD, axis=1)
    low = iota(tile.shape, 1) < HEAD
    return jnp.where(low, tile, turned), jnp.where(low, turned, tile)


def back_normal(values, upstream, gain):
    xhat, scale = normal(values)
    scaled = upstream * gain
    first = jnp.mean(scaled, axis=-1, keepdims=True)
    second = jnp.mean(scaled * xhat, axis=-1, keepdims=True)
    return scale * (scaled - first - xhat * second), upstream * xhat


def by_eights(values):
    return jnp.sum(values.reshape(-1, 8, values.shape[1]), axis=0)


def own_columns(at, source, target):
    width = target.shape[1]
    for j in range(4):

        @pl.when(at.m == j)
        def _(j=j):
            target[...] = source[:, j * width : (j + 1) * width]


def self_mask(rows, keys, start, clip_start):
    row = iota((rows, keys), 0) + start
    col = iota((rows, keys), 1)
    return jnp.logical_and(col <= row, (row >= clip_start) == (col >= clip_start))


def self_projections(r):
    rows = r.tokens.shape[0]

    def normed(block):
        xhat, _ = normal(r.tokens[block].astype(f32))
        r.n1[block] = (xhat * r.norm_gains[0:1] + r.norm_biases[0:1]).astype(bf16)

    row_blocks(rows, 64, normed)
    r.q1[...] = (nt(r.n1[...], r.self_in[0]) + r.in_biases[0:1]).astype(bf16)
    r.k1[...] = nt(r.n1[...], r.self_in[1]).astype(bf16)
    r.v1[...] = (nt(r.n1[...], r.self_in[2]) + r.in_biases[1:2]).astype(bf16)


def self_forward(r, part, clip_start):
    half = r.tokens.shape[0] // 2
    block, keys = pl.ds(part * half, half), (part + 1) * half
    allowed = self_mask(half, keys, part * half, clip_start)
    for h in range(r.q1.shape[1] // HEAD):
        cols = pl.ds(h * HEAD, HEAD)
        scores = nt(r.q1[block, cols] * bf16(factor), r.k1[0:keys, cols])
        scores = jnp.where(allowed, scores, masked_value)
        top = jnp.max(scores, axis=1, keepdims=True)
        power = jnp.exp(scores - top)
        total = jnp.sum(power, axis=1, keepdims=True)
        chance = (power * (1 / total)).astype(bf16)
        r.o1[block, cols] = nn(chance, r.v1[0:keys, cols]).astype(bf16)
        r.lse1[block, pl.ds(h, 1)] = top + jnp.log(total)


def self_backward(r, part, clip_start):
    half = r.tokens.shape[0] // 2
    block, keys = pl.ds(part * half, half), (part + 1) * half
    allowed = self_mask(half, keys, part * half, clip_start)
    for h in range(r.q1.shape[1] // HEAD):
        cols = pl.ds(h * HEAD, HEAD)
        query, upstream = r.q1[block, cols] * bf16(factor), r.do1[block, cols]
        scores = jnp.where(allowed, nt(query, r.k1[0:keys, cols]), masked_value)
        chance = jnp.exp(scores - r.lse1[block, pl.ds(h, 1)])
        slope = nt(upstream, r.v1[0:keys, cols])
        inner = jnp.sum(chance * slope, axis=1, keepdims=True)
        change = (chance * (slope - inner)).astype(bf16)
        query_grad = nn(change, r.k1[0:keys, cols]) * factor
        r.dq1[block, cols] = query_grad.astype(bf16)
        bias = jnp.sum(query_grad, axis=0, keepdims=True)
        key_grad, value_grad = tn(query, change), tn(upstream, chance.astype(bf16))
        if part:
            r.in_bias_sums[0:1, cols] = bias
            r.dk_sum[cols, :] = key_grad
            r.dv_sum[cols, :] = value_grad
        else:
            r.in_bias_sums[0:1, cols] += bias
            r.dk_sum[cols, 0:keys] += key_grad
            r.dv_sum[cols, 0:keys] += value_grad
    r.dk1[block] = r.dk_sum[:, block].T.astype(bf16)
    r.dv1[block] = r.dv_sum[:, block].T.astype(bf16)


def keys_and_values(r, matrix, bias, pairs):
    both = [nt(r.frames[clip], r.big[matrix]) for clip in range(2)]
    if bias is not None:
        both = [value + r.bias[bias : bias + 1] for value in both]
    for t in range(both[0].shape[1] // PAIR):
        first, second = (value[:, t * PAIR : (t + 1) * PAIR] for value in both)
        low = iota(first.shape, 1) < HEAD
        turned_first, turned_second = pltpu.roll(first, HEAD, axis=1), pltpu.roll(second, HEAD, axis=1)
        pairs[:, 2 * t * PAIR : (2 * t + 1) * PAIR] = jnp.where(low, first, turned_second).astype(bf16)
        pairs[:, (2 * t + 1) * PAIR : (2 * t + 2) * PAIR] = jnp.where(low, turned_first, second).astype(bf16)


def to_pairs(value, pairs, block, clip_start, scale):
    rows = value.shape[0]
    keep = (iota((rows, PAIR), 1) < HEAD) == (iota((rows, PAIR), 0) + block.start < clip_start)
    for t in range(value.shape[1] // PAIR):
        for e, tile in enumerate(pair_tiles(value[:, t * PAIR : (t + 1) * PAIR])):
            at = (2 * t + e) * PAIR
            pairs[block, at : at + PAIR] = (jnp.where(keep, tile, 0.0) * scale).astype(bf16)


def from_pair(even, odd, first):
    low = iota(even.shape, 1) < HEAD
    even = jnp.where(first, even, pltpu.roll(even, HEAD, axis=1))
    odd = jnp.where(first, pltpu.roll(odd, HEAD, axis=1), odd)
    return jnp.where(low, even, odd)


GROUP = 2 * PAIR
GROUP_HEADS = 4


def of_clip(block, clip_start):
    return iota((block.size, PAIR), 0) + block.start < clip_start


def real_frames(rows, frame_count):
    return iota((rows, FRAMES), 1) < frame_count


def cross_forward(r, block, g, j, clip_start, frame_count):
    lane = iota((block.size, PAIR), 1)
    first = of_clip(block, clip_start)
    valid = real_frames(block.size, frame_count)
    halves = []
    stats = jnp.zeros((block.size, PAIR), f32) if j == 0 else r.stats[g, block]
    for e in (0, 1):
        cols = pl.ds(2 * GROUP * g + 2 * PAIR * j + PAIR * e, PAIR)
        scores = jnp.where(valid, nt(r.q_pair[block, cols], r.k_pair[:, cols]), masked_value)
        top = jnp.max(scores, axis=1, keepdims=True)
        power = jnp.exp(scores - top)
        total = jnp.sum(power, axis=1, keepdims=True)
        halves.append(nn(power.astype(bf16), r.v_pair[:, cols]) * (1 / total))
        stats = jnp.where(lane == 2 * j + e, top + jnp.log(total), stats)
    r.stats[g, block] = stats
    r.g3[block, pl.ds(GROUP * g + PAIR * j, PAIR)] = from_pair(*halves, first)


def cross_slopes(r, block, cols, lane, stats, index, valid):
    def column(i):
        return jnp.sum(jnp.where(lane == i, stats, 0.0), axis=1, keepdims=True)

    scores = jnp.where(valid, nt(r.q_pair[block, cols], r.k_pair[:, cols]), masked_value)
    chance = jnp.exp(scores - column(index))
    slope = nt(r.do_pair[block, cols], r.v_pair[:, cols])
    return chance, (chance * (slope - column(16 + index))).astype(bf16)


def cross_queries(r, block, g, j, clip_start, frame_count):
    lane = iota((block.size, PAIR), 1)
    first = of_clip(block, clip_start)
    valid = real_frames(block.size, frame_count)
    stats = r.stats[g, block]
    halves = []
    for e in (0, 1):
        cols = pl.ds(2 * GROUP * g + 2 * PAIR * j + PAIR * e, PAIR)
        _, change = cross_slopes(r, block, cols, lane, stats, 2 * j + e, valid)
        halves.append(nn(change, r.k_pair[:, cols]) * factor)
    r.part_a[block, pl.ds(GROUP * g + PAIR * j, PAIR)] = from_pair(*halves, first).astype(bf16)


def cross_frames(r, g, j, frame_count):
    rows = r.q_pair.shape[0]
    block = pl.ds(0, rows)
    lane = iota((rows, PAIR), 1)
    valid = real_frames(rows, frame_count)
    for e in (0, 1):
        cols = pl.ds(2 * GROUP * g + 2 * PAIR * j + PAIR * e, PAIR)
        chance, change = cross_slopes(r, block, cols, lane, r.stats[g], 2 * j + e, valid)
        value_grad = tn(r.do_pair[:, cols], chance.astype(bf16)).astype(bf16)
        key_grad = tn(r.q_pair[:, cols], change).astype(bf16)
        head = pl.ds(GROUP * g + PAIR * j + HEAD * e, HEAD)
        for clip in range(2):
            r.dv_t[clip, head] = value_grad[clip * HEAD : (clip + 1) * HEAD]
            r.dk_t[clip, head] = key_grad[clip * HEAD : (clip + 1) * HEAD]


def put_blocks(x, column, first_row, value):
    per = x.shape[1]
    for i in range(value.shape[0] // per):
        x[first_row // per + i, :, column : column + value.shape[1]] = value[i * per : (i + 1) * per].astype(bf16)


def weight_grad(x, column, left, right):
    part = left.shape[1] // 2
    return [
        functools.partial(
            lambda i: put_blocks(x, column, i * part, tn(left[:, i * part : (i + 1) * part], right[...])), i
        )
        for i in range(2)
    ]


class Pump:
    latency, rate, step, issue = 1.8, 47.0e3, 0.27, 0.1

    def __init__(self):
        self.blocks, self.folded, self.closed = [], 0, 0
        self.edge, self.inner = 0.0, 0.0
        self.free = dict(inward=0.0, across=0.0, outward=0.0)

    def travel(self, link, block, start):
        self.free[link] = max(self.free[link], start) + block["bytes"] / self.rate
        return self.free[link] + self.latency

    def add(self, total, chosen, after=None, after_time=0.0):
        for c in chosen:
            total.send(c)
            self.edge += self.issue
            block = dict(total=total, c=c, after=after, time=after_time, bytes=total.size)
            block["came"] = self.travel("inward", block, self.edge)
            self.blocks.append(block)
        return len(self.blocks)

    def fold(self):
        block = self.blocks[self.folded]
        block["total"].fold(block["c"])
        self.inner = max(self.inner, block["came"]) + self.step
        block["crossed"] = self.travel("across", block, self.inner)
        self.folded += 1

    def close(self):
        block = self.blocks[self.closed]
        block["total"].close(block["c"])
        self.inner = max(self.inner, block["crossed"]) + self.step
        block["back"] = self.travel("outward", block, self.inner)
        self.closed += 1
        if block["after"] is not None:
            block["after"](block["c"])
            self.inner += block["time"]
            self.edge = max(self.edge, block["back"]) + block["time"]

    def next_times(self):
        never = float("inf")
        fold = self.blocks[self.folded]["came"] if self.folded < len(self.blocks) else never
        close = self.blocks[self.closed]["crossed"] if self.closed < self.folded else never
        return fold, close

    def handle(self, until):
        while True:
            fold, close = self.next_times()
            if min(fold, close) > until():
                return
            if close <= fold:
                self.close()
            else:
                self.fold()

    def __call__(self, spent):
        self.edge += spent
        self.inner += spent
        self.handle(lambda: self.inner)

    def until(self, mark):
        while self.closed < mark:
            fold, close = self.next_times()
            if close <= fold:
                self.close()
            else:
                self.fold()

    def take(self, mark):
        self.until(mark)
        self.edge = max(self.edge, self.blocks[mark - 1]["back"])


def layer_kernel(names, n, *refs):
    r = types.SimpleNamespace(**dict(zip(names, refs)))
    at = Place()
    own = r.self_out.shape[0]
    rows, width = r.tokens.shape
    frame_count = r.encoder.shape[1]
    clip_start = r.lengths[0, 0]
    half, quarter = rows // 2, rows // 4
    groups = width // GROUP
    halves = [pl.ds(0, half), pl.ds(half, half)]
    order = (1, 0)
    lower, upper = pl.ds(0, rows), pl.ds(rows, rows)
    r.low = r.big.at[0, lower]
    r.n2, r.n3, r.part_b, r.part_c = (r.packed.at[o, place] for o in (0, 1) for place in (lower, upper))
    r.dn3, r.down, r.dq2, r.other_b = (r.packed.at[o, place] for o in (2, 3) for place in (lower, upper))
    r.dn1, r.a, r.dul = r.dn3, r.layer_out, r.token_grad
    greet([(lax.rem(at.d + k, n), at.m) for k in range(1, n)] + [at.line(lax.rem(at.m + k, 4)) for k in (1, 2, 3)])

    own_rows = [r.packed.at[at.m, pl.ds(i * own, own)] for i in range(5)]
    loads = [
        pltpu.make_async_copy(source, target, r.load.at[i])
        for i, (source, target) in enumerate(
            (
                (r.self_out, own_rows[0]), (r.cross_in.at[0], own_rows[1]), (r.cross_in.at[1], own_rows[2]),
                (r.cross_in.at[2], own_rows[3]), (r.cross_out, own_rows[4]), (r.fc_up_in, r.fc_up),
                (r.fc_down_in, r.fc_down), (r.cotangent_in, r.cotangent),
            )
        )
    ]
    for load in loads:
        load.start()
    for load in loads[:5]:
        load.wait()
    r.packed[at.m, 5 * own : PLANE * SLICE] = jnp.zeros((PLANE * SLICE - 5 * own, width), bf16)
    r.bias_slots[at.m, 0:2, 0:own] = r.in_biases[2:4]
    await_greetings(n + 2)

    gather = Gather(at, r.packed, *(getattr(r, f"g_{i}") for i in range(6)))
    gather.start()
    biases = Direct(at, r.bias_slots, r.b_0, r.b_1)
    biases.start()
    parts = [Parts(at, r.parts.at[h], r.p_0.at[h], r.p_1.at[h]) for h in range(2)]

    def send_attended(h):
        self_forward(r, h, clip_start)
        for i in range(2):
            source = pl.ds(h * half + i * quarter, quarter)
            r.parts[h, at.m, :, i * own : (i + 1) * own] = r.o1[source]

    first, second = order
    self_projections(r)
    send_attended(first)
    gather.from_line(0)
    send_attended(second)
    for clip in range(2):
        r.frames[clip] = jnp.zeros_like(r.frames[clip])
        r.frames[clip, 0:frame_count] = r.encoder[clip]
    gather.from_line(1)
    gather.from_sides(0)
    gather.from_line(2)
    parts[first].start()
    gather.from_sides(1)
    gather.from_corner(0)
    parts[first].step(0)
    gather.from_sides(2)
    parts[second].start()
    gather.from_corner(1)
    parts[first].step(1)
    gather.from_corner(2)
    biases.finish()
    for o in range(4):
        r.bias[:, o * own : (o + 1) * own] = r.bias_slots[o, :, 0:own]
    for j in range(3):
        gather.from_core(j)
    for o in range(4):
        for i in range(5):
            r.big[i, o * own : (o + 1) * own] = r.packed[o, i * own : (i + 1) * own]
    gather.finish()
    keys_and_values(r, 2, None, r.k_pair)
    parts[first].step(2)
    parts[second].step(0)
    keys_and_values(r, 3, 1, r.v_pair)

    quarters = [
        [
            (pl.ds(h * half + i * quarter, quarter), pl.ds(g * GROUP, GROUP))
            for g in range(groups) for i in range(2)
        ]
        for h in range(2)
    ]
    strips = [[pl.ds(h * half + c * 64, 64) for c in range(half // 64)] for h in range(2)]

    def totals(blocks, x, ends, other, out, letter, rooms=None):
        semaphores = [getattr(r, f"{letter}_{i}") for i in range(6)]
        return [
            Total(at, halves[h], blocks[h], x, ends, other, out, *(one.at[h] for one in semaphores), rooms=rooms)
            for h in range(2)
        ]

    o2_plain = totals(quarters, r.part_a, r.ends, r.other_a, r.o2, "t")
    o2_sum = [SoftTotal(at, r, h, halves[h], quarters[h], o2_plain[h], "s", groups) for h in range(2)]
    dn3_sum = totals(strips, r.part_a, r.ends, r.other_b, r.dn3, "u")
    down_sum = totals(strips, r.part_b, r.ends_b, r.other_c, r.down, "v", rooms=strips[0])
    dq_sum = totals(quarters, r.part_a, r.ends, r.other_a, r.dq2, "q")
    dn1_sum = totals(strips, r.part_c, r.ends, r.other_b, r.dn1, "z")
    pump = Pump()
    marks = {}

    def before_cross(h):
        block = halves[h]
        for o in range(4):
            cols = pl.ds(o * own, own)
            for i in range(2):
                target = pl.ds(h * half + i * quarter, quarter)
                r.part_b[target, cols] = r.parts[h, o, :, i * own : (i + 1) * own]
        r.x2[block] = r.tokens[block].astype(f32) + nn(r.part_b[block], r.big[0]) + r.out_biases[0:1]

        def normed(inside):
            rows_of = pl.ds(pl.multiple_of(h * half + inside.start, 64), 64)
            xhat, _ = normal(r.x2[rows_of])
            r.n2[rows_of] = (xhat * r.norm_gains[1:2] + r.norm_biases[1:2]).astype(bf16)

        row_blocks(half, 64, normed)
        queries = (nt(r.n2[block], r.big[1]) + r.bias[0:1]).astype(bf16).astype(f32)
        to_pairs(queries, r.q_pair, block, clip_start, factor)

    def attend(h):
        for g in range(groups):
            for j in range(2):
                cross_forward(r, halves[h], g, j, clip_start, frame_count)
                pump(0.75)
            r.lse_own[h, g] = r.stats[g, halves[h]].T[0:8]
            marks["o2", h] = pump.add(o2_sum[h], (2 * g, 2 * g + 1))

    before_cross(first)
    attend(first)
    for j in (1, 2):
        parts[second].step(j)
    before_cross(second)
    pump(1.4)
    attend(second)

    for load in loads[5:]:
        load.wait()
    for k in range(3):
        r.bias_sums[k] = jnp.zeros_like(r.bias_sums[k])
        r.gain_sums[k] = jnp.zeros_like(r.gain_sums[k])
        r.out_sums[k] = jnp.zeros_like(r.out_sums[k])

    def back_third(h, c):
        dn3_sum[h].take(c)
        block = strips[h][c]
        upstream = r.dn3[block].astype(f32)
        grad = r.cotangent[block].astype(f32)
        change, gain = back_normal(r.x3[block], upstream, r.norm_gains[2:3])
        total = grad + change
        r.g3[block] = total
        r.low[block] = total.astype(bf16)
        r.gain_sums[2] += by_eights(gain)
        r.bias_sums[2] += by_eights(upstream)
        r.out_sums[1] += by_eights(total)
        r.out_sums[2] += by_eights(grad)

    def feed_forward(h):
        block = halves[h]
        pump.take(marks["o2", h])
        value = r.x2[block] + r.out_biases[1:2]
        for g in range(groups):
            for c in (2 * g, 2 * g + 1):
                o2_sum[h].take(c)
            cols = pl.ds(g * GROUP, GROUP)
            value = value + nn(r.o2[block, cols], r.big[4, cols])
        r.x3[block] = value
        pump(0.5)

        def normed(inside):
            rows_of = pl.ds(pl.multiple_of(h * half + inside.start, 64), 64)
            xhat, _ = normal(r.x3[rows_of])
            r.n3[rows_of] = (xhat * r.norm_gains[2:3] + r.norm_biases[2:3]).astype(bf16)

        row_blocks(half, 64, normed)
        pump(0.4)
        upward = nn(r.n3[block], r.fc_up[...]) + r.up_bias[...]
        normal_share = 0.5 * (1.0 + lax.erf(upward * (0.5**0.5)))
        density = jnp.exp(-0.5 * upward * upward) * 0.3989422804014327
        r.a[block] = (upward * normal_share).astype(bf16)
        pump(0.7)
        change = nt(r.cotangent[block], r.fc_down[...]) * (normal_share + upward * density)
        r.up_sum[h] = by_eights(change)
        r.dul[block] = change.astype(bf16)
        pump(0.6)
        o2_sum[h].finish()
        r.part_a[block] = nt(r.dul[block], r.fc_up[...]).astype(bf16)
        pump(0.4)
        marks["dn3", h] = pump.add(dn3_sum[h], range(dn3_sum[h].count), functools.partial(back_third, h), 0.3)

    feed_forward(first)
    feed_forward(second)
    for part in parts:
        part.finish()

    scatter_1 = Scatter(at, n, r.grads_1, r.came_1, r.slots_1, *(getattr(r, f"x_{i}") for i in range(4)))
    scatter_2 = Scatter(at, n, r.grads_1, r.came_2, r.slots_2, *(getattr(r, f"y_{i}") for i in range(4)))
    scatter_3 = Scatter(at, n, r.grads_3, r.came_3, r.slots_3, *(getattr(r, f"w_{i}") for i in range(4)))

    def send_down(h):
        marks["down", h] = pump.add(down_sum[h], range(down_sum[h].count))

    def take_down(h):
        pump.take(marks["down", h])
        for c in range(down_sum[h].count):
            down_sum[h].take(c)
        down_sum[h].finish()
        block = halves[h]
        r.layer_out[block] = (r.x3[block] + r.down[block].astype(f32) + r.out_biases[2:3]).astype(bf16)

    def down_part(h):
        r.part_b[halves[h]] = nn(r.a[halves[h]], r.fc_down[...]).astype(bf16)

    def run(jobs, time):
        for job in jobs:
            job()
            pump(time)

    run(weight_grad(r.grads_1, 0, r.n3, r.dul) + weight_grad(r.grads_1, width, r.cotangent, r.a), 0.5)
    scatter_1.start()
    run([functools.partial(down_part, h) for h in order], 0.4)
    send_down(first)

    def before_queries(h):
        block = halves[h]
        pump.until(marks["dn3", h])
        dn3_sum[h].finish()
        upstream = nt(r.low[block], r.big[4]).astype(bf16).astype(f32)
        to_pairs(upstream, r.do_pair, block, clip_start, 1.0)
        r.do2_sum[h] = by_eights(upstream)
        pump(0.6)
        lane = iota((half, PAIR), 1)
        for g in range(groups):
            stats = r.stats[g, block]
            for j in range(2):
                cols = slice(g * GROUP + j * PAIR, g * GROUP + (j + 1) * PAIR)
                terms = upstream[:, cols] * r.o2[block, cols].astype(f32)
                even = jnp.sum(jnp.where(lane < HEAD, terms, 0.0), axis=1, keepdims=True)
                odd = jnp.sum(jnp.where(lane < HEAD, 0.0, terms), axis=1, keepdims=True)
                stats = jnp.where(lane == 16 + 2 * j, even, jnp.where(lane == 17 + 2 * j, odd, stats))
            r.stats[g, block] = stats
        pump(0.5)

    def query_grads(h):
        before_queries(h)
        total = dq_sum[h]
        for g in range(groups):
            for j in range(2):
                cross_queries(r, halves[h], g, j, clip_start, frame_count)
                pump(0.8)
            marks["dq", h] = pump.add(total, (2 * g, 2 * g + 1))

    query_grads(first)
    scatter_1.fold()
    query_grads(second)

    def result_1():
        total = scatter_1.finish()
        r.fc_up_grad[...] = total[:, 0:width]
        r.fc_down_grad[...] = total[:, width:]

    def frame_grads(clip):
        value = tn(r.dk_t[clip], r.big[2]) + tn(r.dv_t[clip], r.big[3])
        r.encoder_grad[clip] = value[0:frame_count].astype(bf16)

    def cross_weight(source, column):
        value = sum(nn(source[clip], r.frames[clip]) for clip in range(2))
        put_blocks(r.grads_1, column, 0, value.astype(bf16).T)

    def cross_out_grad():
        own_columns(at, r.o2, r.do1)
        for job in weight_grad(r.grads_3, 5 * own, r.low, r.do1):
            job()

    def back_second(h):
        block = halves[h]
        pump.take(marks["dq", h])
        value = None
        for g in range(groups):
            for c in (2 * g, 2 * g + 1):
                dq_sum[h].take(c)
            cols = pl.ds(g * GROUP, GROUP)
            term = nn(r.dq2[block, cols], r.big[1, cols])
            value = term if value is None else value + term
        r.dn2[...] = value
        pump(0.5)

        def back(inside):
            rows_of = pl.ds(pl.multiple_of(h * half + inside.start, 64), 64)
            upstream = r.dn2[inside]
            change, gain = back_normal(r.x2[rows_of], upstream, r.norm_gains[1:2])
            total = r.g3[rows_of] + change
            r.x2[rows_of] = total
            r.low[rows_of] = total.astype(bf16)
            r.gain_sums[1] += by_eights(gain)
            r.bias_sums[1] += by_eights(upstream)
            r.out_sums[0] += by_eights(total)

        row_blocks(half, 64, back)
        pump(0.7)
        r.do1[block] = nt(r.low[block], r.self_out[...]).astype(bf16)
        self_backward(r, h, clip_start)
        pump(2.0 if h else 1.4)
        dq_sum[h].finish()
        value = nn(r.dq1[block], r.self_in[0]) + nn(r.dk1[block], r.self_in[1])
        r.part_c[block] = (value + nn(r.dv1[block], r.self_in[2])).astype(bf16)
        pump(0.4)
        marks["dn1", h] = pump.add(dn1_sum[h], range(dn1_sum[h].count), functools.partial(back_first, h), 0.3)

    def back_first(h, c):
        dn1_sum[h].take(c)
        block = strips[h][c]
        upstream = r.dn1[block].astype(f32)
        change, gain = back_normal(r.tokens[block].astype(f32), upstream, r.norm_gains[0:1])
        r.token_grad[block] = (change + r.x2[block]).astype(bf16)
        r.gain_sums[0] += by_eights(gain)
        r.bias_sums[0] += by_eights(upstream)

    def query_weight():
        own_columns(at, r.dq2, r.q1)
        for job in weight_grad(r.grads_3, 3 * own, r.n2, r.q1):
            job()
        total = jnp.sum(r.q1[...].astype(f32), axis=0, keepdims=True)
        r.in_bias_sums[2:3, 0:own] = total

    def squeeze(values):
        return jnp.sum(values, axis=0, keepdims=True)

    early = [Everyone(at, PLANE, 1, r.early_slots, r.e_0, r.e_1)]
    late = [Everyone(at, PLANE, 1, r.late_slots, r.l_0, r.l_1)]
    if n > PLANE:
        early.append(Everyone(at, n // PLANE, PLANE, r.early_slots_2, r.m_0, r.m_1))
        late.append(Everyone(at, n // PLANE, PLANE, r.late_slots_2, r.n_0, r.n_1))

    def finish_all(stages):
        total = stages[0].finish()
        for stage in stages[1:]:
            stage.slots[stage.place] = total
            stage.start()
            total = stage.finish()
        return total

    def early_vectors():
        r.in_bias_sums[1:2, 0:own] = squeeze(r.do1[...].astype(f32))
        total = squeeze(r.do2_sum[0] + r.do2_sum[1])
        for j in range(4):

            @pl.when(at.m == j)
            def _(j=j):
                r.in_bias_sums[3:4, 0:own] = total[:, j * own : (j + 1) * own]

        lines = [squeeze(r.gain_sums[k]) for k in (1, 2)] + [squeeze(r.bias_sums[k]) for k in (1, 2)]
        lines += [squeeze(r.out_sums[k]) for k in range(3)] + [squeeze(r.up_sum[0] + r.up_sum[1])]
        place = early[0].place
        r.early_slots[place, 0:8] = jnp.concatenate(lines, axis=0)
        r.early_slots[place, 8:16] = jnp.zeros((8, width), f32)
        for k in range(4):
            r.early_slots[place, 8:9, k * own : (k + 1) * own] = r.in_bias_sums[k : k + 1, 0:own]
        early[0].start()

    def early_results():
        total = finish_all(early)
        r.norm_gains_grad[1:3] = total[0:2]
        r.norm_biases_grad[1:3] = total[2:4]
        r.out_biases_grad[...] = total[4:7]
        r.up_bias_grad[...] = total[7:8]
        for k in range(4):
            r.in_biases_grad[k : k + 1] = total[8:9, k * own : (k + 1) * own]

    def result_2():
        total = scatter_2.finish()
        for j in range(4):
            for t in range(2):
                cols = slice(t * width + j * own, t * width + (j + 1) * own)
                r.plane_out[j, t] = total[:, cols].astype(bf16)
        for k in (1, 2, 3):
            to_plane(k).start()

    def to_plane(k):
        to = lax.rem(at.m + k, 4)
        return remote(r.plane_out.at[to], r.plane_slots.at[at.m], r.d_0.at[k], r.d_1.at[at.m], at.line(to))

    def result_2_end():
        total = r.plane_out[at.m].astype(f32)
        for k in (1, 2, 3):
            o = lax.rem(at.m + k, 4)
            remote(r.plane_out.at[o], r.plane_slots.at[o], r.d_0.at[k], r.d_1.at[o], at.line(o)).wait_recv()
            total = total + r.plane_slots[o].astype(f32)
        r.cross_in_grad[1:3] = total
        for k in (1, 2, 3):
            to_plane(k).wait_send()

    def result_3():
        total = scatter_3.finish()
        for i in range(3):
            r.self_in_grad[i] = total[:, i * own : (i + 1) * own]
        r.cross_in_grad[0] = total[:, 3 * own : 4 * own]
        r.self_out_grad[...] = total[:, 4 * own : 5 * own].T
        r.cross_out_grad[...] = total[:, 5 * own : 6 * own].T

    result_1()
    run([functools.partial(cross_frames, r, g, j, frame_count) for g in range(groups) for j in range(2)], 1.1)
    run([functools.partial(cross_weight, r.dk_t, 0), functools.partial(cross_weight, r.dv_t, width)], 0.8)
    scatter_2.start()
    cross_out_grad()
    pump(0.6)
    back_second(first)
    scatter_2.fold()
    pump(0.5)
    take_down(first)
    pump(0.4)
    back_second(second)
    send_down(second)
    run([query_weight] + weight_grad(r.grads_3, 4 * own, r.low, r.o1), 0.4)
    jobs = weight_grad(r.grads_3, 0, r.n1, r.dq1) + weight_grad(r.grads_3, own, r.n1, r.dk1)
    run(jobs + weight_grad(r.grads_3, 2 * own, r.n1, r.dv1), 0.3)
    scatter_3.start()
    early_vectors()
    run([functools.partial(frame_grads, clip) for clip in range(2)], 1.2)
    scatter_3.fold()
    result_2()
    pump.until(marks["dn1", second])
    for h in order:
        dn1_sum[h].finish()
    place = late[0].place
    r.late_slots[place] = jnp.zeros_like(r.late_slots[place])
    r.late_slots[place, 0:1] = squeeze(r.gain_sums[0])
    r.late_slots[place, 1:2] = squeeze(r.bias_sums[0])
    late[0].start()
    early_results()
    result_2_end()
    result_3()
    take_down(second)
    total = finish_all(late)
    r.norm_gains_grad[0:1] = total[0:1]
    r.norm_biases_grad[0:1] = total[1:2]


def layer(n, inputs):
    tokens, self_in = inputs["tokens"], inputs["self_in"]
    rows, width = tokens.shape
    own = self_in.shape[1]
    hidden = inputs["fc_up_in"].shape[1]
    groups = width // GROUP
    per = width // n
    S = jax.ShapeDtypeStruct
    outs = dict(
        layer_out=S((rows, width), bf16), token_grad=S((rows, width), bf16),
        encoder_grad=S(inputs["encoder"].shape, bf16), norm_gains_grad=S((3, width), f32),
        norm_biases_grad=S((3, width), f32), self_in_grad=S((3, per, own), f32), cross_in_grad=S((3, per, own), f32),
        in_biases_grad=S((4, own), f32), self_out_grad=S((own, per), f32), cross_out_grad=S((own, per), f32),
        out_biases_grad=S((3, width), f32), fc_up_grad=S((per, hidden), f32), up_bias_grad=S((1, hidden), f32),
        fc_down_grad=S((per, hidden), f32),
    )
    dma = pltpu.SemaphoreType.DMA
    low, full = pltpu.VMEM((rows, width), bf16), pltpu.VMEM((rows, width), f32)
    thin = pltpu.VMEM((rows, own), bf16)
    wide = pltpu.VMEM((rows, 2 * width), bf16)
    frame_pair = pltpu.VMEM((FRAMES, 2 * width), bf16)
    scratch = dict(
        fc_up=pltpu.VMEM((width, hidden), bf16), fc_down=pltpu.VMEM((hidden, width), bf16), cotangent=low,
        load=dma((8,)), big=pltpu.VMEM((5, width, width), bf16), packed=pltpu.VMEM((4, PLANE * SLICE, width), bf16), bias=pltpu.VMEM((8, width), f32),
        bias_slots=pltpu.VMEM((4, 8, 256), f32), parts=pltpu.VMEM((2, 4, rows // 4, 2 * own), bf16),
        frames=pltpu.VMEM((2, FRAMES, width), bf16), n1=low, o2=low, part_a=low, ends=low, ends_b=pltpu.VMEM((rows // 2, width), bf16), other_a=low,
        other_c=pltpu.VMEM((rows // 2, width), bf16), x2=full, x3=full, g3=full, dn2=pltpu.VMEM((rows // 2, width), f32), q1=thin, k1=thin, v1=thin, o1=thin, do1=thin, dq1=thin,
        dk1=thin, dv1=thin, lse1=pltpu.VMEM((rows, 8), f32), q_pair=wide, do_pair=wide,
        k_pair=frame_pair, v_pair=frame_pair, stats=pltpu.VMEM((groups, rows, PAIR), f32),
        **{f"lse_{name}": pltpu.VMEM((2, groups, 8, rows // 2), f32) for name in ("own", "end", "mid", "far", "all")}, dk_t=pltpu.VMEM((2, width, FRAMES), bf16),
        dv_t=pltpu.VMEM((2, width, FRAMES), bf16), dk_sum=pltpu.VMEM((own, rows), f32),
        dv_sum=pltpu.VMEM((own, rows), f32), gain_sums=pltpu.VMEM((3, 8, width), f32),
        bias_sums=pltpu.VMEM((3, 8, width), f32), out_sums=pltpu.VMEM((3, 8, width), f32),
        up_sum=pltpu.VMEM((2, 8, hidden), f32), do2_sum=pltpu.VMEM((2, 8, width), f32),
        in_bias_sums=pltpu.VMEM((8, 256), f32), early_slots=pltpu.VMEM((PLANE, 16, width), f32),
        late_slots=pltpu.VMEM((PLANE, 8, width), f32), plane_out=pltpu.VMEM((4, 2, per, own), bf16),
        plane_slots=pltpu.VMEM((4, 2, per, own), bf16), grads_1=pltpu.VMEM((n, per, 2 * width), bf16),
        grads_3=pltpu.VMEM((n, per, 6 * own), bf16),
    )
    group_dma = Total.semaphores(groups)
    part_dma = [dma((2, 5)), dma((2, 4))]
    tiles, strips = Total.semaphores(2 * groups), Total.semaphores(rows // 128)
    for letter, group in (
        ("g", Gather.semaphores()), ("b", Direct.semaphores()), ("p", part_dma), ("s", group_dma),
        ("t", tiles), ("u", strips), ("v", strips), ("q", tiles), ("z", strips), ("e", Everyone.semaphores(PLANE)), ("l", Everyone.semaphores(PLANE)),
        ("d", Direct.semaphores()),
    ):
        for i, one in enumerate(group):
            scratch[f"{letter}_{i}"] = one
    if n > PLANE:
        scratch["early_slots_2"] = pltpu.VMEM((n // PLANE, 16, width), f32)
        scratch["late_slots_2"] = pltpu.VMEM((n // PLANE, 8, width), f32)
        for letter in ("m", "n"):
            for i, one in enumerate(Everyone.semaphores(n // PLANE)):
                scratch[f"{letter}_{i}"] = one
    for k, letter, cols in ((1, "x", 2 * width), (2, "y", 2 * width), (3, "w", 6 * own)):
        came, slots, *semaphores = Scatter.buffers(n, per, cols)
        scratch[f"came_{k}"], scratch[f"slots_{k}"] = came, slots
        for i, one in enumerate(semaphores):
            scratch[f"{letter}_{i}"] = one
    names = list(inputs) + list(outs) + list(scratch)
    late = ("fc_up_in", "fc_down_in", "cotangent_in", "cross_in", "cross_out")
    result = pl.pallas_call(
        functools.partial(layer_kernel, names, n),
        out_shape=list(outs.values()),
        in_specs=[SMEM if name == "lengths" else ANY if name in late else VMEM for name in inputs],
        out_specs=[VMEM] * len(outs),
        scratch_shapes=list(scratch.values()),
        compiler_params=pltpu.CompilerParams(
            collective_id=1, has_side_effects=True, vmem_limit_bytes=127 * 2**19
        ),
        name="layer",
    )(*inputs.values())
    return dict(zip(outs, result))


def shards(
    n, tokens, encoder, lengths, norm_gains, norm_biases, self_in, cross_in, in_biases, self_out, cross_out,
    out_biases, fc_up, up_bias, fc_down, cotangent,
):
    outs = layer(
        n,
        dict(
            tokens=tokens, encoder=encoder, lengths=lengths, norm_gains=norm_gains, norm_biases=norm_biases,
            self_in=self_in.transpose(0, 2, 1),
            cross_in=cross_in.transpose(0, 2, 1), in_biases=in_biases, self_out=self_out, cross_out=cross_out,
            out_biases=out_biases, up_bias=up_bias.reshape(1, -1), fc_up_in=fc_up, fc_down_in=fc_down,
            cotangent_in=cotangent,
        ),
    )
    outs["fc_down_grad"] = outs["fc_down_grad"].T
    outs["up_bias_grad"] = outs["up_bias_grad"].reshape(-1)
    return tuple(outs.values())


def solution(mesh):
    in_specs = (
        P("dp", None), P("dp", "mp", None), P("dp", None), P(), P(), P(None, None, "mp"), P(None, None, "mp"),
        P(None, "mp"), P("mp", None), P("mp", None), P(), P(None, "mp"), P("mp"), P("mp", None), P("dp", None),
    )
    out_specs = (
        P("dp", None), P("dp", None), P("dp", "mp", None), P(), P(), P(None, "dp", "mp"), P(None, "dp", "mp"),
        P(None, "mp"), P("mp", "dp"), P("mp", "dp"), P(), P("dp", "mp"), P("mp"), P("mp", "dp"),
    )
    body = functools.partial(shards, mesh.shape["dp"])
    return jax.shard_map(body, mesh=mesh, in_specs=in_specs, out_specs=out_specs, check_vma=False)
```

```python
import functools
import types

import jax
import jax.numpy as jnp
from jax import lax
from jax.experimental import pallas as pl
from jax.experimental.pallas import tpu as pltpu
from jax.sharding import PartitionSpec as P

HEAD = 64
PAIR = 2 * HEAD
PLANE = 8
FRAMES = 384
epsilon = 1e-05
factor = 0.125
masked_value = -1e30
f32 = jnp.float32
bf16 = jnp.bfloat16
MESH = pl.DeviceIdType.MESH
VMEM = pl.BlockSpec(memory_space=pltpu.VMEM)
SMEM = pl.BlockSpec(memory_space=pltpu.SMEM)
ANY = pl.BlockSpec(memory_space=pl.ANY)


def nn(a, b):
    return jnp.dot(a, b, preferred_element_type=f32)


def nt(a, b):
    return lax.dot_general(a, b, (((1,), (1,)), ((), ())), preferred_element_type=f32)


def tn(a, b):
    return lax.dot_general(a, b, (((0,), (0,)), ((), ())), preferred_element_type=f32)


def flip(index, bit):
    return index + bit - 2 * bit * lax.rem(index // bit, 2)


def remote(src, dst, send, recv, device):
    return pltpu.make_async_remote_copy(
        src_ref=src, dst_ref=dst, send_sem=send, recv_sem=recv, device_id=device, device_id_type=MESH
    )


def greet(devices):
    barrier = pltpu.get_barrier_semaphore()
    for device in devices:
        pl.semaphore_signal(barrier, inc=1, device_id=device, device_id_type=MESH)


def await_greetings(count):
    pl.semaphore_wait(pltpu.get_barrier_semaphore(), count)


def pair_sum(left, right):
    return (left.astype(f32) + right.astype(f32)).astype(bf16)


class Place:
    def __init__(self):
        self.d, self.m = d, m = lax.axis_index("dp"), lax.axis_index("mp")
        self.mine = lax.rem(d, PLANE)
        self.base = d - self.mine
        self.half = m // 2
        self.rank = m + self.half * (3 - 2 * m)
        self.edge, self.inner = self.rank == 0, self.rank == 1
        self.near = flip(m, 1)
        self.peer = 3 - m

    def origin(self, j):
        index = 1 - self.rank if j == 0 else j + 1
        return index + self.half * (3 - 2 * index)

    def line(self, m):
        return (self.d, m)

    def plane(self, s):
        return (self.base + s, self.m)

    def way(self, k):
        s = self.mine
        for bit in (1, 2, 4):
            if k & bit:
                s = flip(s, bit)
        return s


class Gather:
    def __init__(self, at, big, own, cuts, line_send, side_send, corner_send, core_send, recv, core_recv):
        self.at, self.big, self.own, self.cuts = at, big, own, cuts
        self.line_send, self.side_send, self.corner_send = line_send, side_send, corner_send
        self.core_send, self.recv, self.core_recv = core_send, recv, core_recv
        self.core, self.chip = lax.rem(at.mine, 2), at.mine // 2
        self.pieces = range(cuts)

    def copy(self, o, chip, i, send, device):
        block = self.block(o, chip, i)
        return remote(block, block, send, self.recv.at[o, chip, i], device)

    def came(self, o, chip, i):
        self.copy(o, chip, i, self.line_send, self.at.line(self.at.m)).wait_recv()

    def start(self):
        at = self.at
        for i in self.pieces:
            self.copy(at.m, self.chip, i, self.line_send, at.line(at.near)).start()

            @pl.when(at.inner)
            def _(i=i):
                self.copy(at.m, self.chip, i, self.line_send, at.line(at.peer)).start()

    def from_line(self, j):
        at = self.at
        o = at.origin(j)
        for i in self.pieces:
            self.came(o, self.chip, i)

            @pl.when(at.inner)
            def _(i=i):
                to = at.peer if j == 0 else at.near
                self.copy(o, self.chip, i, self.line_send, at.line(to)).start()

            for k in (2, 4):
                self.copy(o, self.chip, i, self.side_send, at.plane(at.way(k))).start()

    def passed_on(self):
        return ((2, 0), (4, 1))[: self.cuts]

    def from_sides(self, j):
        at = self.at
        o = at.origin(j)
        for k, i in self.passed_on():
            chip = flip(self.chip, k // 2)
            self.came(o, chip, i)
            self.copy(o, chip, i, self.corner_send, at.plane(at.way(6 - k))).start()

    def core_copy(self, j, mine):
        block = self.core_block(self.at.origin(j), self.core if mine else 1 - self.core)
        return remote(block, block, self.core_send.at[j], self.core_recv.at[j], self.at.plane(self.at.way(1)))

    def from_corner(self, j):
        o = self.at.origin(j)
        for k in (2, 4):
            for i in self.pieces:
                if (k, i) not in self.passed_on():
                    self.came(o, flip(self.chip, k // 2), i)
        for i in self.pieces:
            self.came(o, flip(flip(self.chip, 1), 2), i)
        self.core_copy(j, True).start()

    def from_core(self, j):
        self.core_copy(j, False).wait_recv()

    def sent(self, slices, send):
        block = self.slices(slices)
        remote(block, block, send, self.core_recv.at[0], self.at.line(self.at.near)).wait_send()

    def finish(self):
        at = self.at

        @pl.when(at.edge)
        def _():
            self.sent(1, self.line_send)

        @pl.when(at.inner)
        def _():
            self.sent(5, self.line_send)

        self.sent(6, self.side_send)
        self.sent(3, self.corner_send)
        for j in range(3):
            self.core_copy(j, True).wait_send()

    @staticmethod
    def semaphores():
        dma = pltpu.SemaphoreType.DMA
        return [dma, dma, dma, dma((3,)), dma((4, 4, 2)), dma((3,))]


class GatherFour(Gather):
    def block(self, o, chip, i):
        row = o * self.own + lax.rem(chip, 2) * (self.own // 2) + i * (self.own // 4)
        return self.big.at[2 * self.core + chip // 2, pl.ds(pl.multiple_of(row, 16), self.own // 4)]

    def core_block(self, o, core):
        return self.big.at[pl.ds(2 * core, 2), pl.ds(pl.multiple_of(o * self.own, 16), self.own)]

    def slices(self, count):
        return self.big.at[0, pl.ds(0, count * self.own // 2)]


class GatherLast(Gather):
    def columns(self, core):
        half = self.big.shape[2] // 2
        return pl.ds(pl.multiple_of(core * half, PAIR), half)

    def block(self, o, chip, i):
        row = pl.multiple_of(o * self.own + chip * (self.own // 4), 16)
        return self.big.at[4, pl.ds(row, self.own // 4), self.columns(self.core)]

    def core_block(self, o, core):
        return self.big.at[4, pl.ds(pl.multiple_of(o * self.own, 16), self.own), self.columns(core)]

    def slices(self, count):
        return self.big.at[4, pl.ds(0, count * self.own // 4), pl.ds(0, self.big.shape[2] // 2)]


class Parts:
    def __init__(self, at, slots, send, recv):
        self.at, self.slots, self.send, self.recv = at, slots, send, recv

    def copy(self, o, send, to):
        return remote(self.slots.at[o], self.slots.at[o], send, self.recv.at[o], self.at.line(to))

    def own(self, to_peer):
        at = self.at
        return self.copy(at.m, self.send.at[to_peer], at.peer if to_peer else at.near)

    def forward(self, j):
        at = self.at
        return self.copy(at.origin(j), self.send.at[2 + j], at.peer if j == 0 else at.near)

    def start_edge(self):
        @pl.when(self.at.edge)
        def _():
            self.own(0).start()

    def start_inner(self):
        @pl.when(self.at.inner)
        def _():
            self.own(0).start()
            self.own(1).start()

    def came(self, j):
        self.copy(self.at.origin(j), self.send.at[0], self.at.m).wait_recv()

    def relay(self, j):
        @pl.when(self.at.inner)
        def _():
            self.came(j)
            self.forward(j).start()

    def take(self):
        @pl.when(self.at.edge)
        def _():
            for j in range(3):
                self.came(j)

    def finish(self):
        self.own(0).wait_send()

        @pl.when(self.at.inner)
        def _():
            self.own(1).wait_send()
            for j in range(3):
                self.forward(j).wait_send()

    @staticmethod
    def semaphores():
        dma = pltpu.SemaphoreType.DMA
        return [dma((5,)), dma((4,))]


class Direct:
    def __init__(self, at, slots, send, recv):
        self.at, self.slots, self.send, self.recv = at, slots, send, recv

    def copy(self, o, k):
        to = lax.rem(self.at.m + k, 4)
        return remote(self.slots.at[o], self.slots.at[o], self.send.at[k], self.recv.at[o], self.at.line(to))

    def start(self):
        for k in (1, 2, 3):
            self.copy(self.at.m, k).start()

    def finish(self):
        for k in (1, 2, 3):
            self.copy(lax.rem(self.at.m + k, 4), k).wait_recv()
        for k in (1, 2, 3):
            self.copy(self.at.m, k).wait_send()

    @staticmethod
    def semaphores():
        dma = pltpu.SemaphoreType.DMA
        return [dma((4,)), dma((4,))]


class Everyone:
    def __init__(self, at, size, stride, slots, send, recv):
        self.at, self.size, self.stride, self.slots, self.send, self.recv = at, size, stride, slots, send, recv
        self.place = lax.rem(at.d // stride, size)

    def copy(self, o, k):
        to = self.at.d + (lax.rem(self.place + k, self.size) - self.place) * self.stride
        return remote(
            self.slots.at[o], self.slots.at[o], self.send.at[k], self.recv.at[o], (to, self.at.m)
        )

    def start(self):
        for k in range(1, self.size):
            self.copy(self.place, k).start()

    def finish(self):
        for k in range(1, self.size):
            self.copy(lax.rem(self.place + k, self.size), k).wait_recv()
        for k in range(1, self.size):
            self.copy(self.place, k).wait_send()
        total = self.slots[0]
        for o in range(1, self.size):
            total = total + self.slots[o]
        return total

    @staticmethod
    def semaphores(size):
        dma = pltpu.SemaphoreType.DMA
        return [dma((size,)), dma((size,))]


class Scatter:
    def __init__(self, at, n, x, came, slots, s1, r1, s2, r2):
        self.at, self.x, self.came, self.slots = at, x, came, slots
        self.s1, self.r1, self.s2, self.r2 = s1, r1, s2, r2
        self.core, self.chip, self.chips = lax.rem(at.d, 2), at.d // 2, n // 2
        self.order = list(range(1, self.chips)) + [0]

    def to_sibling(self, k):
        c = lax.rem(self.chip + k, self.chips)
        other = 1 - self.core
        return remote(
            self.x.at[2 * c + other], self.came.at[c], self.s1.at[c], self.r1.at[c],
            (2 * self.chip + other, self.at.m),
        )

    def between(self, k, slot):
        c = lax.rem(self.chip + k, self.chips)
        return remote(
            self.x.at[2 * c + self.core], self.slots.at[slot], self.s2.at[c], self.r2.at[slot],
            (2 * c + self.core, self.at.m),
        )

    def start(self):
        for k in self.order:
            self.to_sibling(k).start()

    def fold(self):
        for k in self.order:
            c = lax.rem(self.chip + k, self.chips)
            self.to_sibling(k).wait_recv()
            block = 2 * c + self.core
            self.x[block] = pair_sum(self.x[block], self.came[c])
            if k:
                self.between(k, self.chip).start()

    def finish(self):
        total = self.x[2 * self.chip + self.core].astype(f32)
        for k in range(1, self.chips):
            c = lax.rem(self.chip + k, self.chips)
            self.between(k, c).wait_recv()
            total = total + self.slots[c].astype(f32)
        for k in self.order:
            self.to_sibling(k).wait_send()
        for k in range(1, self.chips):
            self.between(k, self.chip).wait_send()
        return total

    @staticmethod
    def buffers(n, rows, cols):
        half = pltpu.VMEM((n // 2, rows, cols), bf16)
        dma = pltpu.SemaphoreType.DMA((n // 2,))
        return [half, half, dma, dma, dma, dma]


class Total:
    def __init__(self, at, whole, blocks, x, ends, other, out, sa, ra, sb, rb, sr, rr, rooms=None):
        self.at, self.whole, self.blocks, self.rooms = at, whole, blocks, rooms or blocks
        self.x, self.ends, self.other, self.out = x, ends, other, out
        self.sa, self.ra, self.sb, self.rb, self.sr, self.rr = sa, ra, sb, rb, sr, rr
        self.count = len(blocks)
        self.size = whole.size * x.shape[1] * 2 / self.count

    def inward(self, c):
        room = self.ends.at[self.rooms[c]]
        return remote(self.x.at[self.blocks[c]], room, self.sa, self.ra.at[c], self.at.line(self.at.near))

    def across(self, c):
        room = self.other.at[self.rooms[c]]
        return remote(self.x.at[self.blocks[c]], room, self.sb, self.rb.at[c], self.at.line(self.at.peer))

    def outward(self, c):
        block = self.out.at[self.blocks[c]]
        return remote(block, block, self.sr, self.rr.at[c], self.at.line(self.at.near))

    def send(self, c):
        @pl.when(self.at.edge)
        def _():
            self.inward(c).start()

    def fold(self, c):
        @pl.when(self.at.inner)
        def _():
            b = self.blocks[c]
            self.inward(c).wait_recv()
            self.x[b] = pair_sum(self.x[b], self.ends[self.rooms[c]])
            self.across(c).start()

    def close(self, c):
        @pl.when(self.at.inner)
        def _():
            b = self.blocks[c]
            self.across(c).wait_recv()
            self.out[b] = pair_sum(self.x[b], self.other[self.rooms[c]])
            self.outward(c).start()

    def take(self, c):
        @pl.when(self.at.edge)
        def _():
            self.outward(c).wait_recv()

    def sent(self, source, send):
        block = source.at[self.whole]
        remote(block, block, send, self.ra.at[0], self.at.line(self.at.near)).wait_send()

    def finish(self):
        @pl.when(self.at.edge)
        def _():
            self.sent(self.x, self.sa)

        @pl.when(self.at.inner)
        def _():
            self.sent(self.x, self.sb)
            self.sent(self.out, self.sr)

    @staticmethod
    def semaphores(count):
        dma = pltpu.SemaphoreType.DMA
        return [dma((2,)), dma((2, count))] * 3


class SoftTotal:
    def __init__(self, at, r, h, block, blocks, sums, letter, groups):
        self.at, self.r, self.h, self.block, self.sums = at, r, h, block, sums
        self.semaphores = [getattr(r, f"{letter}_{i}").at[h] for i in range(6)]
        self.blocks, self.groups = blocks, groups
        self.count = len(blocks)
        self.each = self.count // groups
        self.size = sums.size

    def small(self, kind, source, target, g, to):
        send, recv = self.semaphores[2 * kind], self.semaphores[2 * kind + 1]
        return remote(source.at[self.h, g], target.at[self.h, g], send, recv.at[g], self.at.line(to))

    def small_sent(self, kind, source):
        whole = source.at[self.h]
        send, recv = self.semaphores[2 * kind], self.semaphores[2 * kind + 1]
        remote(whole, whole, send, recv.at[0], self.at.line(self.at.near)).wait_send()

    def inward(self, g):
        return self.small(0, self.r.lse_own, self.r.lse_end, g, self.at.near)

    def across(self, g):
        return self.small(1, self.r.lse_mid, self.r.lse_far, g, self.at.peer)

    def outward(self, g):
        return self.small(2, self.r.lse_all, self.r.lse_all, g, self.at.near)

    def spread(self, tables, rows, tile):
        low = iota((rows.size, PAIR), 1) < HEAD
        return jnp.where(low, tables[:, 2 * tile : 2 * tile + 1], tables[:, 2 * tile + 1 : 2 * tile + 2])

    def columns(self, *tables):
        spare = jnp.zeros((PAIR - 8 * len(tables), self.block.size), f32)
        return jnp.concatenate([*tables, spare], axis=0).T

    def merge(self, left, right):
        top = jnp.maximum(left, right)
        total = top + jnp.log(jnp.exp(left - top) + jnp.exp(right - top))
        return total, jnp.exp(left - total), jnp.exp(right - total)

    def send(self, c):
        g = c // self.each

        @pl.when(self.at.edge)
        def _():
            if c % self.each == 0:
                self.inward(g).start()
            rows, cols = self.blocks[c]
            self.r.part_a[rows, cols] = self.r.g3[rows, cols].astype(bf16)

        self.sums.send(c)

    def fold(self, c):
        r, sums, g = self.r, self.sums, c // self.each

        @pl.when(self.at.inner)
        def _():
            if c % self.each == 0:
                self.inward(g).wait_recv()
                total, own, end = self.merge(r.lse_own[self.h, g], r.lse_end[self.h, g])
                r.lse_mid[self.h, g] = total
                self.across(g).start()
                r.stats[g, self.block] = self.columns(own, end)
            sums.inward(c).wait_recv()
            rows, cols = self.blocks[c]
            table = r.stats[g, rows]
            for t in range(2):
                tile = pl.ds(cols.start + t * PAIR, PAIR)
                value = r.g3[rows, tile] * self.spread(table, rows, t)
                value = value + r.ends[rows, tile].astype(f32) * self.spread(table[:, 8:], rows, t)
                r.part_a[rows, tile] = value.astype(bf16)
            sums.across(c).start()

    def close(self, c):
        r, sums, g, at = self.r, self.sums, c // self.each, self.at

        @pl.when(at.inner)
        def _():
            lower = at.half == 0
            if c % self.each == 0:
                self.across(g).wait_recv()
                mid, far = r.lse_mid[self.h, g], r.lse_far[self.h, g]
                total, left, right = self.merge(jnp.where(lower, mid, far), jnp.where(lower, far, mid))
                r.lse_all[self.h, g] = total
                self.outward(g).start()
                r.stats[g, self.block] = self.columns(total, left, right)
            sums.across(c).wait_recv()
            rows, cols = self.blocks[c]
            table = r.stats[g, rows]
            for t in range(2):
                tile = pl.ds(cols.start + t * PAIR, PAIR)
                mid, far = r.part_a[rows, tile].astype(f32), r.other_a[rows, tile].astype(f32)
                left, right = jnp.where(lower, mid, far), jnp.where(lower, far, mid)
                value = left * self.spread(table[:, 8:], rows, t) + right * self.spread(table[:, 16:], rows, t)
                r.o2[rows, tile] = value.astype(bf16)
            sums.outward(c).start()

    def take(self, c):
        g = c // self.each
        self.sums.take(c)
        if c % self.each == 0:

            @pl.when(self.at.edge)
            def _():
                self.outward(g).wait_recv()
                self.r.stats[g, self.block] = self.columns(self.r.lse_all[self.h, g])

    def finish(self):
        self.sums.finish()

        @pl.when(self.at.edge)
        def _():
            self.small_sent(0, self.r.lse_own)

        @pl.when(self.at.inner)
        def _():
            self.small_sent(1, self.r.lse_mid)
            self.small_sent(2, self.r.lse_all)


def normal(values):
    average = jnp.mean(values, axis=-1, keepdims=True)
    centred = values - average
    variance = jnp.mean(centred * centred, axis=-1, keepdims=True)
    scale = lax.rsqrt(variance + epsilon)
    return centred * scale, scale


def row_blocks(count, size, body):
    def step(i, carry):
        body(pl.ds(pl.multiple_of(i * size, size), size))
        return carry

    lax.fori_loop(0, count // size, step, 0)


def iota(shape, axis):
    return lax.broadcasted_iota(jnp.int32, shape, axis)


def pair_tiles(tile):
    turned = pltpu.roll(tile, HEAD, axis=1)
    low = iota(tile.shape, 1) < HEAD
    return jnp.where(low, tile, turned), jnp.where(low, turned, tile)


def back_normal(values, upstream, gain):
    xhat, scale = normal(values)
    scaled = upstream * gain
    first = jnp.mean(scaled, axis=-1, keepdims=True)
    second = jnp.mean(scaled * xhat, axis=-1, keepdims=True)
    return scale * (scaled - first - xhat * second), upstream * xhat


def by_eights(values):
    return jnp.sum(values.reshape(-1, 8, values.shape[1]), axis=0)


def own_columns(at, source, target):
    width = target.shape[1]
    for j in range(4):

        @pl.when(at.m == j)
        def _(j=j):
            target[...] = source[:, j * width : (j + 1) * width]


def self_mask(rows, keys, start, clip_start):
    row = iota((rows, keys), 0) + start
    col = iota((rows, keys), 1)
    return jnp.logical_and(col <= row, (row >= clip_start) == (col >= clip_start))


def self_projections(r):
    rows = r.tokens.shape[0]

    def normed(block):
        xhat, _ = normal(r.tokens[block].astype(f32))
        r.n1[block] = (xhat * r.norm_gains[0:1] + r.norm_biases[0:1]).astype(bf16)

    row_blocks(rows, 64, normed)
    r.q1[...] = (nt(r.n1[...], r.self_in[0]) + r.in_biases[0:1]).astype(bf16)
    r.k1[...] = nt(r.n1[...], r.self_in[1]).astype(bf16)
    r.v1[...] = (nt(r.n1[...], r.self_in[2]) + r.in_biases[1:2]).astype(bf16)


def self_forward(r, part, clip_start):
    half = r.tokens.shape[0] // 2
    block, keys = pl.ds(part * half, half), (part + 1) * half
    allowed = self_mask(half, keys, part * half, clip_start)
    for h in range(r.q1.shape[1] // HEAD):
        cols = pl.ds(h * HEAD, HEAD)
        scores = nt(r.q1[block, cols] * bf16(factor), r.k1[0:keys, cols])
        scores = jnp.where(allowed, scores, masked_value)
        top = jnp.max(scores, axis=1, keepdims=True)
        power = jnp.exp(scores - top)
        total = jnp.sum(power, axis=1, keepdims=True)
        chance = (power * (1 / total)).astype(bf16)
        r.o1[block, cols] = nn(chance, r.v1[0:keys, cols]).astype(bf16)
        r.lse1[block, pl.ds(h, 1)] = top + jnp.log(total)


def self_backward(r, part, clip_start):
    half = r.tokens.shape[0] // 2
    block, keys = pl.ds(part * half, half), (part + 1) * half
    allowed = self_mask(half, keys, part * half, clip_start)
    for h in range(r.q1.shape[1] // HEAD):
        cols = pl.ds(h * HEAD, HEAD)
        query, upstream = r.q1[block, cols] * bf16(factor), r.do1[block, cols]
        scores = jnp.where(allowed, nt(query, r.k1[0:keys, cols]), masked_value)
        chance = jnp.exp(scores - r.lse1[block, pl.ds(h, 1)])
        slope = nt(upstream, r.v1[0:keys, cols])
        inner = jnp.sum(chance * slope, axis=1, keepdims=True)
        change = (chance * (slope - inner)).astype(bf16)
        query_grad = nn(change, r.k1[0:keys, cols]) * factor
        r.dq1[block, cols] = query_grad.astype(bf16)
        bias = jnp.sum(query_grad, axis=0, keepdims=True)
        key_grad, value_grad = tn(query, change), tn(upstream, chance.astype(bf16))
        if part:
            r.in_bias_sums[0:1, cols] = bias
            r.dk_sum[cols, :] = key_grad
            r.dv_sum[cols, :] = value_grad
        else:
            r.in_bias_sums[0:1, cols] += bias
            r.dk_sum[cols, 0:keys] += key_grad
            r.dv_sum[cols, 0:keys] += value_grad
    r.dk1[block] = r.dk_sum[:, block].T.astype(bf16)
    r.dv1[block] = r.dv_sum[:, block].T.astype(bf16)


def keys_and_values(r, matrix, bias, pairs):
    both = [nt(r.frames[clip], r.big[matrix]) for clip in range(2)]
    if bias is not None:
        both = [value + r.bias[bias : bias + 1] for value in both]
    for t in range(both[0].shape[1] // PAIR):
        first, second = (value[:, t * PAIR : (t + 1) * PAIR] for value in both)
        low = iota(first.shape, 1) < HEAD
        turned_first, turned_second = pltpu.roll(first, HEAD, axis=1), pltpu.roll(second, HEAD, axis=1)
        pairs[:, 2 * t * PAIR : (2 * t + 1) * PAIR] = jnp.where(low, first, turned_second).astype(bf16)
        pairs[:, (2 * t + 1) * PAIR : (2 * t + 2) * PAIR] = jnp.where(low, turned_first, second).astype(bf16)


def to_pairs(value, pairs, block, clip_start, scale):
    rows = value.shape[0]
    keep = (iota((rows, PAIR), 1) < HEAD) == (iota((rows, PAIR), 0) + block.start < clip_start)
    for t in range(value.shape[1] // PAIR):
        for e, tile in enumerate(pair_tiles(value[:, t * PAIR : (t + 1) * PAIR])):
            at = (2 * t + e) * PAIR
            pairs[block, at : at + PAIR] = (jnp.where(keep, tile, 0.0) * scale).astype(bf16)


def from_pair(even, odd, first):
    low = iota(even.shape, 1) < HEAD
    even = jnp.where(first, even, pltpu.roll(even, HEAD, axis=1))
    odd = jnp.where(first, pltpu.roll(odd, HEAD, axis=1), odd)
    return jnp.where(low, even, odd)


GROUP = 2 * PAIR
GROUP_HEADS = 4


def of_clip(block, clip_start):
    return iota((block.size, PAIR), 0) + block.start < clip_start


def real_frames(rows, frame_count):
    return iota((rows, FRAMES), 1) < frame_count


def cross_forward(r, block, g, j, clip_start, frame_count):
    lane = iota((block.size, PAIR), 1)
    first = of_clip(block, clip_start)
    valid = real_frames(block.size, frame_count)
    halves = []
    stats = jnp.zeros((block.size, PAIR), f32) if j == 0 else r.stats[g, block]
    for e in (0, 1):
        cols = pl.ds(2 * GROUP * g + 2 * PAIR * j + PAIR * e, PAIR)
        scores = jnp.where(valid, nt(r.q_pair[block, cols], r.k_pair[:, cols]), masked_value)
        top = jnp.max(scores, axis=1, keepdims=True)
        power = jnp.exp(scores - top)
        total = jnp.sum(power, axis=1, keepdims=True)
        halves.append(nn(power.astype(bf16), r.v_pair[:, cols]) * (1 / total))
        stats = jnp.where(lane == 2 * j + e, top + jnp.log(total), stats)
    r.stats[g, block] = stats
    r.g3[block, pl.ds(GROUP * g + PAIR * j, PAIR)] = from_pair(*halves, first)


def cross_slopes(r, block, cols, lane, stats, index, valid):
    def column(i):
        return jnp.sum(jnp.where(lane == i, stats, 0.0), axis=1, keepdims=True)

    scores = jnp.where(valid, nt(r.q_pair[block, cols], r.k_pair[:, cols]), masked_value)
    chance = jnp.exp(scores - column(index))
    slope = nt(r.do_pair[block, cols], r.v_pair[:, cols])
    return chance, (chance * (slope - column(16 + index))).astype(bf16)


def cross_queries(r, block, g, j, clip_start, frame_count):
    lane = iota((block.size, PAIR), 1)
    first = of_clip(block, clip_start)
    valid = real_frames(block.size, frame_count)
    stats = r.stats[g, block]
    halves = []
    for e in (0, 1):
        cols = pl.ds(2 * GROUP * g + 2 * PAIR * j + PAIR * e, PAIR)
        _, change = cross_slopes(r, block, cols, lane, stats, 2 * j + e, valid)
        halves.append(nn(change, r.k_pair[:, cols]) * factor)
    r.part_a[block, pl.ds(GROUP * g + PAIR * j, PAIR)] = from_pair(*halves, first).astype(bf16)


def cross_frames(r, g, j, frame_count):
    rows = r.q_pair.shape[0]
    block = pl.ds(0, rows)
    lane = iota((rows, PAIR), 1)
    valid = real_frames(rows, frame_count)
    for e in (0, 1):
        cols = pl.ds(2 * GROUP * g + 2 * PAIR * j + PAIR * e, PAIR)
        chance, change = cross_slopes(r, block, cols, lane, r.stats[g], 2 * j + e, valid)
        value_grad = tn(r.do_pair[:, cols], chance.astype(bf16)).astype(bf16)
        key_grad = tn(r.q_pair[:, cols], change).astype(bf16)
        head = pl.ds(GROUP * g + PAIR * j + HEAD * e, HEAD)
        for clip in range(2):
            r.dv_t[clip, head] = value_grad[clip * HEAD : (clip + 1) * HEAD]
            r.dk_t[clip, head] = key_grad[clip * HEAD : (clip + 1) * HEAD]


def put_blocks(x, column, first_row, value):
    per = x.shape[1]
    for i in range(value.shape[0] // per):
        x[first_row // per + i, :, column : column + value.shape[1]] = value[i * per : (i + 1) * per].astype(bf16)


def weight_grad(x, column, left, right):
    part = left.shape[1] // 2
    return [
        functools.partial(
            lambda i: put_blocks(x, column, i * part, tn(left[:, i * part : (i + 1) * part], right[...])), i
        )
        for i in range(2)
    ]


class Pump:
    latency, rate, step, issue = 1.8, 47.0e3, 0.27, 0.1

    def __init__(self):
        self.blocks, self.folded, self.closed, self.tasks = [], 0, 0, []
        self.edge, self.inner = 0.0, 0.0
        self.free = dict(inward=0.0, across=0.0, outward=0.0)

    def travel(self, link, block, start):
        self.free[link] = max(self.free[link], start) + block["bytes"] / self.rate
        return self.free[link] + self.latency

    def add(self, total, chosen, after=None, after_time=0.0):
        for c in chosen:
            total.send(c)
            self.edge += self.issue
            block = dict(total=total, c=c, after=after, time=after_time, bytes=total.size)
            block["came"] = self.travel("inward", block, self.edge)
            self.blocks.append(block)
        return len(self.blocks)

    def fold(self):
        block = self.blocks[self.folded]
        block["total"].fold(block["c"])
        self.inner = max(self.inner, block["came"]) + self.step
        block["crossed"] = self.travel("across", block, self.inner)
        self.folded += 1

    def close(self):
        block = self.blocks[self.closed]
        block["total"].close(block["c"])
        self.inner = max(self.inner, block["crossed"]) + self.step
        block["back"] = self.travel("outward", block, self.inner)
        self.closed += 1
        if block["after"] is not None:
            block["after"](block["c"])
            self.inner += block["time"]
            self.edge = max(self.edge, block["back"]) + block["time"]

    def next_step(self):
        steps = []
        if self.closed < self.folded:
            steps.append((self.blocks[self.closed]["crossed"], self.close))
        if self.folded < len(self.blocks):
            steps.append((self.blocks[self.folded]["came"], self.fold))
        if self.tasks:
            steps.append((self.tasks[0][0], self.run_task))
        return min(steps, key=lambda step: step[0], default=(float("inf"), None))

    def __call__(self, spent):
        self.edge += spent
        self.inner += spent
        while True:
            time, step = self.next_step()
            if time > self.inner:
                return
            step()

    def until(self, mark):
        while self.closed < mark:
            self.next_step()[1]()

    def now(self):
        return max(self.edge, self.inner)

    def later(self, wait, spent, task):
        self.tasks.append((self.now() + wait, spent, task))
        self.tasks.sort(key=lambda entry: entry[0])

    def run_task(self):
        ready, spent, task = self.tasks.pop(0)
        self.edge, self.inner = max(self.edge, ready) + spent, max(self.inner, ready) + spent
        task()

    def flush(self):
        while self.tasks:
            self.run_task()

    def take(self, mark):
        self.until(mark)
        self.edge = max(self.edge, self.blocks[mark - 1]["back"])


def layer_kernel(names, n, *refs):
    r = types.SimpleNamespace(**dict(zip(names, refs)))
    at = Place()
    own = r.self_out.shape[0]
    rows, width = r.tokens.shape
    frame_count = r.encoder.shape[0]
    clip_start = r.lengths[0, 0]
    half, quarter = rows // 2, rows // 4
    groups = width // GROUP
    halves = [pl.ds(0, half), pl.ds(half, half)]
    order = (1, 0)
    r.low = r.big.at[0, pl.ds(0, rows)]
    r.dn1, r.a, r.dul = r.dn3, r.layer_out, r.token_grad
    greet([(lax.rem(at.d + k, n), at.m) for k in range(1, n)] + [at.line(lax.rem(at.m + k, 4)) for k in (1, 2, 3)])

    own_rows = [r.big.at[i, pl.ds(pl.multiple_of(at.m * own, 16), own)] for i in range(5)]
    loads = [
        pltpu.make_async_copy(source, target, r.load.at[i])
        for i, (source, target) in enumerate(
            (
                (r.self_out, own_rows[0]), (r.cross_in.at[0], own_rows[1]), (r.cross_in.at[1], own_rows[2]),
                (r.cross_in.at[2], own_rows[3]), (r.cross_out, own_rows[4]), (r.fc_up_in, r.fc_up),
                (r.fc_down_in, r.fc_down), (r.cotangent_in, r.cotangent),
            )
        )
    ]
    for load in loads:
        load.start()
    for load in loads[:5]:
        load.wait()
    r.bias_slots[at.m, 0:2, 0:own] = r.in_biases[2:4]
    await_greetings(n + 2)

    gather = GatherFour(at, r.big, own, 2, *(getattr(r, f"g_{i}") for i in range(6)))
    last = GatherLast(at, r.big, own, 1, *(getattr(r, f"h_{i}") for i in range(6)))
    gather.start()
    biases = Direct(at, r.bias_slots, r.b_0, r.b_1)
    biases.start()
    parts = [Parts(at, r.parts.at[h], r.p_0.at[h], r.p_1.at[h]) for h in range(2)]

    def send_attended(h):
        self_forward(r, h, clip_start)
        for i in range(2):
            source = pl.ds(h * half + i * quarter, quarter)
            r.parts[h, at.m, :, i * own : (i + 1) * own] = r.o1[source]

    first, second = order
    self_projections(r)
    send_attended(first)
    parts[first].start_edge()
    gather.from_line(0)
    send_attended(second)
    parts[second].start_edge()
    frames = jnp.swapaxes(r.encoder[...], 0, 1)
    for clip in range(2):
        r.frames[clip] = jnp.zeros_like(r.frames[clip])
        r.frames[clip, 0:frame_count] = frames[clip]
    gather.from_line(1)
    parts[first].relay(0)
    gather.from_sides(0)
    gather.from_line(2)
    parts[first].start_inner()
    gather.from_sides(1)
    gather.from_corner(0)
    parts[first].relay(1)
    parts[first].relay(2)
    parts[second].start_inner()
    parts[second].relay(0)
    gather.from_sides(2)
    gather.from_corner(1)
    gather.from_corner(2)
    biases.finish()
    for o in range(4):
        r.bias[:, o * own : (o + 1) * own] = r.bias_slots[o, :, 0:own]
    for j in range(3):
        gather.from_core(j)
    parts[second].relay(1)
    parts[second].relay(2)
    last.start()
    keys_and_values(r, 2, None, r.k_pair)
    keys_and_values(r, 3, 1, r.v_pair)
    parts[first].take()

    quarters = [
        [
            (pl.ds(h * half + i * quarter, quarter), pl.ds(g * GROUP, GROUP))
            for g in range(groups) for i in range(2)
        ]
        for h in range(2)
    ]
    strips = [[pl.ds(h * half + c * 64, 64) for c in range(half // 64)] for h in range(2)]

    def totals(blocks, x, ends, other, out, letter, rooms=None):
        semaphores = [getattr(r, f"{letter}_{i}") for i in range(6)]
        return [
            Total(at, halves[h], blocks[h], x, ends, other, out, *(one.at[h] for one in semaphores), rooms=rooms)
            for h in range(2)
        ]

    o2_plain = totals(quarters, r.part_a, r.ends, r.other_a, r.o2, "t")
    o2_sum = [SoftTotal(at, r, h, halves[h], quarters[h], o2_plain[h], "s", groups) for h in range(2)]
    dn3_sum = totals(strips, r.part_a, r.ends, r.other_b, r.dn3, "u")
    down_sum = totals(strips, r.part_b, r.ends_b, r.other_c, r.down, "v", rooms=strips[0])
    dq_sum = totals(quarters, r.part_a, r.ends, r.other_a, r.dq2, "q")
    dn1_sum = totals(strips, r.part_c, r.ends, r.other_b, r.dn1, "z")
    pump = Pump()
    marks = {}

    def before_cross(h):
        block = halves[h]
        for o in range(4):
            cols = pl.ds(o * own, own)
            for i in range(2):
                target = pl.ds(h * half + i * quarter, quarter)
                r.part_b[target, cols] = r.parts[h, o, :, i * own : (i + 1) * own]
        r.x2[block] = r.tokens[block].astype(f32) + nn(r.part_b[block], r.big[0]) + r.out_biases[0:1]

        def normed(inside):
            rows_of = pl.ds(pl.multiple_of(h * half + inside.start, 64), 64)
            xhat, _ = normal(r.x2[rows_of])
            r.n2[rows_of] = (xhat * r.norm_gains[1:2] + r.norm_biases[1:2]).astype(bf16)

        row_blocks(half, 64, normed)
        queries = (nt(r.n2[block], r.big[1]) + r.bias[0:1]).astype(bf16).astype(f32)
        to_pairs(queries, r.q_pair, block, clip_start, factor)

    def attend(h, between):
        for g in range(groups):
            for j in range(2):
                cross_forward(r, halves[h], g, j, clip_start, frame_count)
                pump(0.75)
            r.lse_own[h, g] = r.stats[g, halves[h]].T[0:8]
            marks["o2", h] = pump.add(o2_sum[h], (2 * g, 2 * g + 1))
            for step in between[g]:
                step()

    def last_step(name, j):
        return functools.partial(getattr(last, name), j)

    before_cross(first)
    attend(
        first,
        [
            [last_step("from_line", 0)],
            [last_step("from_line", 1), last_step("from_sides", 0)],
            [last_step("from_line", 2), last_step("from_sides", 1), last_step("from_corner", 0)],
        ],
    )
    parts[second].take()
    before_cross(second)
    pump(1.4)
    attend(
        second,
        [
            [last_step("from_sides", 2), last_step("from_corner", 1)],
            [last_step("from_corner", 2)],
            [last_step("from_core", j) for j in range(3)],
        ],
    )

    for load in loads[5:]:
        load.wait()
    for k in range(3):
        r.bias_sums[k] = jnp.zeros_like(r.bias_sums[k])
        r.gain_sums[k] = jnp.zeros_like(r.gain_sums[k])
        r.out_sums[k] = jnp.zeros_like(r.out_sums[k])

    def back_third(h, c):
        dn3_sum[h].take(c)
        block = strips[h][c]
        upstream = r.dn3[block].astype(f32)
        grad = r.cotangent[block].astype(f32)
        change, gain = back_normal(r.x3[block], upstream, r.norm_gains[2:3])
        total = grad + change
        r.g3[block] = total
        r.low[block] = total.astype(bf16)
        r.gain_sums[2] += by_eights(gain)
        r.bias_sums[2] += by_eights(upstream)
        r.out_sums[1] += by_eights(total)
        r.out_sums[2] += by_eights(grad)

    def feed_forward(h):
        block = halves[h]
        pump.take(marks["o2", h])
        value = r.x2[block] + r.out_biases[1:2]
        for g in range(groups):
            for c in (2 * g, 2 * g + 1):
                o2_sum[h].take(c)
            cols = pl.ds(g * GROUP, GROUP)
            value = value + nn(r.o2[block, cols], r.big[4, cols])
        r.x3[block] = value
        pump(0.5)

        def normed(inside):
            rows_of = pl.ds(pl.multiple_of(h * half + inside.start, 64), 64)
            xhat, _ = normal(r.x3[rows_of])
            r.n3[rows_of] = (xhat * r.norm_gains[2:3] + r.norm_biases[2:3]).astype(bf16)

        row_blocks(half, 64, normed)
        pump(0.4)
        upward = nn(r.n3[block], r.fc_up[...]) + r.up_bias[...].reshape(1, -1)
        normal_share = 0.5 * (1.0 + lax.erf(upward * (0.5**0.5)))
        density = jnp.exp(-0.5 * upward * upward) * 0.3989422804014327
        r.a[block] = (upward * normal_share).astype(bf16)
        pump(0.7)
        change = nt(r.cotangent[block], r.fc_down[...]) * (normal_share + upward * density)
        r.up_sum[h] = by_eights(change)
        r.dul[block] = change.astype(bf16)
        pump(0.6)
        o2_sum[h].finish()
        r.part_a[block] = nt(r.dul[block], r.fc_up[...]).astype(bf16)
        pump(0.4)
        marks["dn3", h] = pump.add(dn3_sum[h], range(dn3_sum[h].count), functools.partial(back_third, h), 0.3)

    feed_forward(first)
    feed_forward(second)
    gather.finish()
    last.finish()
    for part in parts:
        part.finish()

    scatter_1 = Scatter(at, n, r.grads_1, r.came_1, r.slots_1, *(getattr(r, f"x_{i}") for i in range(4)))
    scatter_2 = Scatter(at, n, r.grads_1, r.came_2, r.slots_2, *(getattr(r, f"y_{i}") for i in range(4)))
    scatter_3 = Scatter(at, n, r.grads_3, r.came_3, r.slots_3, *(getattr(r, f"w_{i}") for i in range(4)))

    def down_came(h, c):
        down_sum[h].take(c)
        block = strips[h][c]
        r.layer_out[block] = (r.x3[block] + r.down[block].astype(f32) + r.out_biases[2:3]).astype(bf16)

    def send_down(h):
        marks["down", h] = pump.add(
            down_sum[h], range(down_sum[h].count), functools.partial(down_came, h), 0.15
        )

    def launch(scatter, result):
        size = scatter.x.shape[1] * scatter.x.shape[2] * 2
        scatter.start()

        def between_chips():
            scatter.fold()
            sides["free"] = max(sides["free"], pump.now()) + 4 * size / 94e3
            pump.later(sides["free"] - pump.now() + 3.0, 0.7, result)

        pump.later(4 * size / 400e3 + 2.5, 1.5, between_chips)

    sides, done = dict(free=0.0), []

    def result_1():
        total = scatter_1.finish()
        done.append(1)
        r.fc_up_grad[...] = total[:, 0:width]
        r.fc_down_grad[...] = total[:, width:]


    def down_part(h):
        r.part_b[halves[h]] = nn(r.a[halves[h]], r.fc_down[...]).astype(bf16)

    def run(jobs, time):
        for job in jobs:
            job()
            pump(time)

    run(weight_grad(r.grads_1, 0, r.n3, r.dul) + weight_grad(r.grads_1, width, r.cotangent, r.a), 0.5)
    launch(scatter_1, result_1)
    run([functools.partial(down_part, h) for h in order], 0.4)
    send_down(first)

    def before_queries(h):
        block = halves[h]
        pump.until(marks["dn3", h])
        dn3_sum[h].finish()
        upstream = nt(r.low[block], r.big[4]).astype(bf16).astype(f32)
        to_pairs(upstream, r.do_pair, block, clip_start, 1.0)
        r.do2_sum[h] = by_eights(upstream)
        pump(0.6)
        lane = iota((half, PAIR), 1)
        for g in range(groups):
            stats = r.stats[g, block]
            for j in range(2):
                cols = slice(g * GROUP + j * PAIR, g * GROUP + (j + 1) * PAIR)
                terms = upstream[:, cols] * r.o2[block, cols].astype(f32)
                even = jnp.sum(jnp.where(lane < HEAD, terms, 0.0), axis=1, keepdims=True)
                odd = jnp.sum(jnp.where(lane < HEAD, 0.0, terms), axis=1, keepdims=True)
                stats = jnp.where(lane == 16 + 2 * j, even, jnp.where(lane == 17 + 2 * j, odd, stats))
            r.stats[g, block] = stats
        pump(0.5)

    def query_grads(h):
        before_queries(h)
        total = dq_sum[h]
        for g in range(groups):
            for j in range(2):
                cross_queries(r, halves[h], g, j, clip_start, frame_count)
                pump(0.8)
            marks["dq", h] = pump.add(total, (2 * g, 2 * g + 1))

    query_grads(first)
    query_grads(second)


    def frame_grads(clip):
        value = tn(r.dk_t[clip], r.big[2]) + tn(r.dv_t[clip], r.big[3])
        r.encoder_grad[:, clip, :] = value[0:frame_count].astype(bf16)

    def cross_weight(source, column):
        value = sum(nn(source[clip], r.frames[clip]) for clip in range(2))
        put_blocks(r.grads_1, column, 0, value.astype(bf16).T)

    def cross_out_grad():
        own_columns(at, r.o2, r.do1)
        for job in weight_grad(r.grads_3, 5 * own, r.low, r.do1):
            job()

    def back_second(h):
        block = halves[h]
        pump.take(marks["dq", h])
        value = None
        for g in range(groups):
            for c in (2 * g, 2 * g + 1):
                dq_sum[h].take(c)
            cols = pl.ds(g * GROUP, GROUP)
            term = nn(r.dq2[block, cols], r.big[1, cols])
            value = term if value is None else value + term
        r.dn2[...] = value
        pump(0.5)

        def back(inside):
            rows_of = pl.ds(pl.multiple_of(h * half + inside.start, 64), 64)
            upstream = r.dn2[inside]
            change, gain = back_normal(r.x2[rows_of], upstream, r.norm_gains[1:2])
            total = r.g3[rows_of] + change
            r.x2[rows_of] = total
            r.low[rows_of] = total.astype(bf16)
            r.gain_sums[1] += by_eights(gain)
            r.bias_sums[1] += by_eights(upstream)
            r.out_sums[0] += by_eights(total)

        row_blocks(half, 64, back)
        pump(0.7)
        r.do1[block] = nt(r.low[block], r.self_out[...]).astype(bf16)
        self_backward(r, h, clip_start)
        pump(2.0 if h else 1.4)
        dq_sum[h].finish()
        value = nn(r.dq1[block], r.self_in[0]) + nn(r.dk1[block], r.self_in[1])
        r.part_c[block] = (value + nn(r.dv1[block], r.self_in[2])).astype(bf16)
        pump(0.4)
        marks["dn1", h] = pump.add(dn1_sum[h], range(dn1_sum[h].count), functools.partial(back_first, h), 0.3)

    def back_first(h, c):
        dn1_sum[h].take(c)
        block = strips[h][c]
        upstream = r.dn1[block].astype(f32)
        change, gain = back_normal(r.tokens[block].astype(f32), upstream, r.norm_gains[0:1])
        r.token_grad[block] = (change + r.x2[block]).astype(bf16)
        r.gain_sums[0] += by_eights(gain)
        r.bias_sums[0] += by_eights(upstream)

    def query_weight():
        own_columns(at, r.dq2, r.q1)
        for job in weight_grad(r.grads_3, 3 * own, r.n2, r.q1):
            job()
        total = jnp.sum(r.q1[...].astype(f32), axis=0, keepdims=True)
        r.in_bias_sums[2:3, 0:own] = total

    def squeeze(values):
        return jnp.sum(values, axis=0, keepdims=True)

    early = [Everyone(at, PLANE, 1, r.early_slots, r.e_0, r.e_1)]
    late = [Everyone(at, PLANE, 1, r.late_slots, r.l_0, r.l_1)]
    if n > PLANE:
        early.append(Everyone(at, n // PLANE, PLANE, r.early_slots_2, r.m_0, r.m_1))
        late.append(Everyone(at, n // PLANE, PLANE, r.late_slots_2, r.n_0, r.n_1))

    def finish_all(stages):
        total = stages[0].finish()
        for stage in stages[1:]:
            stage.slots[stage.place] = total
            stage.start()
            total = stage.finish()
        return total

    def early_vectors():
        r.in_bias_sums[1:2, 0:own] = squeeze(r.do1[...].astype(f32))
        total = squeeze(r.do2_sum[0] + r.do2_sum[1])
        for j in range(4):

            @pl.when(at.m == j)
            def _(j=j):
                r.in_bias_sums[3:4, 0:own] = total[:, j * own : (j + 1) * own]

        lines = [squeeze(r.gain_sums[k]) for k in (1, 2)] + [squeeze(r.bias_sums[k]) for k in (1, 2)]
        lines += [squeeze(r.out_sums[k]) for k in range(3)] + [squeeze(r.up_sum[0] + r.up_sum[1])]
        place = early[0].place
        r.early_slots[place, 0:8] = jnp.concatenate(lines, axis=0)
        r.early_slots[place, 8:16] = jnp.zeros((8, width), f32)
        for k in range(4):
            r.early_slots[place, 8:9, k * own : (k + 1) * own] = r.in_bias_sums[k : k + 1, 0:own]
        early[0].start()
        pump.later(8.0, 0.3, early_results)

    def early_results():
        total = finish_all(early)
        r.norm_gains_grad[1:3] = total[0:2]
        r.norm_biases_grad[1:3] = total[2:4]
        r.out_biases_grad[...] = total[4:7]
        r.up_bias_grad[...] = total[7:8]
        for k in range(4):
            r.in_biases_grad[k : k + 1] = total[8:9, k * own : (k + 1) * own]

    def result_2():
        total = scatter_2.finish()
        for j in range(4):
            for t in range(2):
                cols = slice(t * width + j * own, t * width + (j + 1) * own)
                r.plane_out[j, :, t * own : (t + 1) * own] = total[:, cols].astype(bf16)
        for k in (1, 2, 3):
            to_plane(k).start()
        pump.later(12.0, 0.3, result_2_end)

    def to_plane(k):
        to = lax.rem(at.m + k, 4)
        return remote(r.plane_out.at[to], r.plane_slots.at[at.m], r.d_0.at[k], r.d_1.at[at.m], at.line(to))

    def result_2_end():
        total = r.plane_out[at.m].astype(f32)
        for k in (1, 2, 3):
            o = lax.rem(at.m + k, 4)
            remote(r.plane_out.at[o], r.plane_slots.at[o], r.d_0.at[k], r.d_1.at[o], at.line(o)).wait_recv()
            total = total + r.plane_slots[o].astype(f32)
        for t in range(2):
            r.cross_in_grad[1 + t] = total[:, t * own : (t + 1) * own]
        for k in (1, 2, 3):
            to_plane(k).wait_send()

    def result_3():
        total = scatter_3.finish()
        for i in range(3):
            r.self_in_grad[i] = total[:, i * own : (i + 1) * own]
        r.cross_in_grad[0] = total[:, 3 * own : 4 * own]
        r.self_out_grad[...] = total[:, 4 * own : 5 * own].T
        r.cross_out_grad[...] = total[:, 5 * own : 6 * own].T

    run([functools.partial(cross_frames, r, g, j, frame_count) for g in range(groups) for j in range(2)], 1.0)
    while not done:
        pump.run_task()
    run([functools.partial(cross_weight, r.dk_t, 0), functools.partial(cross_weight, r.dv_t, width)], 0.8)
    launch(scatter_2, result_2)
    cross_out_grad()
    pump(0.6)
    back_second(first)
    run([functools.partial(frame_grads, clip) for clip in range(2)], 1.2)
    back_second(second)
    pump.until(marks["down", first])
    down_sum[first].finish()
    send_down(second)
    run([query_weight] + weight_grad(r.grads_3, 4 * own, r.low, r.o1), 0.4)
    jobs = weight_grad(r.grads_3, 0, r.n1, r.dq1) + weight_grad(r.grads_3, own, r.n1, r.dk1)
    run(jobs + weight_grad(r.grads_3, 2 * own, r.n1, r.dv1), 0.3)
    launch(scatter_3, result_3)
    early_vectors()
    pump.until(marks["dn1", second])
    for h in order:
        dn1_sum[h].finish()
    place = late[0].place
    r.late_slots[place] = jnp.zeros_like(r.late_slots[place])
    r.late_slots[place, 0:1] = squeeze(r.gain_sums[0])
    r.late_slots[place, 1:2] = squeeze(r.bias_sums[0])
    late[0].start()
    pump.until(marks["down", second])
    pump.flush()
    down_sum[second].finish()
    total = finish_all(late)
    r.norm_gains_grad[0:1] = total[0:1]
    r.norm_biases_grad[0:1] = total[1:2]


def layer(n, inputs):
    tokens, self_in = inputs["tokens"], inputs["self_in"]
    rows, width = tokens.shape
    own = self_in.shape[1]
    hidden = inputs["fc_up_in"].shape[1]
    groups = width // GROUP
    per = width // n
    S = jax.ShapeDtypeStruct
    outs = dict(
        layer_out=S((rows, width), bf16), token_grad=S((rows, width), bf16),
        encoder_grad=S(inputs["encoder"].shape, bf16), norm_gains_grad=S((3, width), f32),
        norm_biases_grad=S((3, width), f32), self_in_grad=S((3, per, own), f32), cross_in_grad=S((3, per, own), f32),
        in_biases_grad=S((4, own), f32), self_out_grad=S((own, per), f32), cross_out_grad=S((own, per), f32),
        out_biases_grad=S((3, width), f32), fc_up_grad=S((per, hidden), f32), up_bias_grad=S((1, hidden), f32),
        fc_down_grad=S((per, hidden), f32),
    )
    dma = pltpu.SemaphoreType.DMA
    low, full = pltpu.VMEM((rows, width), bf16), pltpu.VMEM((rows, width), f32)
    thin = pltpu.VMEM((rows, own), bf16)
    wide = pltpu.VMEM((rows, 2 * width), bf16)
    frame_pair = pltpu.VMEM((FRAMES, 2 * width), bf16)
    scratch = dict(
        fc_up=pltpu.VMEM((width, hidden), bf16), fc_down=pltpu.VMEM((hidden, width), bf16), cotangent=low,
        load=dma((8,)), big=pltpu.VMEM((5, width, width), bf16), bias=pltpu.VMEM((8, width), f32),
        bias_slots=pltpu.VMEM((4, 8, 256), f32), parts=pltpu.VMEM((2, 4, rows // 4, 2 * own), bf16),
        frames=pltpu.VMEM((2, FRAMES, width), bf16), n1=low, n2=low, n3=low, o2=low, dq2=low, dn3=low, down=low, part_a=low, part_b=low, part_c=low, ends=low,
        other_b=low, ends_b=pltpu.VMEM((rows // 2, width), bf16), other_a=low,
        other_c=pltpu.VMEM((rows // 2, width), bf16), x2=full, x3=full, g3=full, dn2=pltpu.VMEM((rows // 2, width), f32), q1=thin, k1=thin, v1=thin, o1=thin, do1=thin, dq1=thin,
        dk1=thin, dv1=thin, lse1=pltpu.VMEM((rows, 8), f32), q_pair=wide, do_pair=wide,
        k_pair=frame_pair, v_pair=frame_pair, stats=pltpu.VMEM((groups, rows, PAIR), f32),
        **{f"lse_{name}": pltpu.VMEM((2, groups, 8, rows // 2), f32) for name in ("own", "end", "mid", "far", "all")}, dk_t=pltpu.VMEM((2, width, FRAMES), bf16),
        dv_t=pltpu.VMEM((2, width, FRAMES), bf16), dk_sum=pltpu.VMEM((own, rows), f32),
        dv_sum=pltpu.VMEM((own, rows), f32), gain_sums=pltpu.VMEM((3, 8, width), f32),
        bias_sums=pltpu.VMEM((3, 8, width), f32), out_sums=pltpu.VMEM((3, 8, width), f32),
        up_sum=pltpu.VMEM((2, 8, hidden), f32), do2_sum=pltpu.VMEM((2, 8, width), f32),
        in_bias_sums=pltpu.VMEM((8, 256), f32), early_slots=pltpu.VMEM((PLANE, 16, width), f32),
        late_slots=pltpu.VMEM((PLANE, 8, width), f32), plane_out=pltpu.VMEM((4, per, 2 * own), bf16),
        plane_slots=pltpu.VMEM((4, per, 2 * own), bf16), grads_1=pltpu.VMEM((n, per, 2 * width), bf16),
        grads_3=pltpu.VMEM((n, per, 6 * own), bf16),
    )
    group_dma = Total.semaphores(groups)
    part_dma = [dma((2, 5)), dma((2, 4))]
    tiles, strips = Total.semaphores(2 * groups), Total.semaphores(rows // 128)
    for letter, group in (
        ("g", Gather.semaphores()), ("h", Gather.semaphores()), ("b", Direct.semaphores()), ("p", part_dma), ("s", group_dma),
        ("t", tiles), ("u", strips), ("v", strips), ("q", tiles), ("z", strips), ("e", Everyone.semaphores(PLANE)), ("l", Everyone.semaphores(PLANE)),
        ("d", Direct.semaphores()),
    ):
        for i, one in enumerate(group):
            scratch[f"{letter}_{i}"] = one
    if n > PLANE:
        scratch["early_slots_2"] = pltpu.VMEM((n // PLANE, 16, width), f32)
        scratch["late_slots_2"] = pltpu.VMEM((n // PLANE, 8, width), f32)
        for letter in ("m", "n"):
            for i, one in enumerate(Everyone.semaphores(n // PLANE)):
                scratch[f"{letter}_{i}"] = one
    for k, letter, cols in ((1, "x", 2 * width), (2, "y", 2 * width), (3, "w", 6 * own)):
        came, slots, *semaphores = Scatter.buffers(n, per, cols)
        scratch[f"came_{k}"], scratch[f"slots_{k}"] = came, slots
        for i, one in enumerate(semaphores):
            scratch[f"{letter}_{i}"] = one
    names = list(inputs) + list(outs) + list(scratch)
    late = ("fc_up_in", "fc_down_in", "cotangent_in", "cross_in", "cross_out")
    result = pl.pallas_call(
        functools.partial(layer_kernel, names, n),
        out_shape=list(outs.values()),
        in_specs=[SMEM if name == "lengths" else ANY if name in late else VMEM for name in inputs],
        out_specs=[VMEM] * len(outs),
        scratch_shapes=list(scratch.values()),
        compiler_params=pltpu.CompilerParams(
            collective_id=1, has_side_effects=True, vmem_limit_bytes=127 * 2**19
        ),
        name="layer",
    )(*inputs.values())
    return dict(zip(outs, result))


def results_kernel(*refs):
    half = len(refs) // 2
    for source, target in zip(refs[:half], refs[half:]):
        target[...] = source[...].reshape(target.shape)


def results(values):
    shapes = [value.shape if value.shape[0] > 1 else value.shape[1:] for value in values]
    return pl.pallas_call(
        results_kernel,
        out_shape=[jax.ShapeDtypeStruct(shape, value.dtype) for shape, value in zip(shapes, values)],
        in_specs=[VMEM] * len(values),
        out_specs=[VMEM] * len(values),
        compiler_params=pltpu.CompilerParams(vmem_limit_bytes=127 * 2**19),
        name="results",
    )(*values)


def shards(
    n, tokens, encoder, lengths, norm_gains, norm_biases, self_in, cross_in, in_biases, self_out, cross_out,
    out_biases, fc_up, up_bias, fc_down, cotangent,
):
    outs = layer(
        n,
        dict(
            tokens=tokens, encoder=encoder.transpose(1, 0, 2), lengths=lengths, norm_gains=norm_gains, norm_biases=norm_biases,
            self_in=self_in.transpose(0, 2, 1),
            cross_in=cross_in.transpose(0, 2, 1), in_biases=in_biases, self_out=self_out, cross_out=cross_out,
            out_biases=out_biases, up_bias=up_bias, fc_up_in=fc_up, fc_down_in=fc_down,
            cotangent_in=cotangent,
        ),
    )
    outs = dict(zip(outs, results(list(outs.values()))))
    outs["encoder_grad"] = outs["encoder_grad"].transpose(1, 0, 2)
    outs["fc_down_grad"] = outs["fc_down_grad"].T
    return tuple(outs.values())


def solution(mesh):
    in_specs = (
        P("dp", None), P("dp", "mp", None), P("dp", None), P(), P(), P(None, None, "mp"), P(None, None, "mp"),
        P(None, "mp"), P("mp", None), P("mp", None), P(), P(None, "mp"), P("mp"), P("mp", None), P("dp", None),
    )
    out_specs = (
        P("dp", None), P("dp", None), P("dp", "mp", None), P(), P(), P(None, "dp", "mp"), P(None, "dp", "mp"),
        P(None, "mp"), P("mp", "dp"), P("mp", "dp"), P(), P("dp", "mp"), P("mp"), P("mp", "dp"),
    )
    body = functools.partial(shards, mesh.shape["dp"])
    return jax.shard_map(body, mesh=mesh, in_specs=in_specs, out_specs=out_specs, check_vma=False)
```

```python
import functools
import types

import jax
import jax.numpy as jnp
from jax import lax
from jax.experimental import pallas as pl
from jax.experimental.pallas import tpu as pltpu
from jax.sharding import PartitionSpec as P

HEAD = 64
PAIR = 2 * HEAD
PLANE = 8
FRAMES = 384
epsilon = 1e-05
factor = 0.125
masked_value = -1e30
f32 = jnp.float32
bf16 = jnp.bfloat16
MESH = pl.DeviceIdType.MESH
VMEM = pl.BlockSpec(memory_space=pltpu.VMEM)
SMEM = pl.BlockSpec(memory_space=pltpu.SMEM)
ANY = pl.BlockSpec(memory_space=pl.ANY)


def nn(a, b):
    return jnp.dot(a, b, preferred_element_type=f32)


def nt(a, b):
    return lax.dot_general(a, b, (((1,), (1,)), ((), ())), preferred_element_type=f32)


def tn(a, b):
    return lax.dot_general(a, b, (((0,), (0,)), ((), ())), preferred_element_type=f32)


def flip(index, bit):
    return index + bit - 2 * bit * lax.rem(index // bit, 2)


def remote(src, dst, send, recv, device):
    return pltpu.make_async_remote_copy(
        src_ref=src, dst_ref=dst, send_sem=send, recv_sem=recv, device_id=device, device_id_type=MESH
    )


def greet(devices):
    barrier = pltpu.get_barrier_semaphore()
    for device in devices:
        pl.semaphore_signal(barrier, inc=1, device_id=device, device_id_type=MESH)


def await_greetings(count):
    pl.semaphore_wait(pltpu.get_barrier_semaphore(), count)


def pair_sum(left, right):
    return (left.astype(f32) + right.astype(f32)).astype(bf16)


class Place:
    def __init__(self):
        self.d, self.m = d, m = lax.axis_index("dp"), lax.axis_index("mp")
        self.mine = lax.rem(d, PLANE)
        self.base = d - self.mine
        self.half = m // 2
        self.rank = m + self.half * (3 - 2 * m)
        self.edge, self.inner = self.rank == 0, self.rank == 1
        self.near = flip(m, 1)
        self.peer = 3 - m

    def origin(self, j):
        index = 1 - self.rank if j == 0 else j + 1
        return index + self.half * (3 - 2 * index)

    def line(self, m):
        return (self.d, m)

    def plane(self, s):
        return (self.base + s, self.m)

    def way(self, k):
        s = self.mine
        for bit in (1, 2, 4):
            if k & bit:
                s = flip(s, bit)
        return s


class Gather:
    def __init__(self, at, big, own, cuts, line_send, side_send, corner_send, core_send, recv, core_recv):
        self.at, self.big, self.own, self.cuts = at, big, own, cuts
        self.line_send, self.side_send, self.corner_send = line_send, side_send, corner_send
        self.core_send, self.recv, self.core_recv = core_send, recv, core_recv
        self.core, self.chip = lax.rem(at.mine, 2), at.mine // 2
        self.pieces = range(cuts)

    def copy(self, o, chip, i, send, device):
        block = self.block(o, chip, i)
        return remote(block, block, send, self.recv.at[o, chip, i], device)

    def came(self, o, chip, i):
        self.copy(o, chip, i, self.line_send, self.at.line(self.at.m)).wait_recv()

    def start(self):
        at = self.at
        for i in self.pieces:
            self.copy(at.m, self.chip, i, self.line_send, at.line(at.near)).start()

            @pl.when(at.inner)
            def _(i=i):
                self.copy(at.m, self.chip, i, self.line_send, at.line(at.peer)).start()

    def from_line(self, j):
        at = self.at
        o = at.origin(j)
        for i in self.pieces:
            self.came(o, self.chip, i)

            @pl.when(at.inner)
            def _(i=i):
                to = at.peer if j == 0 else at.near
                self.copy(o, self.chip, i, self.line_send, at.line(to)).start()

            for k in (2, 4):
                self.copy(o, self.chip, i, self.side_send, at.plane(at.way(k))).start()

    def passed_on(self):
        return ((2, 0), (4, 1))[: self.cuts]

    def from_sides(self, j):
        at = self.at
        o = at.origin(j)
        for k, i in self.passed_on():
            chip = flip(self.chip, k // 2)
            self.came(o, chip, i)
            self.copy(o, chip, i, self.corner_send, at.plane(at.way(6 - k))).start()

    def core_copy(self, j, mine):
        block = self.core_block(self.at.origin(j), self.core if mine else 1 - self.core)
        return remote(block, block, self.core_send.at[j], self.core_recv.at[j], self.at.plane(self.at.way(1)))

    def from_corner(self, j):
        o = self.at.origin(j)
        for k in (2, 4):
            for i in self.pieces:
                if (k, i) not in self.passed_on():
                    self.came(o, flip(self.chip, k // 2), i)
        for i in self.pieces:
            self.came(o, flip(flip(self.chip, 1), 2), i)
        self.core_copy(j, True).start()

    def from_core(self, j):
        self.core_copy(j, False).wait_recv()

    def sent(self, slices, send):
        block = self.slices(slices)
        remote(block, block, send, self.core_recv.at[0], self.at.line(self.at.near)).wait_send()

    def finish(self):
        at = self.at

        @pl.when(at.edge)
        def _():
            self.sent(1, self.line_send)

        @pl.when(at.inner)
        def _():
            self.sent(5, self.line_send)

        self.sent(6, self.side_send)
        self.sent(3, self.corner_send)
        for j in range(3):
            self.core_copy(j, True).wait_send()

    @staticmethod
    def semaphores():
        dma = pltpu.SemaphoreType.DMA
        return [dma, dma, dma, dma((3,)), dma((4, 4, 2)), dma((3,))]


class GatherFour(Gather):
    def block(self, o, chip, i):
        row = o * self.own + lax.rem(chip, 2) * (self.own // 2) + i * (self.own // 4)
        return self.big.at[2 * self.core + chip // 2, pl.ds(pl.multiple_of(row, 16), self.own // 4)]

    def core_block(self, o, core):
        return self.big.at[pl.ds(2 * core, 2), pl.ds(pl.multiple_of(o * self.own, 16), self.own)]

    def slices(self, count):
        return self.big.at[0, pl.ds(0, count * self.own // 2)]


class GatherLast(Gather):
    def columns(self, core):
        half = self.big.shape[2] // 2
        return pl.ds(pl.multiple_of(core * half, PAIR), half)

    def block(self, o, chip, i):
        row = pl.multiple_of(o * self.own + chip * (self.own // 4), 16)
        return self.big.at[4, pl.ds(row, self.own // 4), self.columns(self.core)]

    def core_block(self, o, core):
        return self.big.at[4, pl.ds(pl.multiple_of(o * self.own, 16), self.own), self.columns(core)]

    def slices(self, count):
        return self.big.at[4, pl.ds(0, count * self.own // 4), pl.ds(0, self.big.shape[2] // 2)]


class Parts:
    def __init__(self, at, slots, send, recv):
        self.at, self.slots, self.send, self.recv = at, slots, send, recv

    def copy(self, o, send, to):
        return remote(self.slots.at[o], self.slots.at[o], send, self.recv.at[o], self.at.line(to))

    def own(self, to_peer):
        at = self.at
        return self.copy(at.m, self.send.at[to_peer], at.peer if to_peer else at.near)

    def forward(self, j):
        at = self.at
        return self.copy(at.origin(j), self.send.at[2 + j], at.peer if j == 0 else at.near)

    def start_edge(self):
        @pl.when(self.at.edge)
        def _():
            self.own(0).start()

    def start_inner(self):
        @pl.when(self.at.inner)
        def _():
            self.own(0).start()
            self.own(1).start()

    def came(self, j):
        self.copy(self.at.origin(j), self.send.at[0], self.at.m).wait_recv()

    def relay(self, j):
        @pl.when(self.at.inner)
        def _():
            self.came(j)
            self.forward(j).start()

    def take(self):
        @pl.when(self.at.edge)
        def _():
            for j in range(3):
                self.came(j)

    def finish(self):
        self.own(0).wait_send()

        @pl.when(self.at.inner)
        def _():
            self.own(1).wait_send()
            for j in range(3):
                self.forward(j).wait_send()

    @staticmethod
    def semaphores():
        dma = pltpu.SemaphoreType.DMA
        return [dma((5,)), dma((4,))]


class Direct:
    def __init__(self, at, slots, send, recv):
        self.at, self.slots, self.send, self.recv = at, slots, send, recv

    def copy(self, o, k):
        to = lax.rem(self.at.m + k, 4)
        return remote(self.slots.at[o], self.slots.at[o], self.send.at[k], self.recv.at[o], self.at.line(to))

    def start(self):
        for k in (1, 2, 3):
            self.copy(self.at.m, k).start()

    def finish(self):
        for k in (1, 2, 3):
            self.copy(lax.rem(self.at.m + k, 4), k).wait_recv()
        for k in (1, 2, 3):
            self.copy(self.at.m, k).wait_send()

    @staticmethod
    def semaphores():
        dma = pltpu.SemaphoreType.DMA
        return [dma((4,)), dma((4,))]


class Everyone:
    def __init__(self, at, size, stride, slots, send, recv):
        self.at, self.size, self.stride, self.slots, self.send, self.recv = at, size, stride, slots, send, recv
        self.place = lax.rem(at.d // stride, size)

    def copy(self, o, k):
        to = self.at.d + (lax.rem(self.place + k, self.size) - self.place) * self.stride
        return remote(
            self.slots.at[o], self.slots.at[o], self.send.at[k], self.recv.at[o], (to, self.at.m)
        )

    def start(self):
        for k in range(1, self.size):
            self.copy(self.place, k).start()

    def finish(self):
        for k in range(1, self.size):
            self.copy(lax.rem(self.place + k, self.size), k).wait_recv()
        for k in range(1, self.size):
            self.copy(self.place, k).wait_send()
        total = self.slots[0]
        for o in range(1, self.size):
            total = total + self.slots[o]
        return total

    @staticmethod
    def semaphores(size):
        dma = pltpu.SemaphoreType.DMA
        return [dma((size,)), dma((size,))]


class Scatter:
    def __init__(self, at, n, x, came, slots, s1, r1, s2, r2):
        self.at, self.x, self.came, self.slots = at, x, came, slots
        self.s1, self.r1, self.s2, self.r2 = s1, r1, s2, r2
        self.core, self.chip, self.chips = lax.rem(at.d, 2), at.d // 2, n // 2
        self.order = list(range(1, self.chips)) + [0]

    def to_sibling(self, k):
        c = lax.rem(self.chip + k, self.chips)
        other = 1 - self.core
        return remote(
            self.x.at[2 * c + other], self.came.at[c], self.s1.at[c], self.r1.at[c],
            (2 * self.chip + other, self.at.m),
        )

    def between(self, k, slot):
        c = lax.rem(self.chip + k, self.chips)
        return remote(
            self.x.at[2 * c + self.core], self.slots.at[slot], self.s2.at[c], self.r2.at[slot],
            (2 * c + self.core, self.at.m),
        )

    def start(self):
        for k in self.order:
            self.to_sibling(k).start()

    def fold(self):
        for k in self.order:
            c = lax.rem(self.chip + k, self.chips)
            self.to_sibling(k).wait_recv()
            block = 2 * c + self.core
            self.x[block] = pair_sum(self.x[block], self.came[c])
            if k:
                self.between(k, self.chip).start()

    def finish(self):
        total = self.x[2 * self.chip + self.core].astype(f32)
        for k in range(1, self.chips):
            c = lax.rem(self.chip + k, self.chips)
            self.between(k, c).wait_recv()
            total = total + self.slots[c].astype(f32)
        for k in self.order:
            self.to_sibling(k).wait_send()
        for k in range(1, self.chips):
            self.between(k, self.chip).wait_send()
        return total

    @staticmethod
    def buffers(n, rows, cols):
        half = pltpu.VMEM((n // 2, rows, cols), bf16)
        dma = pltpu.SemaphoreType.DMA((n // 2,))
        return [half, half, dma, dma, dma, dma]


class Total:
    def __init__(self, at, whole, blocks, x, ends, other, out, sa, ra, sb, rb, sr, rr, rooms=None):
        self.at, self.whole, self.blocks, self.rooms = at, whole, blocks, rooms or blocks
        self.x, self.ends, self.other, self.out = x, ends, other, out
        self.sa, self.ra, self.sb, self.rb, self.sr, self.rr = sa, ra, sb, rb, sr, rr
        self.count = len(blocks)
        self.size = whole.size * x.shape[1] * 2 / self.count

    def inward(self, c):
        room = self.ends.at[self.rooms[c]]
        return remote(self.x.at[self.blocks[c]], room, self.sa, self.ra.at[c], self.at.line(self.at.near))

    def across(self, c):
        room = self.other.at[self.rooms[c]]
        return remote(self.x.at[self.blocks[c]], room, self.sb, self.rb.at[c], self.at.line(self.at.peer))

    def outward(self, c):
        block = self.out.at[self.blocks[c]]
        return remote(block, block, self.sr, self.rr.at[c], self.at.line(self.at.near))

    def send(self, c):
        @pl.when(self.at.edge)
        def _():
            self.inward(c).start()

    def fold(self, c):
        @pl.when(self.at.inner)
        def _():
            b = self.blocks[c]
            self.inward(c).wait_recv()
            self.x[b] = pair_sum(self.x[b], self.ends[self.rooms[c]])
            self.across(c).start()

    def close(self, c):
        @pl.when(self.at.inner)
        def _():
            b = self.blocks[c]
            self.across(c).wait_recv()
            self.out[b] = pair_sum(self.x[b], self.other[self.rooms[c]])
            self.outward(c).start()

    def take(self, c):
        @pl.when(self.at.edge)
        def _():
            self.outward(c).wait_recv()

    def sent(self, source, send):
        block = source.at[self.whole]
        remote(block, block, send, self.ra.at[0], self.at.line(self.at.near)).wait_send()

    def finish(self):
        @pl.when(self.at.edge)
        def _():
            self.sent(self.x, self.sa)

        @pl.when(self.at.inner)
        def _():
            self.sent(self.x, self.sb)
            self.sent(self.out, self.sr)

    @staticmethod
    def semaphores(count):
        dma = pltpu.SemaphoreType.DMA
        return [dma((2,)), dma((2, count))] * 3


class SoftTotal:
    def __init__(self, at, r, h, block, blocks, sums, letter, groups):
        self.at, self.r, self.h, self.block, self.sums = at, r, h, block, sums
        self.semaphores = [getattr(r, f"{letter}_{i}").at[h] for i in range(6)]
        self.blocks, self.groups = blocks, groups
        self.count = len(blocks)
        self.each = self.count // groups
        self.size = sums.size

    def small(self, kind, source, target, g, to):
        send, recv = self.semaphores[2 * kind], self.semaphores[2 * kind + 1]
        return remote(source.at[self.h, g], target.at[self.h, g], send, recv.at[g], self.at.line(to))

    def small_sent(self, kind, source):
        whole = source.at[self.h]
        send, recv = self.semaphores[2 * kind], self.semaphores[2 * kind + 1]
        remote(whole, whole, send, recv.at[0], self.at.line(self.at.near)).wait_send()

    def inward(self, g):
        return self.small(0, self.r.lse_own, self.r.lse_end, g, self.at.near)

    def across(self, g):
        return self.small(1, self.r.lse_mid, self.r.lse_far, g, self.at.peer)

    def outward(self, g):
        return self.small(2, self.r.lse_all, self.r.lse_all, g, self.at.near)

    def spread(self, tables, rows, tile):
        low = iota((rows.size, PAIR), 1) < HEAD
        return jnp.where(low, tables[:, 2 * tile : 2 * tile + 1], tables[:, 2 * tile + 1 : 2 * tile + 2])

    def columns(self, *tables):
        spare = jnp.zeros((PAIR - 8 * len(tables), self.block.size), f32)
        return jnp.concatenate([*tables, spare], axis=0).T

    def merge(self, left, right):
        top = jnp.maximum(left, right)
        total = top + jnp.log(jnp.exp(left - top) + jnp.exp(right - top))
        return total, jnp.exp(left - total), jnp.exp(right - total)

    def send(self, c):
        g = c // self.each

        @pl.when(self.at.edge)
        def _():
            if c % self.each == 0:
                self.inward(g).start()
            rows, cols = self.blocks[c]
            self.r.part_a[rows, cols] = self.r.g3[rows, cols].astype(bf16)

        self.sums.send(c)

    def fold(self, c):
        r, sums, g = self.r, self.sums, c // self.each

        @pl.when(self.at.inner)
        def _():
            if c % self.each == 0:
                self.inward(g).wait_recv()
                total, own, end = self.merge(r.lse_own[self.h, g], r.lse_end[self.h, g])
                r.lse_mid[self.h, g] = total
                self.across(g).start()
                r.stats[g, self.block] = self.columns(own, end)
            sums.inward(c).wait_recv()
            rows, cols = self.blocks[c]
            table = r.stats[g, rows]
            for t in range(2):
                tile = pl.ds(cols.start + t * PAIR, PAIR)
                value = r.g3[rows, tile] * self.spread(table, rows, t)
                value = value + r.ends[rows, tile].astype(f32) * self.spread(table[:, 8:], rows, t)
                r.part_a[rows, tile] = value.astype(bf16)
            sums.across(c).start()

    def close(self, c):
        r, sums, g, at = self.r, self.sums, c // self.each, self.at

        @pl.when(at.inner)
        def _():
            lower = at.half == 0
            if c % self.each == 0:
                self.across(g).wait_recv()
                mid, far = r.lse_mid[self.h, g], r.lse_far[self.h, g]
                total, left, right = self.merge(jnp.where(lower, mid, far), jnp.where(lower, far, mid))
                r.lse_all[self.h, g] = total
                self.outward(g).start()
                r.stats[g, self.block] = self.columns(total, left, right)
            sums.across(c).wait_recv()
            rows, cols = self.blocks[c]
            table = r.stats[g, rows]
            for t in range(2):
                tile = pl.ds(cols.start + t * PAIR, PAIR)
                mid, far = r.part_a[rows, tile].astype(f32), r.other_a[rows, tile].astype(f32)
                left, right = jnp.where(lower, mid, far), jnp.where(lower, far, mid)
                value = left * self.spread(table[:, 8:], rows, t) + right * self.spread(table[:, 16:], rows, t)
                r.o2[rows, tile] = value.astype(bf16)
            sums.outward(c).start()

    def take(self, c):
        g = c // self.each
        self.sums.take(c)
        if c % self.each == 0:

            @pl.when(self.at.edge)
            def _():
                self.outward(g).wait_recv()
                self.r.stats[g, self.block] = self.columns(self.r.lse_all[self.h, g])

    def finish(self):
        self.sums.finish()

        @pl.when(self.at.edge)
        def _():
            self.small_sent(0, self.r.lse_own)

        @pl.when(self.at.inner)
        def _():
            self.small_sent(1, self.r.lse_mid)
            self.small_sent(2, self.r.lse_all)


def normal(values):
    average = jnp.mean(values, axis=-1, keepdims=True)
    centred = values - average
    variance = jnp.mean(centred * centred, axis=-1, keepdims=True)
    scale = lax.rsqrt(variance + epsilon)
    return centred * scale, scale


def row_blocks(count, size, body):
    def step(i, carry):
        body(pl.ds(pl.multiple_of(i * size, size), size))
        return carry

    lax.fori_loop(0, count // size, step, 0)


def iota(shape, axis):
    return lax.broadcasted_iota(jnp.int32, shape, axis)


def pair_tiles(tile):
    turned = pltpu.roll(tile, HEAD, axis=1)
    low = iota(tile.shape, 1) < HEAD
    return jnp.where(low, tile, turned), jnp.where(low, turned, tile)


def back_normal(values, upstream, gain):
    xhat, scale = normal(values)
    scaled = upstream * gain
    first = jnp.mean(scaled, axis=-1, keepdims=True)
    second = jnp.mean(scaled * xhat, axis=-1, keepdims=True)
    return scale * (scaled - first - xhat * second), upstream * xhat


def by_eights(values):
    return jnp.sum(values.reshape(-1, 8, values.shape[1]), axis=0)


def own_columns(at, source, target):
    width = target.shape[1]
    for j in range(4):

        @pl.when(at.m == j)
        def _(j=j):
            target[...] = source[:, j * width : (j + 1) * width]


def self_mask(rows, keys, start, clip_start):
    row = iota((rows, keys), 0) + start
    col = iota((rows, keys), 1)
    return jnp.logical_and(col <= row, (row >= clip_start) == (col >= clip_start))


def self_projections(r):
    rows = r.tokens.shape[0]

    def normed(block):
        xhat, _ = normal(r.tokens[block].astype(f32))
        r.n1[block] = (xhat * r.norm_gains[0:1] + r.norm_biases[0:1]).astype(bf16)

    row_blocks(rows, 64, normed)
    r.q1[...] = (nt(r.n1[...], r.self_in[0]) + r.in_biases[0:1]).astype(bf16)
    r.k1[...] = nt(r.n1[...], r.self_in[1]).astype(bf16)
    r.v1[...] = (nt(r.n1[...], r.self_in[2]) + r.in_biases[1:2]).astype(bf16)


def self_forward(r, part, clip_start):
    half = r.tokens.shape[0] // 2
    block, keys = pl.ds(part * half, half), (part + 1) * half
    allowed = self_mask(half, keys, part * half, clip_start)
    for h in range(r.q1.shape[1] // HEAD):
        cols = pl.ds(h * HEAD, HEAD)
        scores = nt(r.q1[block, cols] * bf16(factor), r.k1[0:keys, cols])
        scores = jnp.where(allowed, scores, masked_value)
        top = jnp.max(scores, axis=1, keepdims=True)
        power = jnp.exp(scores - top)
        total = jnp.sum(power, axis=1, keepdims=True)
        chance = (power * (1 / total)).astype(bf16)
        r.o1[block, cols] = nn(chance, r.v1[0:keys, cols]).astype(bf16)
        r.lse1[block, pl.ds(h, 1)] = top + jnp.log(total)


def self_backward(r, part, clip_start):
    half = r.tokens.shape[0] // 2
    block, keys = pl.ds(part * half, half), (part + 1) * half
    allowed = self_mask(half, keys, part * half, clip_start)
    for h in range(r.q1.shape[1] // HEAD):
        cols = pl.ds(h * HEAD, HEAD)
        query, upstream = r.q1[block, cols] * bf16(factor), r.do1[block, cols]
        scores = jnp.where(allowed, nt(query, r.k1[0:keys, cols]), masked_value)
        chance = jnp.exp(scores - r.lse1[block, pl.ds(h, 1)])
        slope = nt(upstream, r.v1[0:keys, cols])
        inner = jnp.sum(chance * slope, axis=1, keepdims=True)
        change = (chance * (slope - inner)).astype(bf16)
        query_grad = nn(change, r.k1[0:keys, cols]) * factor
        r.dq1[block, cols] = query_grad.astype(bf16)
        bias = jnp.sum(query_grad, axis=0, keepdims=True)
        key_grad, value_grad = tn(query, change), tn(upstream, chance.astype(bf16))
        if part:
            r.in_bias_sums[0:1, cols] = bias
            r.dk_sum[cols, :] = key_grad
            r.dv_sum[cols, :] = value_grad
        else:
            r.in_bias_sums[0:1, cols] += bias
            r.dk_sum[cols, 0:keys] += key_grad
            r.dv_sum[cols, 0:keys] += value_grad
    r.dk1[block] = r.dk_sum[:, block].T.astype(bf16)
    r.dv1[block] = r.dv_sum[:, block].T.astype(bf16)


def keys_and_values(r, matrix, bias, pairs):
    both = [nt(r.frames[clip], r.big[matrix]) for clip in range(2)]
    if bias is not None:
        both = [value + r.bias[bias : bias + 1] for value in both]
    for t in range(both[0].shape[1] // PAIR):
        first, second = (value[:, t * PAIR : (t + 1) * PAIR] for value in both)
        low = iota(first.shape, 1) < HEAD
        turned_first, turned_second = pltpu.roll(first, HEAD, axis=1), pltpu.roll(second, HEAD, axis=1)
        pairs[:, 2 * t * PAIR : (2 * t + 1) * PAIR] = jnp.where(low, first, turned_second).astype(bf16)
        pairs[:, (2 * t + 1) * PAIR : (2 * t + 2) * PAIR] = jnp.where(low, turned_first, second).astype(bf16)


def to_pairs(value, pairs, block, clip_start, scale):
    rows = value.shape[0]
    keep = (iota((rows, PAIR), 1) < HEAD) == (iota((rows, PAIR), 0) + block.start < clip_start)
    for t in range(value.shape[1] // PAIR):
        for e, tile in enumerate(pair_tiles(value[:, t * PAIR : (t + 1) * PAIR])):
            at = (2 * t + e) * PAIR
            pairs[block, at : at + PAIR] = (jnp.where(keep, tile, 0.0) * scale).astype(bf16)


def from_pair(even, odd, first):
    low = iota(even.shape, 1) < HEAD
    even = jnp.where(first, even, pltpu.roll(even, HEAD, axis=1))
    odd = jnp.where(first, pltpu.roll(odd, HEAD, axis=1), odd)
    return jnp.where(low, even, odd)


GROUP = 2 * PAIR
GROUP_HEADS = 4


def of_clip(block, clip_start):
    return iota((block.size, PAIR), 0) + block.start < clip_start


def real_frames(rows, frame_count):
    return iota((rows, FRAMES), 1) < frame_count


def cross_forward(r, block, g, j, clip_start, frame_count):
    lane = iota((block.size, PAIR), 1)
    first = of_clip(block, clip_start)
    valid = real_frames(block.size, frame_count)
    halves = []
    stats = jnp.zeros((block.size, PAIR), f32) if j == 0 else r.stats[g, block]
    for e in (0, 1):
        cols = pl.ds(2 * GROUP * g + 2 * PAIR * j + PAIR * e, PAIR)
        scores = jnp.where(valid, nt(r.q_pair[block, cols], r.k_pair[:, cols]), masked_value)
        top = jnp.max(scores, axis=1, keepdims=True)
        power = jnp.exp(scores - top)
        total = jnp.sum(power, axis=1, keepdims=True)
        halves.append(nn(power.astype(bf16), r.v_pair[:, cols]) * (1 / total))
        stats = jnp.where(lane == 2 * j + e, top + jnp.log(total), stats)
    r.stats[g, block] = stats
    r.g3[block, pl.ds(GROUP * g + PAIR * j, PAIR)] = from_pair(*halves, first)


def cross_slopes(r, block, cols, lane, stats, index, valid):
    def column(i):
        return jnp.sum(jnp.where(lane == i, stats, 0.0), axis=1, keepdims=True)

    scores = jnp.where(valid, nt(r.q_pair[block, cols], r.k_pair[:, cols]), masked_value)
    chance = jnp.exp(scores - column(index))
    slope = nt(r.do_pair[block, cols], r.v_pair[:, cols])
    return chance, (chance * (slope - column(16 + index))).astype(bf16)


def cross_queries(r, block, g, j, clip_start, frame_count):
    lane = iota((block.size, PAIR), 1)
    first = of_clip(block, clip_start)
    valid = real_frames(block.size, frame_count)
    stats = r.stats[g, block]
    halves = []
    for e in (0, 1):
        cols = pl.ds(2 * GROUP * g + 2 * PAIR * j + PAIR * e, PAIR)
        _, change = cross_slopes(r, block, cols, lane, stats, 2 * j + e, valid)
        halves.append(nn(change, r.k_pair[:, cols]) * factor)
    r.part_a[block, pl.ds(GROUP * g + PAIR * j, PAIR)] = from_pair(*halves, first).astype(bf16)


def cross_frames(r, g, j, frame_count):
    rows = r.q_pair.shape[0]
    block = pl.ds(0, rows)
    lane = iota((rows, PAIR), 1)
    valid = real_frames(rows, frame_count)
    for e in (0, 1):
        cols = pl.ds(2 * GROUP * g + 2 * PAIR * j + PAIR * e, PAIR)
        chance, change = cross_slopes(r, block, cols, lane, r.stats[g], 2 * j + e, valid)
        value_grad = tn(r.do_pair[:, cols], chance.astype(bf16)).astype(bf16)
        key_grad = tn(r.q_pair[:, cols], change).astype(bf16)
        head = pl.ds(GROUP * g + PAIR * j + HEAD * e, HEAD)
        for clip in range(2):
            r.dv_t[clip, head] = value_grad[clip * HEAD : (clip + 1) * HEAD]
            r.dk_t[clip, head] = key_grad[clip * HEAD : (clip + 1) * HEAD]


def put_blocks(x, column, first_row, value):
    per = x.shape[1]
    for i in range(value.shape[0] // per):
        x[first_row // per + i, :, column : column + value.shape[1]] = value[i * per : (i + 1) * per].astype(bf16)


def weight_grad(x, column, left, right):
    part = left.shape[1] // 2
    return [
        functools.partial(
            lambda i: put_blocks(x, column, i * part, tn(left[:, i * part : (i + 1) * part], right[...])), i
        )
        for i in range(2)
    ]


class Pump:
    latency, rate, step, issue = 1.8, 47.0e3, 0.2, 0.1

    def __init__(self):
        self.blocks, self.folded, self.closed, self.tasks = [], 0, 0, []
        self.edge, self.inner = 0.0, 0.0
        self.free = dict(inward=0.0, across=0.0, outward=0.0)

    def travel(self, link, block, start):
        self.free[link] = max(self.free[link], start) + block["bytes"] / self.rate
        return self.free[link] + self.latency

    def add(self, total, chosen, after=None, after_time=0.0):
        for c in chosen:
            total.send(c)
            self.edge += self.issue
            block = dict(total=total, c=c, after=after, time=after_time, bytes=total.size)
            block["came"] = self.travel("inward", block, self.edge)
            self.blocks.append(block)
        return len(self.blocks)

    def fold(self):
        block = self.blocks[self.folded]
        block["total"].fold(block["c"])
        self.inner = max(self.inner, block["came"]) + self.step
        block["crossed"] = self.travel("across", block, self.inner)
        self.folded += 1

    def close(self):
        block = self.blocks[self.closed]
        block["total"].close(block["c"])
        self.inner = max(self.inner, block["crossed"]) + self.step
        block["back"] = self.travel("outward", block, self.inner)
        self.closed += 1
        if block["after"] is not None:
            block["after"](block["c"])
            self.inner += block["time"]
            self.edge = max(self.edge, block["back"]) + block["time"]

    def next_step(self):
        steps = []
        if self.closed < self.folded:
            steps.append((self.blocks[self.closed]["crossed"], self.close))
        if self.folded < len(self.blocks):
            steps.append((self.blocks[self.folded]["came"], self.fold))
        if self.tasks:
            steps.append((self.tasks[0][0], self.run_task))
        return min(steps, key=lambda step: step[0], default=(float("inf"), None))

    def __call__(self, spent):
        self.edge += spent
        self.inner += spent
        while True:
            time, step = self.next_step()
            if time > self.inner:
                return
            step()

    def until(self, mark):
        while self.closed < mark:
            self.next_step()[1]()

    def now(self):
        return max(self.edge, self.inner)

    def later(self, wait, spent, task):
        self.tasks.append((self.now() + wait, spent, task))
        self.tasks.sort(key=lambda entry: entry[0])

    def run_task(self):
        ready, spent, task = self.tasks.pop(0)
        self.edge, self.inner = max(self.edge, ready) + spent, max(self.inner, ready) + spent
        task()

    def flush(self):
        while self.tasks:
            self.run_task()

    def take(self, mark):
        self.until(mark)
        self.edge = max(self.edge, self.blocks[mark - 1]["back"])


def layer_kernel(names, n, *refs):
    r = types.SimpleNamespace(**dict(zip(names, refs)))
    at = Place()
    own = r.self_out.shape[0]
    rows, width = r.tokens.shape
    frame_count = r.encoder.shape[0]
    clip_start = r.lengths[0, 0]
    half, quarter = rows // 2, rows // 4
    groups = width // GROUP
    halves = [pl.ds(0, half), pl.ds(half, half)]
    order = (1, 0)
    r.low = r.big.at[0, pl.ds(0, rows)]
    r.dn1, r.a, r.dul = r.dn3, r.layer_out, r.token_grad
    greet([(lax.rem(at.d + k, n), at.m) for k in range(1, n)] + [at.line(lax.rem(at.m + k, 4)) for k in (1, 2, 3)])

    own_rows = [r.big.at[i, pl.ds(pl.multiple_of(at.m * own, 16), own)] for i in range(5)]
    loads = [
        pltpu.make_async_copy(source, target, r.load.at[i])
        for i, (source, target) in enumerate(
            (
                (r.self_out, own_rows[0]), (r.cross_in.at[0], own_rows[1]), (r.cross_in.at[1], own_rows[2]),
                (r.cross_in.at[2], own_rows[3]), (r.cross_out, own_rows[4]), (r.fc_up_in, r.fc_up),
                (r.fc_down_in, r.fc_down), (r.cotangent_in, r.cotangent),
            )
        )
    ]
    for load in loads:
        load.start()
    for load in loads[:5]:
        load.wait()
    r.bias_slots[at.m, 0:2, 0:own] = r.in_biases[2:4]
    await_greetings(n + 2)

    gather = GatherFour(at, r.big, own, 2, *(getattr(r, f"g_{i}") for i in range(6)))
    last = GatherLast(at, r.big, own, 1, *(getattr(r, f"h_{i}") for i in range(6)))
    gather.start()
    biases = Direct(at, r.bias_slots, r.b_0, r.b_1)
    biases.start()
    parts = [Parts(at, r.parts.at[h], r.p_0.at[h], r.p_1.at[h]) for h in range(2)]

    def send_attended(h):
        self_forward(r, h, clip_start)
        for i in range(2):
            source = pl.ds(h * half + i * quarter, quarter)
            r.parts[h, at.m, :, i * own : (i + 1) * own] = r.o1[source]

    first, second = order
    self_projections(r)
    send_attended(first)
    parts[first].start_edge()
    gather.from_line(0)
    send_attended(second)
    parts[second].start_edge()
    frames = jnp.swapaxes(r.encoder[...], 0, 1)
    for clip in range(2):
        r.frames[clip] = jnp.zeros_like(r.frames[clip])
        r.frames[clip, 0:frame_count] = frames[clip]
    gather.from_line(1)
    parts[first].relay(0)
    gather.from_sides(0)
    gather.from_line(2)
    parts[first].start_inner()
    gather.from_sides(1)
    gather.from_corner(0)
    parts[first].relay(1)
    parts[first].relay(2)
    parts[second].start_inner()
    parts[second].relay(0)
    gather.from_sides(2)
    gather.from_corner(1)
    gather.from_corner(2)
    biases.finish()
    for o in range(4):
        r.bias[:, o * own : (o + 1) * own] = r.bias_slots[o, :, 0:own]
    for j in range(3):
        gather.from_core(j)
    parts[second].relay(1)
    parts[second].relay(2)
    last.start()
    keys_and_values(r, 2, None, r.k_pair)
    keys_and_values(r, 3, 1, r.v_pair)
    parts[first].take()

    quarters = [
        [
            (pl.ds(h * half + i * quarter, quarter), pl.ds(g * GROUP, GROUP))
            for g in range(groups) for i in range(2)
        ]
        for h in range(2)
    ]
    strips = [[pl.ds(h * half + c * 64, 64) for c in range(half // 64)] for h in range(2)]

    def totals(blocks, x, ends, other, out, letter, rooms=None):
        semaphores = [getattr(r, f"{letter}_{i}") for i in range(6)]
        return [
            Total(at, halves[h], blocks[h], x, ends, other, out, *(one.at[h] for one in semaphores), rooms=rooms)
            for h in range(2)
        ]

    o2_plain = totals(quarters, r.part_a, r.ends, r.other_a, r.o2, "t")
    o2_sum = [SoftTotal(at, r, h, halves[h], quarters[h], o2_plain[h], "s", groups) for h in range(2)]
    dn3_sum = totals(strips, r.part_a, r.ends, r.other_b, r.dn3, "u")
    down_sum = totals(strips, r.part_b, r.ends_b, r.other_c, r.down, "v", rooms=strips[0])
    dq_sum = totals(quarters, r.part_a, r.ends, r.other_a, r.dq2, "q")
    dn1_sum = totals(strips, r.part_c, r.ends, r.other_b, r.dn1, "z")
    pump = Pump()
    marks = {}

    def before_cross(h):
        block = halves[h]
        for o in range(4):
            cols = pl.ds(o * own, own)
            for i in range(2):
                target = pl.ds(h * half + i * quarter, quarter)
                r.part_b[target, cols] = r.parts[h, o, :, i * own : (i + 1) * own]
        r.x2[block] = r.tokens[block].astype(f32) + nn(r.part_b[block], r.big[0]) + r.out_biases[0:1]

        def normed(inside):
            rows_of = pl.ds(pl.multiple_of(h * half + inside.start, 64), 64)
            xhat, _ = normal(r.x2[rows_of])
            r.n2[rows_of] = (xhat * r.norm_gains[1:2] + r.norm_biases[1:2]).astype(bf16)

        row_blocks(half, 64, normed)
        queries = (nt(r.n2[block], r.big[1]) + r.bias[0:1]).astype(bf16).astype(f32)
        to_pairs(queries, r.q_pair, block, clip_start, factor)

    def attend(h, between):
        for g in range(groups):
            for j in range(2):
                cross_forward(r, halves[h], g, j, clip_start, frame_count)
                pump(0.75)
            r.lse_own[h, g] = r.stats[g, halves[h]].T[0:8]
            marks["o2", h] = pump.add(o2_sum[h], (2 * g, 2 * g + 1))
            for step in between[g]:
                step()

    def last_step(name, j):
        return functools.partial(getattr(last, name), j)

    before_cross(first)
    attend(
        first,
        [
            [last_step("from_line", 0)],
            [last_step("from_line", 1), last_step("from_sides", 0)],
            [last_step("from_line", 2), last_step("from_sides", 1), last_step("from_corner", 0)],
        ],
    )
    parts[second].take()
    before_cross(second)
    pump(1.4)
    attend(
        second,
        [
            [last_step("from_sides", 2), last_step("from_corner", 1)],
            [last_step("from_corner", 2)],
            [last_step("from_core", j) for j in range(3)],
        ],
    )

    for load in loads[5:]:
        load.wait()
    for k in range(3):
        r.bias_sums[k] = jnp.zeros_like(r.bias_sums[k])
        r.gain_sums[k] = jnp.zeros_like(r.gain_sums[k])
        r.out_sums[k] = jnp.zeros_like(r.out_sums[k])

    def back_third(h, c):
        dn3_sum[h].take(c)
        block = strips[h][c]
        upstream = r.dn3[block].astype(f32)
        grad = r.cotangent[block].astype(f32)
        change, gain = back_normal(r.x3[block], upstream, r.norm_gains[2:3])
        total = grad + change
        r.g3[block] = total
        r.low[block] = total.astype(bf16)
        r.gain_sums[2] += by_eights(gain)
        r.bias_sums[2] += by_eights(upstream)
        r.out_sums[1] += by_eights(total)
        r.out_sums[2] += by_eights(grad)

    def feed_forward(h):
        block = halves[h]
        pump.take(marks["o2", h])
        value = r.x2[block] + r.out_biases[1:2]
        for g in range(groups):
            for c in (2 * g, 2 * g + 1):
                o2_sum[h].take(c)
            cols = pl.ds(g * GROUP, GROUP)
            value = value + nn(r.o2[block, cols], r.big[4, cols])
        r.x3[block] = value
        pump(0.5)

        def normed(inside):
            rows_of = pl.ds(pl.multiple_of(h * half + inside.start, 64), 64)
            xhat, _ = normal(r.x3[rows_of])
            r.n3[rows_of] = (xhat * r.norm_gains[2:3] + r.norm_biases[2:3]).astype(bf16)

        row_blocks(half, 64, normed)
        pump(0.4)
        upward = nn(r.n3[block], r.fc_up[...]) + r.up_bias[...].reshape(1, -1)
        normal_share = 0.5 * (1.0 + lax.erf(upward * (0.5**0.5)))
        density = jnp.exp(-0.5 * upward * upward) * 0.3989422804014327
        r.a[block] = (upward * normal_share).astype(bf16)
        pump(0.7)
        change = nt(r.cotangent[block], r.fc_down[...]) * (normal_share + upward * density)
        r.up_sum[h] = by_eights(change)
        r.dul[block] = change.astype(bf16)
        pump(0.6)
        o2_sum[h].finish()
        r.part_a[block] = nt(r.dul[block], r.fc_up[...]).astype(bf16)
        pump(0.4)
        marks["dn3", h] = pump.add(dn3_sum[h], range(dn3_sum[h].count), functools.partial(back_third, h), 0.3)

    feed_forward(first)
    feed_forward(second)
    gather.finish()
    last.finish()
    for part in parts:
        part.finish()

    scatter_1 = Scatter(at, n, r.grads_1, r.came_1, r.slots_1, *(getattr(r, f"x_{i}") for i in range(4)))
    scatter_2 = Scatter(at, n, r.grads_1, r.came_2, r.slots_2, *(getattr(r, f"y_{i}") for i in range(4)))
    scatter_3 = Scatter(at, n, r.grads_3, r.came_3, r.slots_3, *(getattr(r, f"w_{i}") for i in range(4)))

    def down_came(h, c):
        down_sum[h].take(c)
        block = strips[h][c]
        r.layer_out[block] = (r.x3[block] + r.down[block].astype(f32) + r.out_biases[2:3]).astype(bf16)

    def send_down(h):
        marks["down", h] = pump.add(
            down_sum[h], range(down_sum[h].count), functools.partial(down_came, h), 0.15
        )

    def launch(scatter, result):
        size = scatter.x.shape[1] * scatter.x.shape[2] * 2
        scatter.start()

        def between_chips():
            scatter.fold()
            sides["free"] = max(sides["free"], pump.now()) + 4 * size / 94e3
            pump.later(sides["free"] - pump.now() + 3.0, 0.7, result)

        pump.later(4 * size / 400e3 + 2.5, 1.5, between_chips)

    sides, done = dict(free=0.0), []

    def result_1():
        total = scatter_1.finish()
        done.append(1)
        r.fc_up_grad[...] = total[:, 0:width]
        r.fc_down_grad[...] = total[:, width:]


    def down_part(h):
        r.part_b[halves[h]] = nn(r.a[halves[h]], r.fc_down[...]).astype(bf16)

    def run(jobs, time):
        for job in jobs:
            job()
            pump(time)

    run(weight_grad(r.grads_1, 0, r.n3, r.dul) + weight_grad(r.grads_1, width, r.cotangent, r.a), 0.5)
    launch(scatter_1, result_1)
    run([functools.partial(down_part, h) for h in order], 0.4)
    send_down(first)

    def before_queries(h):
        block = halves[h]
        pump.until(marks["dn3", h])
        dn3_sum[h].finish()
        upstream = nt(r.low[block], r.big[4]).astype(bf16).astype(f32)
        to_pairs(upstream, r.do_pair, block, clip_start, 1.0)
        r.do2_sum[h] = by_eights(upstream)
        pump(0.6)
        lane = iota((half, PAIR), 1)
        for g in range(groups):
            stats = r.stats[g, block]
            for j in range(2):
                cols = slice(g * GROUP + j * PAIR, g * GROUP + (j + 1) * PAIR)
                terms = upstream[:, cols] * r.o2[block, cols].astype(f32)
                even = jnp.sum(jnp.where(lane < HEAD, terms, 0.0), axis=1, keepdims=True)
                odd = jnp.sum(jnp.where(lane < HEAD, 0.0, terms), axis=1, keepdims=True)
                stats = jnp.where(lane == 16 + 2 * j, even, jnp.where(lane == 17 + 2 * j, odd, stats))
            r.stats[g, block] = stats
        pump(0.5)

    def query_grads(h):
        before_queries(h)
        total = dq_sum[h]
        for g in range(groups):
            for j in range(2):
                cross_queries(r, halves[h], g, j, clip_start, frame_count)
                pump(0.8)
            marks["dq", h] = pump.add(total, (2 * g, 2 * g + 1))

    query_grads(first)
    query_grads(second)


    def frame_grads(clip):
        value = tn(r.dk_t[clip], r.big[2]) + tn(r.dv_t[clip], r.big[3])
        r.encoder_grad[:, clip, :] = value[0:frame_count].astype(bf16)

    def cross_weight(source, column):
        value = sum(nn(source[clip], r.frames[clip]) for clip in range(2))
        put_blocks(r.grads_1, column, 0, value.astype(bf16).T)

    def cross_out_grad():
        own_columns(at, r.o2, r.do1)
        for job in weight_grad(r.grads_3, 5 * own, r.low, r.do1):
            job()

    def back_second(h):
        block = halves[h]
        pump.take(marks["dq", h])
        value = None
        for g in range(groups):
            for c in (2 * g, 2 * g + 1):
                dq_sum[h].take(c)
            cols = pl.ds(g * GROUP, GROUP)
            term = nn(r.dq2[block, cols], r.big[1, cols])
            value = term if value is None else value + term
        r.dn2[...] = value
        pump(0.5)

        def back(inside):
            rows_of = pl.ds(pl.multiple_of(h * half + inside.start, 64), 64)
            upstream = r.dn2[inside]
            change, gain = back_normal(r.x2[rows_of], upstream, r.norm_gains[1:2])
            total = r.g3[rows_of] + change
            r.x2[rows_of] = total
            r.low[rows_of] = total.astype(bf16)
            r.gain_sums[1] += by_eights(gain)
            r.bias_sums[1] += by_eights(upstream)
            r.out_sums[0] += by_eights(total)

        row_blocks(half, 64, back)
        pump(0.7)
        r.do1[block] = nt(r.low[block], r.self_out[...]).astype(bf16)
        self_backward(r, h, clip_start)
        pump(2.0 if h else 1.4)
        dq_sum[h].finish()
        value = nn(r.dq1[block], r.self_in[0]) + nn(r.dk1[block], r.self_in[1])
        r.part_c[block] = (value + nn(r.dv1[block], r.self_in[2])).astype(bf16)
        pump(0.4)
        marks["dn1", h] = pump.add(dn1_sum[h], range(dn1_sum[h].count), functools.partial(back_first, h), 0.3)

    def back_first(h, c):
        dn1_sum[h].take(c)
        block = strips[h][c]
        upstream = r.dn1[block].astype(f32)
        change, gain = back_normal(r.tokens[block].astype(f32), upstream, r.norm_gains[0:1])
        r.token_grad[block] = (change + r.x2[block]).astype(bf16)
        r.gain_sums[0] += by_eights(gain)
        r.bias_sums[0] += by_eights(upstream)

    def query_weight():
        own_columns(at, r.dq2, r.q1)
        for job in weight_grad(r.grads_3, 3 * own, r.n2, r.q1):
            job()
        total = jnp.sum(r.q1[...].astype(f32), axis=0, keepdims=True)
        r.in_bias_sums[2:3, 0:own] = total

    def squeeze(values):
        return jnp.sum(values, axis=0, keepdims=True)

    early = [Everyone(at, PLANE, 1, r.early_slots, r.e_0, r.e_1)]
    late = [Everyone(at, PLANE, 1, r.late_slots, r.l_0, r.l_1)]
    if n > PLANE:
        early.append(Everyone(at, n // PLANE, PLANE, r.early_slots_2, r.m_0, r.m_1))
        late.append(Everyone(at, n // PLANE, PLANE, r.late_slots_2, r.n_0, r.n_1))

    def finish_all(stages):
        total = stages[0].finish()
        for stage in stages[1:]:
            stage.slots[stage.place] = total
            stage.start()
            total = stage.finish()
        return total

    def early_vectors():
        r.in_bias_sums[1:2, 0:own] = squeeze(r.do1[...].astype(f32))
        total = squeeze(r.do2_sum[0] + r.do2_sum[1])
        for j in range(4):

            @pl.when(at.m == j)
            def _(j=j):
                r.in_bias_sums[3:4, 0:own] = total[:, j * own : (j + 1) * own]

        lines = [squeeze(r.gain_sums[k]) for k in (1, 2)] + [squeeze(r.bias_sums[k]) for k in (1, 2)]
        lines += [squeeze(r.out_sums[k]) for k in range(3)] + [squeeze(r.up_sum[0] + r.up_sum[1])]
        place = early[0].place
        r.early_slots[place, 0:8] = jnp.concatenate(lines, axis=0)
        r.early_slots[place, 8:16] = jnp.zeros((8, width), f32)
        for k in range(4):
            r.early_slots[place, 8:9, k * own : (k + 1) * own] = r.in_bias_sums[k : k + 1, 0:own]
        early[0].start()
        pump.later(8.0, 0.3, early_results)

    def early_results():
        total = finish_all(early)
        r.norm_gains_grad[1:3] = total[0:2]
        r.norm_biases_grad[1:3] = total[2:4]
        r.out_biases_grad[...] = total[4:7]
        r.up_bias_grad[...] = total[7:8].reshape(-1)
        for k in range(4):
            r.in_biases_grad[k : k + 1] = total[8:9, k * own : (k + 1) * own]

    def result_2():
        total = scatter_2.finish()
        for j in range(4):
            for t in range(2):
                cols = slice(t * width + j * own, t * width + (j + 1) * own)
                r.plane_out[j, :, t * own : (t + 1) * own] = total[:, cols].astype(bf16)
        for k in (1, 2, 3):
            to_plane(k).start()
        pump.later(12.0, 0.3, result_2_end)

    def to_plane(k):
        to = lax.rem(at.m + k, 4)
        return remote(r.plane_out.at[to], r.plane_slots.at[at.m], r.d_0.at[k], r.d_1.at[at.m], at.line(to))

    def result_2_end():
        total = r.plane_out[at.m].astype(f32)
        for k in (1, 2, 3):
            o = lax.rem(at.m + k, 4)
            remote(r.plane_out.at[o], r.plane_slots.at[o], r.d_0.at[k], r.d_1.at[o], at.line(o)).wait_recv()
            total = total + r.plane_slots[o].astype(f32)
        for t in range(2):
            r.cross_in_grad[1 + t] = total[:, t * own : (t + 1) * own]
        for k in (1, 2, 3):
            to_plane(k).wait_send()

    def result_3():
        total = scatter_3.finish()
        for i in range(3):
            r.self_in_grad[i] = total[:, i * own : (i + 1) * own]
        r.cross_in_grad[0] = total[:, 3 * own : 4 * own]
        r.self_out_grad[...] = total[:, 4 * own : 5 * own].T
        r.cross_out_grad[...] = total[:, 5 * own : 6 * own].T

    run([functools.partial(cross_frames, r, g, j, frame_count) for g in range(groups) for j in range(2)], 0.7)
    while not done:
        pump.run_task()
    run([functools.partial(cross_weight, r.dk_t, 0), functools.partial(cross_weight, r.dv_t, width)], 0.8)
    launch(scatter_2, result_2)
    cross_out_grad()
    pump(0.6)
    back_second(first)
    run([functools.partial(frame_grads, clip) for clip in range(2)], 1.2)
    back_second(second)
    pump.until(marks["down", first])
    down_sum[first].finish()
    send_down(second)
    run([query_weight] + weight_grad(r.grads_3, 4 * own, r.low, r.o1), 0.4)
    jobs = weight_grad(r.grads_3, 0, r.n1, r.dq1) + weight_grad(r.grads_3, own, r.n1, r.dk1)
    run(jobs + weight_grad(r.grads_3, 2 * own, r.n1, r.dv1), 0.3)
    launch(scatter_3, result_3)
    early_vectors()
    pump.until(marks["dn1", second])
    for h in order:
        dn1_sum[h].finish()
    place = late[0].place
    r.late_slots[place] = jnp.zeros_like(r.late_slots[place])
    r.late_slots[place, 0:1] = squeeze(r.gain_sums[0])
    r.late_slots[place, 1:2] = squeeze(r.bias_sums[0])
    late[0].start()
    pump.until(marks["down", second])
    pump.flush()
    down_sum[second].finish()
    total = finish_all(late)
    r.norm_gains_grad[0:1] = total[0:1]
    r.norm_biases_grad[0:1] = total[1:2]


def layer(n, inputs):
    tokens, self_in = inputs["tokens"], inputs["self_in"]
    rows, width = tokens.shape
    own = self_in.shape[1]
    hidden = inputs["fc_up_in"].shape[1]
    groups = width // GROUP
    per = width // n
    S = jax.ShapeDtypeStruct
    outs = dict(
        layer_out=S((rows, width), bf16), token_grad=S((rows, width), bf16),
        encoder_grad=S(inputs["encoder"].shape, bf16), norm_gains_grad=S((3, width), f32),
        norm_biases_grad=S((3, width), f32), self_in_grad=S((3, per, own), f32), cross_in_grad=S((3, per, own), f32),
        in_biases_grad=S((4, own), f32), self_out_grad=S((own, per), f32), cross_out_grad=S((own, per), f32),
        out_biases_grad=S((3, width), f32), fc_up_grad=S((per, hidden), f32), up_bias_grad=S((hidden,), f32),
        fc_down_grad=S((per, hidden), f32),
    )
    dma = pltpu.SemaphoreType.DMA
    low, full = pltpu.VMEM((rows, width), bf16), pltpu.VMEM((rows, width), f32)
    thin = pltpu.VMEM((rows, own), bf16)
    wide = pltpu.VMEM((rows, 2 * width), bf16)
    frame_pair = pltpu.VMEM((FRAMES, 2 * width), bf16)
    scratch = dict(
        fc_up=pltpu.VMEM((width, hidden), bf16), fc_down=pltpu.VMEM((hidden, width), bf16), cotangent=low,
        load=dma((8,)), big=pltpu.VMEM((5, width, width), bf16), bias=pltpu.VMEM((8, width), f32),
        bias_slots=pltpu.VMEM((4, 8, 256), f32), parts=pltpu.VMEM((2, 4, rows // 4, 2 * own), bf16),
        frames=pltpu.VMEM((2, FRAMES, width), bf16), n1=low, n2=low, n3=low, o2=low, dq2=low, dn3=low, down=low, part_a=low, part_b=low, part_c=low, ends=low,
        other_b=low, ends_b=pltpu.VMEM((rows // 2, width), bf16), other_a=low,
        other_c=pltpu.VMEM((rows // 2, width), bf16), x2=full, x3=full, g3=full, dn2=pltpu.VMEM((rows // 2, width), f32), q1=thin, k1=thin, v1=thin, o1=thin, do1=thin, dq1=thin,
        dk1=thin, dv1=thin, lse1=pltpu.VMEM((rows, 8), f32), q_pair=wide, do_pair=wide,
        k_pair=frame_pair, v_pair=frame_pair, stats=pltpu.VMEM((groups, rows, PAIR), f32),
        **{f"lse_{name}": pltpu.VMEM((2, groups, 8, rows // 2), f32) for name in ("own", "end", "mid", "far", "all")}, dk_t=pltpu.VMEM((2, width, FRAMES), bf16),
        dv_t=pltpu.VMEM((2, width, FRAMES), bf16), dk_sum=pltpu.VMEM((own, rows), f32),
        dv_sum=pltpu.VMEM((own, rows), f32), gain_sums=pltpu.VMEM((3, 8, width), f32),
        bias_sums=pltpu.VMEM((3, 8, width), f32), out_sums=pltpu.VMEM((3, 8, width), f32),
        up_sum=pltpu.VMEM((2, 8, hidden), f32), do2_sum=pltpu.VMEM((2, 8, width), f32),
        in_bias_sums=pltpu.VMEM((8, 256), f32), early_slots=pltpu.VMEM((PLANE, 16, width), f32),
        late_slots=pltpu.VMEM((PLANE, 8, width), f32), plane_out=pltpu.VMEM((4, per, 2 * own), bf16),
        plane_slots=pltpu.VMEM((4, per, 2 * own), bf16), grads_1=pltpu.VMEM((n, per, 2 * width), bf16),
        grads_3=pltpu.VMEM((n, per, 6 * own), bf16),
    )
    group_dma = Total.semaphores(groups)
    part_dma = [dma((2, 5)), dma((2, 4))]
    tiles, strips = Total.semaphores(2 * groups), Total.semaphores(rows // 128)
    for letter, group in (
        ("g", Gather.semaphores()), ("h", Gather.semaphores()), ("b", Direct.semaphores()), ("p", part_dma), ("s", group_dma),
        ("t", tiles), ("u", strips), ("v", strips), ("q", tiles), ("z", strips), ("e", Everyone.semaphores(PLANE)), ("l", Everyone.semaphores(PLANE)),
        ("d", Direct.semaphores()),
    ):
        for i, one in enumerate(group):
            scratch[f"{letter}_{i}"] = one
    if n > PLANE:
        scratch["early_slots_2"] = pltpu.VMEM((n // PLANE, 16, width), f32)
        scratch["late_slots_2"] = pltpu.VMEM((n // PLANE, 8, width), f32)
        for letter in ("m", "n"):
            for i, one in enumerate(Everyone.semaphores(n // PLANE)):
                scratch[f"{letter}_{i}"] = one
    for k, letter, cols in ((1, "x", 2 * width), (2, "y", 2 * width), (3, "w", 6 * own)):
        came, slots, *semaphores = Scatter.buffers(n, per, cols)
        scratch[f"came_{k}"], scratch[f"slots_{k}"] = came, slots
        for i, one in enumerate(semaphores):
            scratch[f"{letter}_{i}"] = one
    names = list(inputs) + list(outs) + list(scratch)
    late = ("fc_up_in", "fc_down_in", "cotangent_in", "cross_in", "cross_out")
    result = pl.pallas_call(
        functools.partial(layer_kernel, names, n),
        out_shape=list(outs.values()),
        in_specs=[SMEM if name == "lengths" else ANY if name in late else VMEM for name in inputs],
        out_specs=[VMEM] * len(outs),
        scratch_shapes=list(scratch.values()),
        compiler_params=pltpu.CompilerParams(
            collective_id=1, has_side_effects=True, vmem_limit_bytes=127 * 2**19
        ),
        name="layer",
    )(*inputs.values())
    return dict(zip(outs, result))


def results_kernel(count, *refs):
    sources, targets, rooms = (refs[k * count : (k + 1) * count] for k in range(3))
    come, go = refs[3 * count :]
    reads = [
        pltpu.make_async_copy(source, room, come.at[k]) for k, (source, room) in enumerate(zip(sources, rooms))
    ]
    writes = [
        pltpu.make_async_copy(room, target, go.at[k]) for k, (room, target) in enumerate(zip(rooms, targets))
    ]
    for read in reads:
        read.start()
    for read, write in zip(reads, writes):
        read.wait()
        write.start()
    for write in writes:
        write.wait()


def results(values):
    count = len(values)
    dma = pltpu.SemaphoreType.DMA
    return pl.pallas_call(
        functools.partial(results_kernel, count),
        out_shape=[jax.ShapeDtypeStruct(value.shape, value.dtype) for value in values],
        in_specs=[ANY] * count,
        out_specs=[ANY] * count,
        scratch_shapes=[pltpu.VMEM(value.shape, value.dtype) for value in values] + [dma((count,)), dma((count,))],
        compiler_params=pltpu.CompilerParams(vmem_limit_bytes=127 * 2**19),
        name="results",
    )(*values)


def shards(
    n, tokens, encoder, lengths, norm_gains, norm_biases, self_in, cross_in, in_biases, self_out, cross_out,
    out_biases, fc_up, up_bias, fc_down, cotangent,
):
    outs = layer(
        n,
        dict(
            tokens=tokens, encoder=encoder.transpose(1, 0, 2), lengths=lengths, norm_gains=norm_gains, norm_biases=norm_biases,
            self_in=self_in.transpose(0, 2, 1),
            cross_in=cross_in.transpose(0, 2, 1), in_biases=in_biases, self_out=self_out, cross_out=cross_out,
            out_biases=out_biases, up_bias=up_bias, fc_up_in=fc_up, fc_down_in=fc_down,
            cotangent_in=cotangent,
        ),
    )
    outs = dict(zip(outs, results(list(outs.values()))))
    outs["encoder_grad"] = outs["encoder_grad"].transpose(1, 0, 2)
    outs["fc_down_grad"] = outs["fc_down_grad"].T
    return tuple(outs.values())


def solution(mesh):
    in_specs = (
        P("dp", None), P("dp", "mp", None), P("dp", None), P(), P(), P(None, None, "mp"), P(None, None, "mp"),
        P(None, "mp"), P("mp", None), P("mp", None), P(), P(None, "mp"), P("mp"), P("mp", None), P("dp", None),
    )
    out_specs = (
        P("dp", None), P("dp", None), P("dp", "mp", None), P(), P(), P(None, "dp", "mp"), P(None, "dp", "mp"),
        P(None, "mp"), P("mp", "dp"), P("mp", "dp"), P(), P("dp", "mp"), P("mp"), P("mp", "dp"),
    )
    body = functools.partial(shards, mesh.shape["dp"])
    return jax.shard_map(body, mesh=mesh, in_specs=in_specs, out_specs=out_specs, check_vma=False)
```

```python
import functools
import types

import jax
import jax.numpy as jnp
from jax import lax
from jax.experimental import pallas as pl
from jax.experimental.pallas import tpu as pltpu
from jax.sharding import PartitionSpec as P

HEAD = 64
PAIR = 2 * HEAD
PLANE = 8
FRAMES = 384
epsilon = 1e-05
factor = 0.125
masked_value = -1e30
f32 = jnp.float32
bf16 = jnp.bfloat16
MESH = pl.DeviceIdType.MESH
VMEM = pl.BlockSpec(memory_space=pltpu.VMEM)
SMEM = pl.BlockSpec(memory_space=pltpu.SMEM)
ANY = pl.BlockSpec(memory_space=pl.ANY)


def nn(a, b):
    return jnp.dot(a, b, preferred_element_type=f32)


def nt(a, b):
    return lax.dot_general(a, b, (((1,), (1,)), ((), ())), preferred_element_type=f32)


def tn(a, b):
    return lax.dot_general(a, b, (((0,), (0,)), ((), ())), preferred_element_type=f32)


def flip(index, bit):
    return index + bit - 2 * bit * lax.rem(index // bit, 2)


def remote(src, dst, send, recv, device):
    return pltpu.make_async_remote_copy(
        src_ref=src, dst_ref=dst, send_sem=send, recv_sem=recv, device_id=device, device_id_type=MESH
    )


def greet(devices):
    barrier = pltpu.get_barrier_semaphore()
    for device in devices:
        pl.semaphore_signal(barrier, inc=1, device_id=device, device_id_type=MESH)


def await_greetings(count):
    pl.semaphore_wait(pltpu.get_barrier_semaphore(), count)


def pair_sum(left, right):
    return (left.astype(f32) + right.astype(f32)).astype(bf16)


class Place:
    def __init__(self):
        self.d, self.m = d, m = lax.axis_index("dp"), lax.axis_index("mp")
        self.mine = lax.rem(d, PLANE)
        self.base = d - self.mine
        self.half = m // 2
        self.rank = m + self.half * (3 - 2 * m)
        self.edge, self.inner = self.rank == 0, self.rank == 1
        self.near = flip(m, 1)
        self.peer = 3 - m

    def origin(self, j):
        index = 1 - self.rank if j == 0 else j + 1
        return index + self.half * (3 - 2 * index)

    def line(self, m):
        return (self.d, m)

    def plane(self, s):
        return (self.base + s, self.m)

    def way(self, k):
        s = self.mine
        for bit in (1, 2, 4):
            if k & bit:
                s = flip(s, bit)
        return s


class Gather:
    def __init__(self, at, big, own, cuts, line_send, side_send, corner_send, core_send, recv, core_recv):
        self.at, self.big, self.own, self.cuts = at, big, own, cuts
        self.line_send, self.side_send, self.corner_send = line_send, side_send, corner_send
        self.core_send, self.recv, self.core_recv = core_send, recv, core_recv
        self.core, self.chip = lax.rem(at.mine, 2), at.mine // 2
        self.pieces = range(cuts)

    def copy(self, o, chip, i, send, device):
        block = self.block(o, chip, i)
        return remote(block, block, send, self.recv.at[o, chip, i], device)

    def came(self, o, chip, i):
        self.copy(o, chip, i, self.line_send, self.at.line(self.at.m)).wait_recv()

    def start(self):
        at = self.at
        for i in self.pieces:
            self.copy(at.m, self.chip, i, self.line_send, at.line(at.near)).start()

            @pl.when(at.inner)
            def _(i=i):
                self.copy(at.m, self.chip, i, self.line_send, at.line(at.peer)).start()

    def from_line(self, j):
        at = self.at
        o = at.origin(j)
        for i in self.pieces:
            self.came(o, self.chip, i)

            @pl.when(at.inner)
            def _(i=i):
                to = at.peer if j == 0 else at.near
                self.copy(o, self.chip, i, self.line_send, at.line(to)).start()

            for k in (2, 4):
                self.copy(o, self.chip, i, self.side_send, at.plane(at.way(k))).start()

    def passed_on(self):
        return ((2, 0), (4, 1))[: self.cuts]

    def from_sides(self, j):
        at = self.at
        o = at.origin(j)
        for k, i in self.passed_on():
            chip = flip(self.chip, k // 2)
            self.came(o, chip, i)
            self.copy(o, chip, i, self.corner_send, at.plane(at.way(6 - k))).start()

    def core_copy(self, j, mine):
        block = self.core_block(self.at.origin(j), self.core if mine else 1 - self.core)
        return remote(block, block, self.core_send.at[j], self.core_recv.at[j], self.at.plane(self.at.way(1)))

    def from_corner(self, j):
        o = self.at.origin(j)
        for k in (2, 4):
            for i in self.pieces:
                if (k, i) not in self.passed_on():
                    self.came(o, flip(self.chip, k // 2), i)
        for i in self.pieces:
            self.came(o, flip(flip(self.chip, 1), 2), i)
        self.core_copy(j, True).start()

    def from_core(self, j):
        self.core_copy(j, False).wait_recv()

    def sent(self, slices, send):
        block = self.slices(slices)
        remote(block, block, send, self.core_recv.at[0], self.at.line(self.at.near)).wait_send()

    def finish(self):
        at = self.at

        @pl.when(at.edge)
        def _():
            self.sent(1, self.line_send)

        @pl.when(at.inner)
        def _():
            self.sent(5, self.line_send)

        self.sent(6, self.side_send)
        self.sent(3, self.corner_send)
        for j in range(3):
            self.core_copy(j, True).wait_send()

    @staticmethod
    def semaphores():
        dma = pltpu.SemaphoreType.DMA
        return [dma, dma, dma, dma((3,)), dma((4, 4, 2)), dma((3,))]


class GatherFour(Gather):
    def block(self, o, chip, i):
        row = o * self.own + lax.rem(chip, 2) * (self.own // 2) + i * (self.own // 4)
        return self.big.at[2 * self.core + chip // 2, pl.ds(pl.multiple_of(row, 16), self.own // 4)]

    def core_block(self, o, core):
        return self.big.at[pl.ds(2 * core, 2), pl.ds(pl.multiple_of(o * self.own, 16), self.own)]

    def slices(self, count):
        return self.big.at[0, pl.ds(0, count * self.own // 2)]


class GatherLast(Gather):
    def columns(self, core):
        half = self.big.shape[2] // 2
        return pl.ds(pl.multiple_of(core * half, PAIR), half)

    def block(self, o, chip, i):
        row = pl.multiple_of(o * self.own + chip * (self.own // 4), 16)
        return self.big.at[4, pl.ds(row, self.own // 4), self.columns(self.core)]

    def core_block(self, o, core):
        return self.big.at[4, pl.ds(pl.multiple_of(o * self.own, 16), self.own), self.columns(core)]

    def slices(self, count):
        return self.big.at[4, pl.ds(0, count * self.own // 4), pl.ds(0, self.big.shape[2] // 2)]


class Parts:
    def __init__(self, at, slots, send, recv):
        self.at, self.slots, self.send, self.recv = at, slots, send, recv

    def copy(self, o, send, to):
        return remote(self.slots.at[o], self.slots.at[o], send, self.recv.at[o], self.at.line(to))

    def own(self, to_peer):
        at = self.at
        return self.copy(at.m, self.send.at[to_peer], at.peer if to_peer else at.near)

    def forward(self, j):
        at = self.at
        return self.copy(at.origin(j), self.send.at[2 + j], at.peer if j == 0 else at.near)

    def start_edge(self):
        @pl.when(self.at.edge)
        def _():
            self.own(0).start()

    def start_inner(self):
        @pl.when(self.at.inner)
        def _():
            self.own(0).start()
            self.own(1).start()

    def came(self, j):
        self.copy(self.at.origin(j), self.send.at[0], self.at.m).wait_recv()

    def relay(self, j):
        @pl.when(self.at.inner)
        def _():
            self.came(j)
            self.forward(j).start()

    def take(self):
        @pl.when(self.at.edge)
        def _():
            for j in range(3):
                self.came(j)

    def finish(self):
        self.own(0).wait_send()

        @pl.when(self.at.inner)
        def _():
            self.own(1).wait_send()
            for j in range(3):
                self.forward(j).wait_send()

    @staticmethod
    def semaphores():
        dma = pltpu.SemaphoreType.DMA
        return [dma((5,)), dma((4,))]


class Direct:
    def __init__(self, at, slots, send, recv):
        self.at, self.slots, self.send, self.recv = at, slots, send, recv

    def copy(self, o, k):
        to = lax.rem(self.at.m + k, 4)
        return remote(self.slots.at[o], self.slots.at[o], self.send.at[k], self.recv.at[o], self.at.line(to))

    def start(self):
        for k in (1, 2, 3):
            self.copy(self.at.m, k).start()

    def finish(self):
        for k in (1, 2, 3):
            self.copy(lax.rem(self.at.m + k, 4), k).wait_recv()
        for k in (1, 2, 3):
            self.copy(self.at.m, k).wait_send()

    @staticmethod
    def semaphores():
        dma = pltpu.SemaphoreType.DMA
        return [dma((4,)), dma((4,))]


class Everyone:
    def __init__(self, at, size, stride, slots, send, recv):
        self.at, self.size, self.stride, self.slots, self.send, self.recv = at, size, stride, slots, send, recv
        self.place = lax.rem(at.d // stride, size)

    def copy(self, o, k):
        to = self.at.d + (lax.rem(self.place + k, self.size) - self.place) * self.stride
        return remote(
            self.slots.at[o], self.slots.at[o], self.send.at[k], self.recv.at[o], (to, self.at.m)
        )

    def start(self):
        for k in range(1, self.size):
            self.copy(self.place, k).start()

    def finish(self):
        for k in range(1, self.size):
            self.copy(lax.rem(self.place + k, self.size), k).wait_recv()
        for k in range(1, self.size):
            self.copy(self.place, k).wait_send()
        total = self.slots[0]
        for o in range(1, self.size):
            total = total + self.slots[o]
        return total

    @staticmethod
    def semaphores(size):
        dma = pltpu.SemaphoreType.DMA
        return [dma((size,)), dma((size,))]


class Scatter:
    def __init__(self, at, n, x, came, slots, s1, r1, s2, r2):
        self.at, self.x, self.came, self.slots = at, x, came, slots
        self.s1, self.r1, self.s2, self.r2 = s1, r1, s2, r2
        self.core, self.chip, self.chips = lax.rem(at.d, 2), at.d // 2, n // 2
        self.order = list(range(1, self.chips)) + [0]

    def to_sibling(self, k):
        c = lax.rem(self.chip + k, self.chips)
        other = 1 - self.core
        return remote(
            self.x.at[2 * c + other], self.came.at[c], self.s1.at[c], self.r1.at[c],
            (2 * self.chip + other, self.at.m),
        )

    def between(self, k, slot):
        c = lax.rem(self.chip + k, self.chips)
        return remote(
            self.x.at[2 * c + self.core], self.slots.at[slot], self.s2.at[c], self.r2.at[slot],
            (2 * c + self.core, self.at.m),
        )

    def start(self):
        for k in self.order:
            self.to_sibling(k).start()

    def fold(self):
        for k in self.order:
            c = lax.rem(self.chip + k, self.chips)
            self.to_sibling(k).wait_recv()
            block = 2 * c + self.core
            self.x[block] = pair_sum(self.x[block], self.came[c])
            if k:
                self.between(k, self.chip).start()

    def finish(self):
        total = self.x[2 * self.chip + self.core].astype(f32)
        for k in range(1, self.chips):
            c = lax.rem(self.chip + k, self.chips)
            self.between(k, c).wait_recv()
            total = total + self.slots[c].astype(f32)
        for k in self.order:
            self.to_sibling(k).wait_send()
        for k in range(1, self.chips):
            self.between(k, self.chip).wait_send()
        return total

    @staticmethod
    def buffers(n, rows, cols):
        half = pltpu.VMEM((n // 2, rows, cols), bf16)
        dma = pltpu.SemaphoreType.DMA((n // 2,))
        return [half, half, dma, dma, dma, dma]


class Total:
    def __init__(self, at, whole, blocks, x, ends, other, out, sa, ra, sb, rb, sr, rr, rooms=None):
        self.at, self.whole, self.blocks, self.rooms = at, whole, blocks, rooms or blocks
        self.x, self.ends, self.other, self.out = x, ends, other, out
        self.sa, self.ra, self.sb, self.rb, self.sr, self.rr = sa, ra, sb, rb, sr, rr
        self.count = len(blocks)
        self.size = whole.size * x.shape[1] * 2 / self.count

    def inward(self, c):
        room = self.ends.at[self.rooms[c]]
        return remote(self.x.at[self.blocks[c]], room, self.sa, self.ra.at[c], self.at.line(self.at.near))

    def across(self, c):
        room = self.other.at[self.rooms[c]]
        return remote(self.x.at[self.blocks[c]], room, self.sb, self.rb.at[c], self.at.line(self.at.peer))

    def outward(self, c):
        block = self.out.at[self.blocks[c]]
        return remote(block, block, self.sr, self.rr.at[c], self.at.line(self.at.near))

    def send(self, c):
        @pl.when(self.at.edge)
        def _():
            self.inward(c).start()

    def fold(self, c):
        @pl.when(self.at.inner)
        def _():
            b = self.blocks[c]
            self.inward(c).wait_recv()
            self.x[b] = pair_sum(self.x[b], self.ends[self.rooms[c]])
            self.across(c).start()

    def close(self, c):
        @pl.when(self.at.inner)
        def _():
            b = self.blocks[c]
            self.across(c).wait_recv()
            self.out[b] = pair_sum(self.x[b], self.other[self.rooms[c]])
            self.outward(c).start()

    def take(self, c):
        @pl.when(self.at.edge)
        def _():
            self.outward(c).wait_recv()

    def sent(self, source, send):
        block = source.at[self.whole]
        remote(block, block, send, self.ra.at[0], self.at.line(self.at.near)).wait_send()

    def finish(self):
        @pl.when(self.at.edge)
        def _():
            self.sent(self.x, self.sa)

        @pl.when(self.at.inner)
        def _():
            self.sent(self.x, self.sb)
            self.sent(self.out, self.sr)

    @staticmethod
    def semaphores(count):
        dma = pltpu.SemaphoreType.DMA
        return [dma((2,)), dma((2, count))] * 3


class SoftTotal:
    def __init__(self, at, r, h, block, blocks, sums, letter, groups):
        self.at, self.r, self.h, self.block, self.sums = at, r, h, block, sums
        self.semaphores = [getattr(r, f"{letter}_{i}").at[h] for i in range(6)]
        self.blocks, self.groups = blocks, groups
        self.count = len(blocks)
        self.each = self.count // groups
        self.size = sums.size

    def small(self, kind, source, target, g, to):
        send, recv = self.semaphores[2 * kind], self.semaphores[2 * kind + 1]
        return remote(source.at[self.h, g], target.at[self.h, g], send, recv.at[g], self.at.line(to))

    def small_sent(self, kind, source):
        whole = source.at[self.h]
        send, recv = self.semaphores[2 * kind], self.semaphores[2 * kind + 1]
        remote(whole, whole, send, recv.at[0], self.at.line(self.at.near)).wait_send()

    def inward(self, g):
        return self.small(0, self.r.lse_own, self.r.lse_end, g, self.at.near)

    def across(self, g):
        return self.small(1, self.r.lse_mid, self.r.lse_far, g, self.at.peer)

    def outward(self, g):
        return self.small(2, self.r.lse_all, self.r.lse_all, g, self.at.near)

    def spread(self, tables, rows, tile):
        low = iota((rows.size, PAIR), 1) < HEAD
        return jnp.where(low, tables[:, 2 * tile : 2 * tile + 1], tables[:, 2 * tile + 1 : 2 * tile + 2])

    def columns(self, *tables):
        spare = jnp.zeros((PAIR - 8 * len(tables), self.block.size), f32)
        return jnp.concatenate([*tables, spare], axis=0).T

    def merge(self, left, right):
        top = jnp.maximum(left, right)
        total = top + jnp.log(jnp.exp(left - top) + jnp.exp(right - top))
        return total, jnp.exp(left - total), jnp.exp(right - total)

    def send(self, c):
        g = c // self.each

        @pl.when(self.at.edge)
        def _():
            if c % self.each == 0:
                self.inward(g).start()
            rows, cols = self.blocks[c]
            self.r.part_a[rows, cols] = self.r.g3[rows, cols].astype(bf16)

        self.sums.send(c)

    def fold(self, c):
        r, sums, g = self.r, self.sums, c // self.each

        @pl.when(self.at.inner)
        def _():
            if c % self.each == 0:
                self.inward(g).wait_recv()
                total, own, end = self.merge(r.lse_own[self.h, g], r.lse_end[self.h, g])
                r.lse_mid[self.h, g] = total
                self.across(g).start()
                r.stats[g, self.block] = self.columns(own, end)
            sums.inward(c).wait_recv()
            rows, cols = self.blocks[c]
            table = r.stats[g, rows]
            for t in range(2):
                tile = pl.ds(cols.start + t * PAIR, PAIR)
                value = r.g3[rows, tile] * self.spread(table, rows, t)
                value = value + r.ends[rows, tile].astype(f32) * self.spread(table[:, 8:], rows, t)
                r.part_a[rows, tile] = value.astype(bf16)
            sums.across(c).start()

    def close(self, c):
        r, sums, g, at = self.r, self.sums, c // self.each, self.at

        @pl.when(at.inner)
        def _():
            lower = at.half == 0
            if c % self.each == 0:
                self.across(g).wait_recv()
                mid, far = r.lse_mid[self.h, g], r.lse_far[self.h, g]
                total, left, right = self.merge(jnp.where(lower, mid, far), jnp.where(lower, far, mid))
                r.lse_all[self.h, g] = total
                self.outward(g).start()
                r.stats[g, self.block] = self.columns(total, left, right)
            sums.across(c).wait_recv()
            rows, cols = self.blocks[c]
            table = r.stats[g, rows]
            for t in range(2):
                tile = pl.ds(cols.start + t * PAIR, PAIR)
                mid, far = r.part_a[rows, tile].astype(f32), r.other_a[rows, tile].astype(f32)
                left, right = jnp.where(lower, mid, far), jnp.where(lower, far, mid)
                value = left * self.spread(table[:, 8:], rows, t) + right * self.spread(table[:, 16:], rows, t)
                r.o2[rows, tile] = value.astype(bf16)
            sums.outward(c).start()

    def take(self, c):
        g = c // self.each
        self.sums.take(c)
        if c % self.each == 0:

            @pl.when(self.at.edge)
            def _():
                self.outward(g).wait_recv()
                self.r.stats[g, self.block] = self.columns(self.r.lse_all[self.h, g])

    def finish(self):
        self.sums.finish()

        @pl.when(self.at.edge)
        def _():
            self.small_sent(0, self.r.lse_own)

        @pl.when(self.at.inner)
        def _():
            self.small_sent(1, self.r.lse_mid)
            self.small_sent(2, self.r.lse_all)


def normal(values):
    average = jnp.mean(values, axis=-1, keepdims=True)
    centred = values - average
    variance = jnp.mean(centred * centred, axis=-1, keepdims=True)
    scale = lax.rsqrt(variance + epsilon)
    return centred * scale, scale


def row_blocks(count, size, body):
    def step(i, carry):
        body(pl.ds(pl.multiple_of(i * size, size), size))
        return carry

    lax.fori_loop(0, count // size, step, 0)


def iota(shape, axis):
    return lax.broadcasted_iota(jnp.int32, shape, axis)


def pair_tiles(tile):
    turned = pltpu.roll(tile, HEAD, axis=1)
    low = iota(tile.shape, 1) < HEAD
    return jnp.where(low, tile, turned), jnp.where(low, turned, tile)


def back_normal(values, upstream, gain):
    xhat, scale = normal(values)
    scaled = upstream * gain
    first = jnp.mean(scaled, axis=-1, keepdims=True)
    second = jnp.mean(scaled * xhat, axis=-1, keepdims=True)
    return scale * (scaled - first - xhat * second), upstream * xhat


def by_eights(values):
    return jnp.sum(values.reshape(-1, 8, values.shape[1]), axis=0)


def own_columns(at, source, target):
    width = target.shape[1]
    for j in range(4):

        @pl.when(at.m == j)
        def _(j=j):
            target[...] = source[:, j * width : (j + 1) * width]


def self_mask(rows, keys, start, clip_start):
    row = iota((rows, keys), 0) + start
    col = iota((rows, keys), 1)
    return jnp.logical_and(col <= row, (row >= clip_start) == (col >= clip_start))


def self_projections(r):
    rows = r.tokens.shape[0]

    def normed(block):
        xhat, _ = normal(r.tokens[block].astype(f32))
        r.n1[block] = (xhat * r.norm_gains[0:1] + r.norm_biases[0:1]).astype(bf16)

    row_blocks(rows, 64, normed)
    r.q1[...] = (nt(r.n1[...], r.self_in[0]) + r.in_biases[0:1]).astype(bf16)
    r.k1[...] = nt(r.n1[...], r.self_in[1]).astype(bf16)
    r.v1[...] = (nt(r.n1[...], r.self_in[2]) + r.in_biases[1:2]).astype(bf16)


def self_forward(r, part, clip_start):
    half = r.tokens.shape[0] // 2
    block, keys = pl.ds(part * half, half), (part + 1) * half
    allowed = self_mask(half, keys, part * half, clip_start)
    for h in range(r.q1.shape[1] // HEAD):
        cols = pl.ds(h * HEAD, HEAD)
        scores = nt(r.q1[block, cols] * bf16(factor), r.k1[0:keys, cols])
        scores = jnp.where(allowed, scores, masked_value)
        top = jnp.max(scores, axis=1, keepdims=True)
        power = jnp.exp(scores - top)
        total = jnp.sum(power, axis=1, keepdims=True)
        chance = (power * (1 / total)).astype(bf16)
        r.o1[block, cols] = nn(chance, r.v1[0:keys, cols]).astype(bf16)
        r.lse1[block, pl.ds(h, 1)] = top + jnp.log(total)


def self_backward(r, part, clip_start):
    half = r.tokens.shape[0] // 2
    block, keys = pl.ds(part * half, half), (part + 1) * half
    allowed = self_mask(half, keys, part * half, clip_start)
    for h in range(r.q1.shape[1] // HEAD):
        cols = pl.ds(h * HEAD, HEAD)
        query, upstream = r.q1[block, cols] * bf16(factor), r.do1[block, cols]
        scores = jnp.where(allowed, nt(query, r.k1[0:keys, cols]), masked_value)
        chance = jnp.exp(scores - r.lse1[block, pl.ds(h, 1)])
        slope = nt(upstream, r.v1[0:keys, cols])
        inner = jnp.sum(chance * slope, axis=1, keepdims=True)
        change = (chance * (slope - inner)).astype(bf16)
        query_grad = nn(change, r.k1[0:keys, cols]) * factor
        r.dq1[block, cols] = query_grad.astype(bf16)
        bias = jnp.sum(query_grad, axis=0, keepdims=True)
        key_grad, value_grad = tn(query, change), tn(upstream, chance.astype(bf16))
        if part:
            r.in_bias_sums[0:1, cols] = bias
            r.dk_sum[cols, :] = key_grad
            r.dv_sum[cols, :] = value_grad
        else:
            r.in_bias_sums[0:1, cols] += bias
            r.dk_sum[cols, 0:keys] += key_grad
            r.dv_sum[cols, 0:keys] += value_grad
    r.dk1[block] = r.dk_sum[:, block].T.astype(bf16)
    r.dv1[block] = r.dv_sum[:, block].T.astype(bf16)


def keys_and_values(r, matrix, bias, pairs):
    both = [nt(r.frames[clip], r.big[matrix]) for clip in range(2)]
    if bias is not None:
        both = [value + r.bias[bias : bias + 1] for value in both]
    for t in range(both[0].shape[1] // PAIR):
        first, second = (value[:, t * PAIR : (t + 1) * PAIR] for value in both)
        low = iota(first.shape, 1) < HEAD
        turned_first, turned_second = pltpu.roll(first, HEAD, axis=1), pltpu.roll(second, HEAD, axis=1)
        pairs[:, 2 * t * PAIR : (2 * t + 1) * PAIR] = jnp.where(low, first, turned_second).astype(bf16)
        pairs[:, (2 * t + 1) * PAIR : (2 * t + 2) * PAIR] = jnp.where(low, turned_first, second).astype(bf16)


def to_pairs(value, pairs, block, clip_start, scale):
    rows = value.shape[0]
    keep = (iota((rows, PAIR), 1) < HEAD) == (iota((rows, PAIR), 0) + block.start < clip_start)
    for t in range(value.shape[1] // PAIR):
        for e, tile in enumerate(pair_tiles(value[:, t * PAIR : (t + 1) * PAIR])):
            at = (2 * t + e) * PAIR
            pairs[block, at : at + PAIR] = (jnp.where(keep, tile, 0.0) * scale).astype(bf16)


def from_pair(even, odd, first):
    low = iota(even.shape, 1) < HEAD
    even = jnp.where(first, even, pltpu.roll(even, HEAD, axis=1))
    odd = jnp.where(first, pltpu.roll(odd, HEAD, axis=1), odd)
    return jnp.where(low, even, odd)


GROUP = 2 * PAIR
GROUP_HEADS = 4


def of_clip(block, clip_start):
    return iota((block.size, PAIR), 0) + block.start < clip_start


def real_frames(rows, frame_count):
    return iota((rows, FRAMES), 1) < frame_count


def cross_forward(r, block, g, j, clip_start, frame_count):
    lane = iota((block.size, PAIR), 1)
    first = of_clip(block, clip_start)
    valid = real_frames(block.size, frame_count)
    halves = []
    stats = jnp.zeros((block.size, PAIR), f32) if j == 0 else r.stats[g, block]
    for e in (0, 1):
        cols = pl.ds(2 * GROUP * g + 2 * PAIR * j + PAIR * e, PAIR)
        scores = jnp.where(valid, nt(r.q_pair[block, cols], r.k_pair[:, cols]), masked_value)
        top = jnp.max(scores, axis=1, keepdims=True)
        power = jnp.exp(scores - top)
        total = jnp.sum(power, axis=1, keepdims=True)
        halves.append(nn(power.astype(bf16), r.v_pair[:, cols]) * (1 / total))
        stats = jnp.where(lane == 2 * j + e, top + jnp.log(total), stats)
    r.stats[g, block] = stats
    r.g3[block, pl.ds(GROUP * g + PAIR * j, PAIR)] = from_pair(*halves, first)


def cross_slopes(r, block, cols, lane, stats, index, valid):
    def column(i):
        return jnp.sum(jnp.where(lane == i, stats, 0.0), axis=1, keepdims=True)

    scores = jnp.where(valid, nt(r.q_pair[block, cols], r.k_pair[:, cols]), masked_value)
    chance = jnp.exp(scores - column(index))
    slope = nt(r.do_pair[block, cols], r.v_pair[:, cols])
    return chance, (chance * (slope - column(16 + index))).astype(bf16)


def cross_queries(r, block, g, j, clip_start, frame_count):
    lane = iota((block.size, PAIR), 1)
    first = of_clip(block, clip_start)
    valid = real_frames(block.size, frame_count)
    stats = r.stats[g, block]
    halves = []
    for e in (0, 1):
        cols = pl.ds(2 * GROUP * g + 2 * PAIR * j + PAIR * e, PAIR)
        _, change = cross_slopes(r, block, cols, lane, stats, 2 * j + e, valid)
        halves.append(nn(change, r.k_pair[:, cols]) * factor)
    r.part_a[block, pl.ds(GROUP * g + PAIR * j, PAIR)] = from_pair(*halves, first).astype(bf16)


def cross_frames(r, g, j, frame_count):
    rows = r.q_pair.shape[0]
    block = pl.ds(0, rows)
    lane = iota((rows, PAIR), 1)
    valid = real_frames(rows, frame_count)
    for e in (0, 1):
        cols = pl.ds(2 * GROUP * g + 2 * PAIR * j + PAIR * e, PAIR)
        chance, change = cross_slopes(r, block, cols, lane, r.stats[g], 2 * j + e, valid)
        value_grad = tn(r.do_pair[:, cols], chance.astype(bf16)).astype(bf16)
        key_grad = tn(r.q_pair[:, cols], change).astype(bf16)
        head = pl.ds(GROUP * g + PAIR * j + HEAD * e, HEAD)
        for clip in range(2):
            r.dv_t[clip, head] = value_grad[clip * HEAD : (clip + 1) * HEAD]
            r.dk_t[clip, head] = key_grad[clip * HEAD : (clip + 1) * HEAD]


def put_blocks(x, column, first_row, value):
    per = x.shape[1]
    for i in range(value.shape[0] // per):
        x[first_row // per + i, :, column : column + value.shape[1]] = value[i * per : (i + 1) * per].astype(bf16)


def weight_grad(x, column, left, right):
    part = left.shape[1] // 2
    return [
        functools.partial(
            lambda i: put_blocks(x, column, i * part, tn(left[:, i * part : (i + 1) * part], right[...])), i
        )
        for i in range(2)
    ]


class Pump:
    latency, rate, step, issue = 1.8, 47.0e3, 0.2, 0.1

    def __init__(self):
        self.blocks, self.folded, self.closed, self.tasks = [], 0, 0, []
        self.edge, self.inner = 0.0, 0.0
        self.free = dict(inward=0.0, across=0.0, outward=0.0)

    def travel(self, link, block, start):
        self.free[link] = max(self.free[link], start) + block["bytes"] / self.rate
        return self.free[link] + self.latency

    def add(self, total, chosen, after=None, after_time=0.0):
        for c in chosen:
            total.send(c)
            self.edge += self.issue
            block = dict(total=total, c=c, after=after, time=after_time, bytes=total.size)
            block["came"] = self.travel("inward", block, self.edge)
            self.blocks.append(block)
        return len(self.blocks)

    def fold(self):
        block = self.blocks[self.folded]
        block["total"].fold(block["c"])
        self.inner = max(self.inner, block["came"]) + self.step
        block["crossed"] = self.travel("across", block, self.inner)
        self.folded += 1

    def close(self):
        block = self.blocks[self.closed]
        block["total"].close(block["c"])
        self.inner = max(self.inner, block["crossed"]) + self.step
        block["back"] = self.travel("outward", block, self.inner)
        self.closed += 1
        if block["after"] is not None:
            block["after"](block["c"])
            self.inner += block["time"]
            self.edge = max(self.edge, block["back"]) + block["time"]

    def next_step(self):
        steps = []
        if self.closed < self.folded:
            steps.append((self.blocks[self.closed]["crossed"], self.close))
        if self.folded < len(self.blocks):
            steps.append((self.blocks[self.folded]["came"], self.fold))
        if self.tasks:
            steps.append((self.tasks[0][0], self.run_task))
        return min(steps, key=lambda step: step[0], default=(float("inf"), None))

    def __call__(self, spent):
        self.edge += spent
        self.inner += spent
        while True:
            time, step = self.next_step()
            if time > self.inner:
                return
            step()

    def until(self, mark):
        while self.closed < mark:
            self.next_step()[1]()

    def now(self):
        return max(self.edge, self.inner)

    def later(self, wait, spent, task):
        self.tasks.append((self.now() + wait, spent, task))
        self.tasks.sort(key=lambda entry: entry[0])

    def run_task(self):
        ready, spent, task = self.tasks.pop(0)
        self.edge, self.inner = max(self.edge, ready) + spent, max(self.inner, ready) + spent
        task()

    def flush(self):
        while self.tasks:
            self.run_task()

    def take(self, mark):
        self.until(mark)
        self.edge = max(self.edge, self.blocks[mark - 1]["back"])


def layer_kernel(names, n, *refs):
    r = types.SimpleNamespace(**dict(zip(names, refs)))
    at = Place()
    own = r.self_out.shape[0]
    rows, width = r.tokens.shape
    frame_count = r.encoder.shape[0]
    clip_start = r.lengths[0, 0]
    half, quarter = rows // 2, rows // 4
    groups = width // GROUP
    halves = [pl.ds(0, half), pl.ds(half, half)]
    order = (1, 0)
    r.low = r.big.at[0, pl.ds(0, rows)]
    r.dn1, r.a, r.dul = r.dn3, r.layer_out, r.token_grad
    greet([(lax.rem(at.d + k, n), at.m) for k in range(1, n)] + [at.line(lax.rem(at.m + k, 4)) for k in (1, 2, 3)])

    own_rows = [r.big.at[i, pl.ds(pl.multiple_of(at.m * own, 16), own)] for i in range(5)]
    loads = [
        pltpu.make_async_copy(source, target, r.load.at[i])
        for i, (source, target) in enumerate(
            (
                (r.self_out, own_rows[0]), (r.cross_in.at[0], own_rows[1]), (r.cross_in.at[1], own_rows[2]),
                (r.cross_in.at[2], own_rows[3]), (r.cross_out, own_rows[4]), (r.fc_up_in, r.fc_up),
                (r.fc_down_in, r.fc_down), (r.cotangent_in, r.cotangent),
            )
        )
    ]
    for load in loads:
        load.start()
    for load in loads[:5]:
        load.wait()
    r.bias_slots[at.m, 0:2, 0:own] = r.in_biases[2:4]
    await_greetings(n + 2)

    gather = GatherFour(at, r.big, own, 2, *(getattr(r, f"g_{i}") for i in range(6)))
    last = GatherLast(at, r.big, own, 1, *(getattr(r, f"h_{i}") for i in range(6)))
    gather.start()
    biases = Direct(at, r.bias_slots, r.b_0, r.b_1)
    biases.start()
    parts = [Parts(at, r.parts.at[h], r.p_0.at[h], r.p_1.at[h]) for h in range(2)]

    def send_attended(h):
        self_forward(r, h, clip_start)
        for i in range(2):
            source = pl.ds(h * half + i * quarter, quarter)
            r.parts[h, at.m, :, i * own : (i + 1) * own] = r.o1[source]

    first, second = order
    self_projections(r)
    send_attended(first)
    parts[first].start_edge()
    gather.from_line(0)
    send_attended(second)
    parts[second].start_edge()
    frames = jnp.swapaxes(r.encoder[...], 0, 1)
    for clip in range(2):
        r.frames[clip] = jnp.zeros_like(r.frames[clip])
        r.frames[clip, 0:frame_count] = frames[clip]
    gather.from_line(1)
    parts[first].relay(0)
    gather.from_sides(0)
    gather.from_line(2)
    parts[first].start_inner()
    gather.from_sides(1)
    gather.from_corner(0)
    parts[first].relay(1)
    parts[first].relay(2)
    parts[second].start_inner()
    parts[second].relay(0)
    gather.from_sides(2)
    gather.from_corner(1)
    gather.from_corner(2)
    biases.finish()
    for o in range(4):
        r.bias[:, o * own : (o + 1) * own] = r.bias_slots[o, :, 0:own]
    for j in range(3):
        gather.from_core(j)
    keys_and_values(r, 2, None, r.k_pair)
    parts[second].relay(1)
    keys_and_values(r, 3, 1, r.v_pair)
    parts[second].relay(2)
    last.start()
    parts[first].take()

    quarters = [
        [
            (pl.ds(h * half + i * quarter, quarter), pl.ds(g * GROUP, GROUP))
            for g in range(groups) for i in range(2)
        ]
        for h in range(2)
    ]
    strips = [[pl.ds(h * half + c * 64, 64) for c in range(half // 64)] for h in range(2)]

    def totals(blocks, x, ends, other, out, letter, rooms=None):
        semaphores = [getattr(r, f"{letter}_{i}") for i in range(6)]
        return [
            Total(at, halves[h], blocks[h], x, ends, other, out, *(one.at[h] for one in semaphores), rooms=rooms)
            for h in range(2)
        ]

    o2_plain = totals(quarters, r.part_a, r.ends, r.other_a, r.o2, "t")
    o2_sum = [SoftTotal(at, r, h, halves[h], quarters[h], o2_plain[h], "s", groups) for h in range(2)]
    dn3_sum = totals(strips, r.part_a, r.ends, r.other_b, r.dn3, "u")
    down_sum = totals(strips, r.part_b, r.ends_b, r.other_c, r.down, "v", rooms=strips[0])
    dq_sum = totals(quarters, r.part_a, r.ends, r.other_a, r.dq2, "q")
    dn1_sum = totals(strips, r.part_c, r.ends, r.other_b, r.dn1, "z")
    pump = Pump()
    marks = {}

    def before_cross(h):
        block = halves[h]
        for o in range(4):
            cols = pl.ds(o * own, own)
            for i in range(2):
                target = pl.ds(h * half + i * quarter, quarter)
                r.part_b[target, cols] = r.parts[h, o, :, i * own : (i + 1) * own]
        r.x2[block] = r.tokens[block].astype(f32) + nn(r.part_b[block], r.big[0]) + r.out_biases[0:1]

        def normed(inside):
            rows_of = pl.ds(pl.multiple_of(h * half + inside.start, 64), 64)
            xhat, _ = normal(r.x2[rows_of])
            r.n2[rows_of] = (xhat * r.norm_gains[1:2] + r.norm_biases[1:2]).astype(bf16)

        row_blocks(half, 64, normed)
        queries = (nt(r.n2[block], r.big[1]) + r.bias[0:1]).astype(bf16).astype(f32)
        to_pairs(queries, r.q_pair, block, clip_start, factor)

    def attend(h, between):
        for g in range(groups):
            for j in range(2):
                cross_forward(r, halves[h], g, j, clip_start, frame_count)
                pump(0.75)
            r.lse_own[h, g] = r.stats[g, halves[h]].T[0:8]
            marks["o2", h] = pump.add(o2_sum[h], (2 * g, 2 * g + 1))
            for step in between[g]:
                step()

    def last_step(name, j):
        return functools.partial(getattr(last, name), j)

    before_cross(first)
    attend(
        first,
        [
            [last_step("from_line", 0)],
            [last_step("from_line", 1), last_step("from_sides", 0)],
            [last_step("from_line", 2), last_step("from_sides", 1), last_step("from_corner", 0)],
        ],
    )
    parts[second].take()
    before_cross(second)
    pump(1.4)
    attend(
        second,
        [
            [last_step("from_sides", 2), last_step("from_corner", 1)],
            [last_step("from_corner", 2)],
            [last_step("from_core", j) for j in range(3)],
        ],
    )

    for load in loads[5:]:
        load.wait()
    for k in range(3):
        r.bias_sums[k] = jnp.zeros_like(r.bias_sums[k])
        r.gain_sums[k] = jnp.zeros_like(r.gain_sums[k])
        r.out_sums[k] = jnp.zeros_like(r.out_sums[k])

    def back_third(h, c):
        dn3_sum[h].take(c)
        block = strips[h][c]
        upstream = r.dn3[block].astype(f32)
        grad = r.cotangent[block].astype(f32)
        change, gain = back_normal(r.x3[block], upstream, r.norm_gains[2:3])
        total = grad + change
        r.g3[block] = total
        r.low[block] = total.astype(bf16)
        r.gain_sums[2] += by_eights(gain)
        r.bias_sums[2] += by_eights(upstream)
        r.out_sums[1] += by_eights(total)
        r.out_sums[2] += by_eights(grad)

    def feed_forward(h):
        block = halves[h]
        pump.take(marks["o2", h])
        value = r.x2[block] + r.out_biases[1:2]
        for g in range(groups):
            for c in (2 * g, 2 * g + 1):
                o2_sum[h].take(c)
            cols = pl.ds(g * GROUP, GROUP)
            value = value + nn(r.o2[block, cols], r.big[4, cols])
        r.x3[block] = value
        pump(0.5)

        def normed(inside):
            rows_of = pl.ds(pl.multiple_of(h * half + inside.start, 64), 64)
            xhat, _ = normal(r.x3[rows_of])
            r.n3[rows_of] = (xhat * r.norm_gains[2:3] + r.norm_biases[2:3]).astype(bf16)

        row_blocks(half, 64, normed)
        pump(0.4)
        upward = nn(r.n3[block], r.fc_up[...]) + r.up_bias[...].reshape(1, -1)
        normal_share = 0.5 * (1.0 + lax.erf(upward * (0.5**0.5)))
        density = jnp.exp(-0.5 * upward * upward) * 0.3989422804014327
        r.a[block] = (upward * normal_share).astype(bf16)
        pump(0.7)
        change = nt(r.cotangent[block], r.fc_down[...]) * (normal_share + upward * density)
        r.up_sum[h] = by_eights(change)
        r.dul[block] = change.astype(bf16)
        pump(0.6)
        o2_sum[h].finish()
        r.part_a[block] = nt(r.dul[block], r.fc_up[...]).astype(bf16)
        pump(0.4)
        marks["dn3", h] = pump.add(dn3_sum[h], range(dn3_sum[h].count), functools.partial(back_third, h), 0.3)

    feed_forward(first)
    feed_forward(second)
    gather.finish()
    last.finish()
    for part in parts:
        part.finish()

    scatter_1 = Scatter(at, n, r.grads_1, r.came_1, r.slots_1, *(getattr(r, f"x_{i}") for i in range(4)))
    scatter_2 = Scatter(at, n, r.grads_1, r.came_2, r.slots_2, *(getattr(r, f"y_{i}") for i in range(4)))
    scatter_3 = Scatter(at, n, r.grads_3, r.came_3, r.slots_3, *(getattr(r, f"w_{i}") for i in range(4)))

    def down_came(h, c):
        down_sum[h].take(c)
        block = strips[h][c]
        r.layer_out[block] = (r.x3[block] + r.down[block].astype(f32) + r.out_biases[2:3]).astype(bf16)

    def send_down(h):
        marks["down", h] = pump.add(
            down_sum[h], range(down_sum[h].count), functools.partial(down_came, h), 0.15
        )

    def launch(scatter, result):
        size = scatter.x.shape[1] * scatter.x.shape[2] * 2
        scatter.start()

        def between_chips():
            scatter.fold()
            sides["free"] = max(sides["free"], pump.now()) + 4 * size / 94e3
            pump.later(sides["free"] - pump.now() + 3.0, 0.7, result)

        pump.later(4 * size / 400e3 + 2.5, 1.5, between_chips)

    sides, done = dict(free=0.0), []

    def result_1():
        total = scatter_1.finish()
        done.append(1)
        r.fc_up_grad[...] = total[:, 0:width]
        r.fc_down_grad[...] = total[:, width:]


    def down_part(h):
        r.part_b[halves[h]] = nn(r.a[halves[h]], r.fc_down[...]).astype(bf16)

    def run(jobs, time):
        for job in jobs:
            job()
            pump(time)

    run(weight_grad(r.grads_1, 0, r.n3, r.dul) + weight_grad(r.grads_1, width, r.cotangent, r.a), 0.5)
    launch(scatter_1, result_1)
    run([functools.partial(down_part, h) for h in order], 0.4)
    send_down(first)

    def before_queries(h):
        block = halves[h]
        pump.until(marks["dn3", h])
        dn3_sum[h].finish()
        upstream = nt(r.low[block], r.big[4]).astype(bf16).astype(f32)
        to_pairs(upstream, r.do_pair, block, clip_start, 1.0)
        r.do2_sum[h] = by_eights(upstream)
        pump(0.6)
        lane = iota((half, PAIR), 1)
        for g in range(groups):
            stats = r.stats[g, block]
            for j in range(2):
                cols = slice(g * GROUP + j * PAIR, g * GROUP + (j + 1) * PAIR)
                terms = upstream[:, cols] * r.o2[block, cols].astype(f32)
                even = jnp.sum(jnp.where(lane < HEAD, terms, 0.0), axis=1, keepdims=True)
                odd = jnp.sum(jnp.where(lane < HEAD, 0.0, terms), axis=1, keepdims=True)
                stats = jnp.where(lane == 16 + 2 * j, even, jnp.where(lane == 17 + 2 * j, odd, stats))
            r.stats[g, block] = stats
        pump(0.5)

    def query_grads(h):
        before_queries(h)
        total = dq_sum[h]
        for g in range(groups):
            for j in range(2):
                cross_queries(r, halves[h], g, j, clip_start, frame_count)
                pump(0.8)
            marks["dq", h] = pump.add(total, (2 * g, 2 * g + 1))

    query_grads(first)
    query_grads(second)


    def frame_grads(clip):
        value = tn(r.dk_t[clip], r.big[2]) + tn(r.dv_t[clip], r.big[3])
        r.encoder_grad[:, clip, :] = value[0:frame_count].astype(bf16)

    def cross_weight(source, column):
        value = sum(nn(source[clip], r.frames[clip]) for clip in range(2))
        put_blocks(r.grads_1, column, 0, value.astype(bf16).T)

    def cross_out_grad():
        own_columns(at, r.o2, r.do1)
        for job in weight_grad(r.grads_3, 5 * own, r.low, r.do1):
            job()

    def back_second(h):
        block = halves[h]
        pump.take(marks["dq", h])
        value = None
        for g in range(groups):
            for c in (2 * g, 2 * g + 1):
                dq_sum[h].take(c)
            cols = pl.ds(g * GROUP, GROUP)
            term = nn(r.dq2[block, cols], r.big[1, cols])
            value = term if value is None else value + term
        r.dn2[...] = value
        pump(0.5)

        def back(inside):
            rows_of = pl.ds(pl.multiple_of(h * half + inside.start, 64), 64)
            upstream = r.dn2[inside]
            change, gain = back_normal(r.x2[rows_of], upstream, r.norm_gains[1:2])
            total = r.g3[rows_of] + change
            r.x2[rows_of] = total
            r.low[rows_of] = total.astype(bf16)
            r.gain_sums[1] += by_eights(gain)
            r.bias_sums[1] += by_eights(upstream)
            r.out_sums[0] += by_eights(total)

        row_blocks(half, 64, back)
        pump(0.7)
        r.do1[block] = nt(r.low[block], r.self_out[...]).astype(bf16)
        self_backward(r, h, clip_start)
        pump(2.0 if h else 1.4)
        dq_sum[h].finish()
        value = nn(r.dq1[block], r.self_in[0]) + nn(r.dk1[block], r.self_in[1])
        r.part_c[block] = (value + nn(r.dv1[block], r.self_in[2])).astype(bf16)
        pump(0.4)
        marks["dn1", h] = pump.add(dn1_sum[h], range(dn1_sum[h].count), functools.partial(back_first, h), 0.3)

    def back_first(h, c):
        dn1_sum[h].take(c)
        block = strips[h][c]
        upstream = r.dn1[block].astype(f32)
        change, gain = back_normal(r.tokens[block].astype(f32), upstream, r.norm_gains[0:1])
        r.token_grad[block] = (change + r.x2[block]).astype(bf16)
        r.gain_sums[0] += by_eights(gain)
        r.bias_sums[0] += by_eights(upstream)

    def query_weight():
        own_columns(at, r.dq2, r.q1)
        for job in weight_grad(r.grads_3, 3 * own, r.n2, r.q1):
            job()
        total = jnp.sum(r.q1[...].astype(f32), axis=0, keepdims=True)
        r.in_bias_sums[2:3, 0:own] = total

    def squeeze(values):
        return jnp.sum(values, axis=0, keepdims=True)

    early = [Everyone(at, PLANE, 1, r.early_slots, r.e_0, r.e_1)]
    late = [Everyone(at, PLANE, 1, r.late_slots, r.l_0, r.l_1)]
    if n > PLANE:
        early.append(Everyone(at, n // PLANE, PLANE, r.early_slots_2, r.m_0, r.m_1))
        late.append(Everyone(at, n // PLANE, PLANE, r.late_slots_2, r.n_0, r.n_1))

    def finish_all(stages):
        total = stages[0].finish()
        for stage in stages[1:]:
            stage.slots[stage.place] = total
            stage.start()
            total = stage.finish()
        return total

    def early_vectors():
        r.in_bias_sums[1:2, 0:own] = squeeze(r.do1[...].astype(f32))
        total = squeeze(r.do2_sum[0] + r.do2_sum[1])
        for j in range(4):

            @pl.when(at.m == j)
            def _(j=j):
                r.in_bias_sums[3:4, 0:own] = total[:, j * own : (j + 1) * own]

        lines = [squeeze(r.gain_sums[k]) for k in (1, 2)] + [squeeze(r.bias_sums[k]) for k in (1, 2)]
        lines += [squeeze(r.out_sums[k]) for k in range(3)] + [squeeze(r.up_sum[0] + r.up_sum[1])]
        place = early[0].place
        r.early_slots[place, 0:8] = jnp.concatenate(lines, axis=0)
        r.early_slots[place, 8:16] = jnp.zeros((8, width), f32)
        for k in range(4):
            r.early_slots[place, 8:9, k * own : (k + 1) * own] = r.in_bias_sums[k : k + 1, 0:own]
        early[0].start()
        pump.later(8.0, 0.3, early_results)

    def early_results():
        total = finish_all(early)
        r.norm_gains_grad[1:3] = total[0:2]
        r.norm_biases_grad[1:3] = total[2:4]
        r.out_biases_grad[...] = total[4:7]
        r.up_bias_grad[...] = total[7:8].reshape(-1)
        for k in range(4):
            r.in_biases_grad[k : k + 1] = total[8:9, k * own : (k + 1) * own]

    def result_2():
        total = scatter_2.finish()
        for j in range(4):
            for t in range(2):
                cols = slice(t * width + j * own, t * width + (j + 1) * own)
                r.plane_out[j, :, t * own : (t + 1) * own] = total[:, cols].astype(bf16)
        for k in (1, 2, 3):
            to_plane(k).start()
        pump.later(12.0, 0.3, result_2_end)

    def to_plane(k):
        to = lax.rem(at.m + k, 4)
        return remote(r.plane_out.at[to], r.plane_slots.at[at.m], r.d_0.at[k], r.d_1.at[at.m], at.line(to))

    def result_2_end():
        total = r.plane_out[at.m].astype(f32)
        for k in (1, 2, 3):
            o = lax.rem(at.m + k, 4)
            remote(r.plane_out.at[o], r.plane_slots.at[o], r.d_0.at[k], r.d_1.at[o], at.line(o)).wait_recv()
            total = total + r.plane_slots[o].astype(f32)
        for t in range(2):
            r.cross_in_grad[1 + t] = total[:, t * own : (t + 1) * own]
        for k in (1, 2, 3):
            to_plane(k).wait_send()

    def result_3():
        total = scatter_3.finish()
        for i in range(3):
            r.self_in_grad[i] = total[:, i * own : (i + 1) * own]
        r.cross_in_grad[0] = total[:, 3 * own : 4 * own]
        r.self_out_grad[...] = total[:, 4 * own : 5 * own].T
        r.cross_out_grad[...] = total[:, 5 * own : 6 * own].T

    run([functools.partial(cross_frames, r, g, j, frame_count) for g in range(groups) for j in range(2)], 0.7)
    while not done:
        pump.run_task()
    run([functools.partial(cross_weight, r.dk_t, 0), functools.partial(cross_weight, r.dv_t, width)], 0.8)
    launch(scatter_2, result_2)
    cross_out_grad()
    pump(0.6)
    back_second(first)
    run([functools.partial(frame_grads, clip) for clip in range(2)], 1.2)
    back_second(second)
    pump.until(marks["down", first])
    down_sum[first].finish()
    send_down(second)
    run([query_weight] + weight_grad(r.grads_3, 4 * own, r.low, r.o1), 0.4)
    jobs = weight_grad(r.grads_3, 0, r.n1, r.dq1) + weight_grad(r.grads_3, own, r.n1, r.dk1)
    run(jobs + weight_grad(r.grads_3, 2 * own, r.n1, r.dv1), 0.3)
    launch(scatter_3, result_3)
    early_vectors()
    pump.until(marks["dn1", second])
    for h in order:
        dn1_sum[h].finish()
    place = late[0].place
    r.late_slots[place] = jnp.zeros_like(r.late_slots[place])
    r.late_slots[place, 0:1] = squeeze(r.gain_sums[0])
    r.late_slots[place, 1:2] = squeeze(r.bias_sums[0])
    late[0].start()
    pump.until(marks["down", second])
    pump.flush()
    down_sum[second].finish()
    total = finish_all(late)
    r.norm_gains_grad[0:1] = total[0:1]
    r.norm_biases_grad[0:1] = total[1:2]


def layer(n, inputs):
    tokens, self_in = inputs["tokens"], inputs["self_in"]
    rows, width = tokens.shape
    own = self_in.shape[1]
    hidden = inputs["fc_up_in"].shape[1]
    groups = width // GROUP
    per = width // n
    S = jax.ShapeDtypeStruct
    outs = dict(
        layer_out=S((rows, width), bf16), token_grad=S((rows, width), bf16),
        encoder_grad=S(inputs["encoder"].shape, bf16), norm_gains_grad=S((3, width), f32),
        norm_biases_grad=S((3, width), f32), self_in_grad=S((3, per, own), f32), cross_in_grad=S((3, per, own), f32),
        in_biases_grad=S((4, own), f32), self_out_grad=S((own, per), f32), cross_out_grad=S((own, per), f32),
        out_biases_grad=S((3, width), f32), fc_up_grad=S((per, hidden), f32), up_bias_grad=S((hidden,), f32),
        fc_down_grad=S((per, hidden), f32),
    )
    dma = pltpu.SemaphoreType.DMA
    low, full = pltpu.VMEM((rows, width), bf16), pltpu.VMEM((rows, width), f32)
    thin = pltpu.VMEM((rows, own), bf16)
    wide = pltpu.VMEM((rows, 2 * width), bf16)
    frame_pair = pltpu.VMEM((FRAMES, 2 * width), bf16)
    scratch = dict(
        fc_up=pltpu.VMEM((width, hidden), bf16), fc_down=pltpu.VMEM((hidden, width), bf16), cotangent=low,
        load=dma((8,)), big=pltpu.VMEM((5, width, width), bf16), bias=pltpu.VMEM((8, width), f32),
        bias_slots=pltpu.VMEM((4, 8, 256), f32), parts=pltpu.VMEM((2, 4, rows // 4, 2 * own), bf16),
        frames=pltpu.VMEM((2, FRAMES, width), bf16), n1=low, n2=low, n3=low, o2=low, dq2=low, dn3=low, down=low, part_a=low, part_b=low, part_c=low, ends=low,
        other_b=low, ends_b=pltpu.VMEM((rows // 2, width), bf16), other_a=low,
        other_c=pltpu.VMEM((rows // 2, width), bf16), x2=full, x3=full, g3=full, dn2=pltpu.VMEM((rows // 2, width), f32), q1=thin, k1=thin, v1=thin, o1=thin, do1=thin, dq1=thin,
        dk1=thin, dv1=thin, lse1=pltpu.VMEM((rows, 8), f32), q_pair=wide, do_pair=wide,
        k_pair=frame_pair, v_pair=frame_pair, stats=pltpu.VMEM((groups, rows, PAIR), f32),
        **{f"lse_{name}": pltpu.VMEM((2, groups, 8, rows // 2), f32) for name in ("own", "end", "mid", "far", "all")}, dk_t=pltpu.VMEM((2, width, FRAMES), bf16),
        dv_t=pltpu.VMEM((2, width, FRAMES), bf16), dk_sum=pltpu.VMEM((own, rows), f32),
        dv_sum=pltpu.VMEM((own, rows), f32), gain_sums=pltpu.VMEM((3, 8, width), f32),
        bias_sums=pltpu.VMEM((3, 8, width), f32), out_sums=pltpu.VMEM((3, 8, width), f32),
        up_sum=pltpu.VMEM((2, 8, hidden), f32), do2_sum=pltpu.VMEM((2, 8, width), f32),
        in_bias_sums=pltpu.VMEM((8, 256), f32), early_slots=pltpu.VMEM((PLANE, 16, width), f32),
        late_slots=pltpu.VMEM((PLANE, 8, width), f32), plane_out=pltpu.VMEM((4, per, 2 * own), bf16),
        plane_slots=pltpu.VMEM((4, per, 2 * own), bf16), grads_1=pltpu.VMEM((n, per, 2 * width), bf16),
        grads_3=pltpu.VMEM((n, per, 6 * own), bf16),
    )
    group_dma = Total.semaphores(groups)
    part_dma = [dma((2, 5)), dma((2, 4))]
    tiles, strips = Total.semaphores(2 * groups), Total.semaphores(rows // 128)
    for letter, group in (
        ("g", Gather.semaphores()), ("h", Gather.semaphores()), ("b", Direct.semaphores()), ("p", part_dma), ("s", group_dma),
        ("t", tiles), ("u", strips), ("v", strips), ("q", tiles), ("z", strips), ("e", Everyone.semaphores(PLANE)), ("l", Everyone.semaphores(PLANE)),
        ("d", Direct.semaphores()),
    ):
        for i, one in enumerate(group):
            scratch[f"{letter}_{i}"] = one
    if n > PLANE:
        scratch["early_slots_2"] = pltpu.VMEM((n // PLANE, 16, width), f32)
        scratch["late_slots_2"] = pltpu.VMEM((n // PLANE, 8, width), f32)
        for letter in ("m", "n"):
            for i, one in enumerate(Everyone.semaphores(n // PLANE)):
                scratch[f"{letter}_{i}"] = one
    for k, letter, cols in ((1, "x", 2 * width), (2, "y", 2 * width), (3, "w", 6 * own)):
        came, slots, *semaphores = Scatter.buffers(n, per, cols)
        scratch[f"came_{k}"], scratch[f"slots_{k}"] = came, slots
        for i, one in enumerate(semaphores):
            scratch[f"{letter}_{i}"] = one
    names = list(inputs) + list(outs) + list(scratch)
    late = ("fc_up_in", "fc_down_in", "cotangent_in", "cross_in", "cross_out")
    result = pl.pallas_call(
        functools.partial(layer_kernel, names, n),
        out_shape=list(outs.values()),
        in_specs=[SMEM if name == "lengths" else ANY if name in late else VMEM for name in inputs],
        out_specs=[VMEM] * len(outs),
        scratch_shapes=list(scratch.values()),
        compiler_params=pltpu.CompilerParams(
            collective_id=1, has_side_effects=True, vmem_limit_bytes=127 * 2**19
        ),
        name="layer",
    )(*inputs.values())
    return dict(zip(outs, result))


def results_kernel(count, *refs):
    sources, targets, rooms = (refs[k * count : (k + 1) * count] for k in range(3))
    come, go = refs[3 * count :]
    reads = [
        pltpu.make_async_copy(source, room, come.at[k]) for k, (source, room) in enumerate(zip(sources, rooms))
    ]
    writes = [
        pltpu.make_async_copy(room, target, go.at[k]) for k, (room, target) in enumerate(zip(rooms, targets))
    ]
    for read in reads:
        read.start()
    for read, write in zip(reads, writes):
        read.wait()
        write.start()
    for write in writes:
        write.wait()


def results(values):
    count = len(values)
    dma = pltpu.SemaphoreType.DMA
    return pl.pallas_call(
        functools.partial(results_kernel, count),
        out_shape=[jax.ShapeDtypeStruct(value.shape, value.dtype) for value in values],
        in_specs=[ANY] * count,
        out_specs=[ANY] * count,
        scratch_shapes=[pltpu.VMEM(value.shape, value.dtype) for value in values] + [dma((count,)), dma((count,))],
        compiler_params=pltpu.CompilerParams(vmem_limit_bytes=127 * 2**19),
        name="results",
    )(*values)


def shards(
    n, tokens, encoder, lengths, norm_gains, norm_biases, self_in, cross_in, in_biases, self_out, cross_out,
    out_biases, fc_up, up_bias, fc_down, cotangent,
):
    outs = layer(
        n,
        dict(
            tokens=tokens, encoder=encoder.transpose(1, 0, 2), lengths=lengths, norm_gains=norm_gains, norm_biases=norm_biases,
            self_in=self_in.transpose(0, 2, 1),
            cross_in=cross_in.transpose(0, 2, 1), in_biases=in_biases, self_out=self_out, cross_out=cross_out,
            out_biases=out_biases, up_bias=up_bias, fc_up_in=fc_up, fc_down_in=fc_down,
            cotangent_in=cotangent,
        ),
    )
    outs = dict(zip(outs, results(list(outs.values()))))
    outs["encoder_grad"] = outs["encoder_grad"].transpose(1, 0, 2)
    outs["fc_down_grad"] = outs["fc_down_grad"].T
    return tuple(outs.values())


def solution(mesh):
    in_specs = (
        P("dp", None), P("dp", "mp", None), P("dp", None), P(), P(), P(None, None, "mp"), P(None, None, "mp"),
        P(None, "mp"), P("mp", None), P("mp", None), P(), P(None, "mp"), P("mp"), P("mp", None), P("dp", None),
    )
    out_specs = (
        P("dp", None), P("dp", None), P("dp", "mp", None), P(), P(), P(None, "dp", "mp"), P(None, "dp", "mp"),
        P(None, "mp"), P("mp", "dp"), P("mp", "dp"), P(), P("dp", "mp"), P("mp"), P("mp", "dp"),
    )
    body = functools.partial(shards, mesh.shape["dp"])
    return jax.shard_map(body, mesh=mesh, in_specs=in_specs, out_specs=out_specs, check_vma=False)
```
